32 devices in a mesh: dp: 16 (over z, y, core), branch: 2 (over x).
Axes of the slice: x: 2, y: 2, z: 4, core: 2. Of those that a mesh axis runs over, the one named last changes fastest.
Arguments:
- tokens: bfloat16 [16384, 1024], P('dp'), may hold values from -6 to 6
- offsets: int32 [16], P('dp'), may hold values from 0 to 896, as said below
- lengths: int32 [16], P('dp'), may hold values from 128 to 1024, as said below
- cotangent: bfloat16 [16384, 1024], P('dp'), may hold values from -6 to 6
- ln_gain: float32 [1024], replicated, may hold values from 0.1 to 1.9
- ln_bias: float32 [1024], replicated, may hold values from -1.8 to 1.8
- w_qkv: bfloat16 [1024, 3072], replicated, may hold values from -0.1875 to 0.1875
- w_attn_out: bfloat16 [1024, 1024], replicated, may hold values from -1 to 1
- w_in: bfloat16 [1024, 4096], replicated, may hold values from -0.1875 to 0.1875
- b_in: float32 [4096], replicated, may hold values from -3 to 3
- w_out: bfloat16 [4096, 1024], replicated, may hold values from -0.09375 to 0.09375
- b_out: float32 [1024], replicated, may hold values from -1.8 to 1.8
Outputs:
- activations: bfloat16 [16384, 1024], P('dp')
- input_grad: bfloat16 [16384, 1024], P('dp')
- grad_ln_gain: float32 [1024], P(('dp', 'branch'))
- grad_ln_bias: float32 [1024], P(('dp', 'branch'))
- grad_qkv: float32 [1024, 3072], P(('dp', 'branch'))
- grad_attn_out: float32 [1024, 1024], P(('dp', 'branch'))
- grad_in: float32 [1024, 4096], P(('dp', 'branch'))
- grad_b_in: float32 [4096], P(('dp', 'branch'))
- grad_out: float32 [4096, 1024], P(('dp', 'branch'))
- grad_b_out: float32 [1024], P(('dp', 'branch'))
The draws below stay inside these ranges and needn't reach their ends.
Inputs may be any that keep to these rules, and one draw needn't show every extreme that they name: The live slots of window w are offsets[w] to offsets[w] + lengths[w] - 1, all within its 1024 slots; some window is live in all 1024 slots and another in 128. offsets[w] + lengths[w] is at most 1024.
All inputs are finite; a program needn't handle non-finite values.
Results may differ from the reference program's by a relative error of at most 0.01.
Values may be sent and summed in bfloat16 or wider, within the bound.
No kernel may reach another device: no remote copies, remote signals or barrier semaphores. Data moves between devices by JAX's collectives and lax.ppermute only.
A program may use at most 320 MiB of HBM per device.

```python
import math
import jax
import jax.numpy as jnp
from jax import lax

D = 1024
HEADS = 16
HEAD = 64
ROT = 32
FF = 4096
WIN = 1024
WINDOWS = 16
TOKENS = 16384


def window_spans(key):
    count = WINDOWS
    spans = jax.random.randint(jax.random.fold_in(key, 11), (count,), WIN // 8, WIN + 1)
    first = jax.random.randint(jax.random.fold_in(key, 12), (), 0, count)
    stride = jax.random.randint(jax.random.fold_in(key, 13), (), 1, max(count, 2))
    second = (first + stride) % count
    places = jnp.arange(count)
    spans = jnp.where(places == first, WIN, jnp.where(places == second, WIN // 8, spans))
    starts = jax.random.randint(jax.random.fold_in(key, 14), (count,), 0, WIN - spans + 1)
    starts = jnp.where(places == second, WIN - WIN // 8, starts)
    return (spans.astype(jnp.int32), starts.astype(jnp.int32))


def draw_lengths(key, part):
    spans, starts = window_spans(key)
    return spans


def draw_offsets(key, part):
    spans, starts = window_spans(key)
    return starts


def strengthened(values, own_key, source, target, parts, factor):
    owner, partner = [(jnp.arange(values.shape[dim]) // (values.shape[dim] // parts)).reshape([-1 if axis == dim else 1 for axis in range(values.ndim)]) for dim in (source, target)]
    chosen = jax.random.permutation(own_key, parts)[partner]
    strong = (owner == chosen) | (owner == (partner + parts // 2) % parts)
    return jnp.where(strong, factor * values, values)


def steps_of(own_key, extent, split, low, largest):
    def one(dim, parts):
        draws = jax.random.uniform(jax.random.fold_in(jax.random.fold_in(own_key, 6), dim), (parts,), jnp.float32, low / len(split), largest / len(split))
        return jnp.repeat(jnp.exp(draws), extent[dim] // parts).reshape((-1,) + (1,) * (len(extent) - dim - 1))

    loudness = one(*split[0])
    for cut in split[1:]:
        loudness = loudness * one(*cut)
    return loudness


def bell_draw(own_key, extent, width, limit, shards=(), held_as=jnp.bfloat16):
    level = steps_of(own_key, extent, shards, -0.22, 0.18) if shards else 1.0
    values = jax.random.normal(own_key, extent, jnp.float32) * width * level
    return jnp.minimum(jnp.maximum(values, -limit), limit).astype(held_as)


def noise_with(key, shape, deviation, reach, split, heavy, kind=jnp.bfloat16):
    drawn = deviation * jax.random.normal(key, shape, jnp.float32)
    if split:
        drawn = drawn * steps_of(key, shape, split, -0.22, 0.18)
    return jnp.clip(strengthened(drawn, jax.random.fold_in(key, 3), *heavy), -reach, reach).astype(kind)


def setup_inputs(seed: int = 0) -> dict:
    splits = jax.random.split(jax.random.key(seed), 13)
    return {
        "tokens": bell_draw(splits[0], (TOKENS, D), 1.0, 6.0, ((0, 16),)),
        "offsets": draw_offsets(jax.random.fold_in(splits[12], 71), 0),
        "lengths": draw_lengths(jax.random.fold_in(splits[12], 71), 0),
        "cotangent": noise_with(splits[3], (TOKENS, D), 1.0, 6.0, ((0, 16),), (0, 1, 16, 2.0)),
        "ln_gain": jnp.clip(1.0 + 0.18 * jax.random.normal(splits[4], (D,), jnp.float32), 0.1, 1.9),
        "ln_bias": bell_draw(splits[5], (D,), 0.3, 1.8, (), jnp.float32),
        "w_qkv": bell_draw(splits[6], (D, 3 * D), D ** -0.5, 0.1875),
        "w_attn_out": bell_draw(splits[7], (D, D), (D // 32) ** -0.5, 1.0),
        "w_in": bell_draw(splits[8], (D, FF), D ** -0.5, 0.1875),
        "b_in": bell_draw(splits[9], (FF,), 0.5, 3.0, (), jnp.float32),
        "w_out": bell_draw(splits[10], (FF, D), FF ** -0.5, 0.09375),
        "b_out": bell_draw(splits[11], (D,), 0.3, 1.8, (), jnp.float32),
    }


EPSILON = 1e-05
MASKED = -1e+30

@jax.custom_vjp
def low(v):
    return lax.optimization_barrier(v.astype(jnp.bfloat16)).astype(jnp.float32)

@jax.custom_vjp
def low_back(v):
    return v

def low_keep(v):
    return (low(v), None)

def low_pass(kept, grad):
    return (grad,)

def back_keep(v):
    return (v, None)

def back_low(kept, grad):
    return (low(grad),)
low.defvjp(low_keep, low_pass)
low_back.defvjp(back_keep, back_low)

def matmul(left, right):
    return jnp.dot(left, right, precision=lax.Precision.HIGHEST, preferred_element_type=jnp.float32)

def layer_norm(inputs, ln_gain, ln_bias):
    row_mean = lax.optimization_barrier(jnp.mean(inputs, axis=-1, keepdims=True))
    centred = inputs - row_mean
    row_var = lax.optimization_barrier(jnp.mean(centred * centred, axis=-1, keepdims=True))
    return centred * lax.rsqrt(row_var + EPSILON) * ln_gain + ln_bias

def rotary(stacked, rows):
    half_rot = ROT // 2
    places = jnp.arange(rows, dtype=jnp.float32)[:, None]
    freq_idx = jnp.arange(half_rot, dtype=jnp.float32)
    angles = places * jnp.power(10000.0, freq_idx * (-2.0 / ROT))[None, :]
    cosine = jnp.cos(angles)[:, None, :]
    sine = jnp.sin(angles)[:, None, :]
    first = stacked[..., :half_rot]
    second = stacked[..., half_rot:ROT]
    return jnp.concatenate([first * cosine - second * sine, second * cosine + first * sine, stacked[..., ROT:]], axis=-1)

def window_forward(inputs, offset, length, params):
    ln_gain, ln_bias, w_qkv, w_attn_out, w_in, b_in, w_out, b_out = params
    rows = inputs.shape[0]
    scale = 1.0 / math.sqrt(HEAD)
    normed = low(layer_norm(inputs, ln_gain, ln_bias))
    projected = low_back(matmul(normed, w_qkv))
    shaped = projected.reshape(rows, 3, HEADS, HEAD)
    queries = low(rotary(shaped[:, 0], rows))
    key_rows = low(rotary(shaped[:, 1], rows))
    val_rows = low(shaped[:, 2])
    places = jnp.arange(rows)
    live = (places >= offset) & (places < offset + length)
    block_rows = min(512, rows)

    def attend(pair):
        query_blk, start = pair
        raw = jnp.einsum('qhd,khd->hqk', query_blk, key_rows, precision=lax.Precision.HIGHEST, preferred_element_type=jnp.float32) * scale
        scores = low_back(raw)
        row_pos = start + jnp.arange(block_rows)
        allowed = live[None, :] & (places[None, :] <= row_pos[:, None])
        scores = jnp.where(allowed[None], scores, MASKED)
        top = lax.optimization_barrier(jnp.max(scores, axis=-1, keepdims=True))
        expo = jnp.exp(scores - top)
        attn_prob = low(expo / lax.optimization_barrier(jnp.sum(expo, axis=-1, keepdims=True)))
        mixed = jnp.einsum('hqk,khd->qhd', attn_prob, val_rows, precision=lax.Precision.HIGHEST, preferred_element_type=jnp.float32)
        row_live = ((row_pos >= offset) & (row_pos < offset + length)).astype(jnp.float32)
        return mixed * row_live[:, None, None]
    blocks = queries.reshape(rows // block_rows, block_rows, HEADS, HEAD)
    starts = (jnp.arange(rows // block_rows) * block_rows).astype(jnp.int32)
    attended = lax.map(jax.checkpoint(attend), (blocks, starts)).reshape(rows, HEADS * HEAD)
    attended = low(low_back(attended))
    attn_branch = low(matmul(attended, w_attn_out))
    pre = low_back(matmul(normed, w_in) + b_in)
    hidden = low(jax.nn.gelu(pre, approximate=True))
    mlp_branch = low(matmul(hidden, w_out) + b_out)
    return inputs + attn_branch + mlp_branch

def reference(tokens, offsets, lengths, cotangent, ln_gain, ln_bias, w_qkv, w_attn_out, w_in, b_in, w_out, b_out):
    params = tuple((weight.astype(jnp.float32) for weight in (ln_gain, ln_bias, w_qkv, w_attn_out, w_in, b_in, w_out, b_out)))
    windows = tokens.shape[0] // WIN
    inputs = tokens.astype(jnp.float32).reshape(windows, WIN, D)
    grads_in = cotangent.astype(jnp.float32).reshape(windows, WIN, D)

    def step(totals, item):
        window_in, window_grad, offset, length = item

        def forward(values, weights):
            return window_forward(values, offset, length, weights)
        result, pull = jax.vjp(forward, window_in, params)
        value_grad, param_grads = pull(window_grad)
        totals = jax.tree.map(jnp.add, totals, param_grads)
        return (totals, (result.astype(jnp.bfloat16), value_grad.astype(jnp.bfloat16)))
    zero_grads = jax.tree.map(jnp.zeros_like, params)
    totals, (results, value_grads) = lax.scan(step, zero_grads, (inputs, grads_in, offsets, lengths))
    return (results.reshape(TOKENS, D), value_grads.reshape(TOKENS, D), totals[0], totals[1], totals[2], totals[3], totals[4], totals[5], totals[6], totals[7])
```

```python
import functools

import jax
import jax.numpy as jnp
import numpy as np
from jax import lax
from jax.experimental import pallas as pl
from jax.experimental.pallas import tpu as pltpu
from jax.sharding import PartitionSpec as P

HEADS = 16
HEAD = 64
ROT = 32
EPSILON = 1e-05
MASKED = -1e30
BF = jnp.bfloat16
F32 = jnp.float32
QB = 256
PAIR = 128
GROUP = 256
UNIT = 128
SPLIT = 4
LIMIT = 60 * 2**20

NN = (((1,), (0,)), ((), ()))
NT = (((1,), (1,)), ((), ()))
TN = (((0,), (0,)), ((), ()))


def dot(left, right, dims=NN):
    return lax.dot_general(left, right, dims, preferred_element_type=F32)


def norm_stats(rows):
    x = rows.astype(F32)
    mean = jnp.mean(x, axis=-1, keepdims=True)
    centred = x - mean
    inv = lax.rsqrt(jnp.mean(centred * centred, axis=-1, keepdims=True) + EPSILON)
    return centred * inv, inv


def gelu_both(u):
    c = 0.7978845608028654
    u2 = u * u
    t = jnp.tanh(u * (c + (c * 0.044715) * u2))
    half = 0.5 + 0.5 * t
    slope = u * (c + (3 * c * 0.044715) * u2)
    return u * half, half + 0.5 * slope * (1.0 - t * t)


def lanes(shape):
    return lax.broadcasted_iota(jnp.int32, shape, 1)


def head_lanes(shape, h):
    lane = lanes(shape)
    return (lane < HEAD) if h == 0 else (lane >= HEAD)


def turn(part, cosine, low, high):
    return part * cosine + pltpu.roll(part, PAIR - ROT // 2, 1) * low + pltpu.roll(part, ROT // 2, 1) * high


def turn_back(grad, cosine, low, high):
    return grad * cosine + pltpu.roll(grad * low, ROT // 2, 1) + pltpu.roll(grad * high, PAIR - ROT // 2, 1)


def attn_fwd_kernel(tab, off, leng, tok, gain, bias, wq, wk, wv, cos_ref, low_ref, high_ref,
                    normed, q_out, k_out, v_out, p_out, att_out):
    rows = tok.shape[0]
    nq = rows // QB

    @pl.when(pl.program_id(0) == 0)
    def _():
        for r in range(0, rows, QB):
            unit, _ = norm_stats(tok[r : r + QB])
            normed[r : r + QB] = (unit * gain[...] + bias[...]).astype(BF)

    x = normed[...]
    start = off[0]
    stop = start + leng[0]
    place = lax.broadcasted_iota(jnp.int32, (rows, PAIR), 0)
    live = (place >= start) & (place < stop)
    kbias = jnp.where(live, 0.0, MASKED)
    live_f = jnp.where(live, 1.0, 0.0)
    lane = lanes((rows, PAIR))
    diag = lax.broadcasted_iota(jnp.int32, (QB, QB), 0) >= lax.broadcasted_iota(jnp.int32, (QB, QB), 1)
    qa = dot(x, wq[...])
    ka = dot(x, wk[...])
    va = dot(x, wv[...])
    cosine, low, high = cos_ref[...], low_ref[...], high_ref[...]
    for pr in range(GROUP // PAIR):
        cols = slice(pr * PAIR, (pr + 1) * PAIR)
        q = turn(qa[:, cols], cosine, low, high).astype(BF).astype(F32) * 0.125
        k = turn(ka[:, cols], cosine, low, high)
        v = va[:, cols]
        q_out[:, cols] = q.astype(BF)
        k_out[:, cols] = k.astype(BF)
        v_out[:, cols] = v.astype(BF)
        qh, kh, vh = [], [], []
        for h in range(2):
            mine = head_lanes((rows, PAIR), h)
            spare = lane == (HEAD if h == 0 else 0)
            qh.append(jnp.where(mine, q, jnp.where(spare, 1.0, 0.0)).astype(BF))
            kh.append(jnp.where(mine, k, jnp.where(spare, kbias, 0.0)).astype(BF))
            vh.append(jnp.where(mine, v, 0.0).astype(BF))
        for i in range(nq):
            base = i * (i + 1) // 2 * QB
            ext = (i + 1) * QB
            mixed = None
            for h in range(2):
                s = dot(qh[h][i * QB : ext], kh[h][:ext], NT)
                tail = jnp.where(diag, s[:, i * QB :], MASKED)
                s = tail if i == 0 else jnp.concatenate([s[:, : i * QB], tail], axis=1)
                e = jnp.exp(s - jnp.max(s, axis=-1, keepdims=True))
                p = (e * (1.0 / jnp.sum(e, axis=-1, keepdims=True))).astype(BF)
                for kb in range(i + 1):
                    p_out[2 * pr + h, base + kb * QB : base + (kb + 1) * QB, :] = p[:, kb * QB : (kb + 1) * QB]
                part = dot(p, vh[h][:ext])
                mixed = part if mixed is None else mixed + part
            att_out[i * QB : ext, cols] = (mixed * live_f[i * QB : ext]).astype(BF)


def attn_back_kernel(tab, off, leng, tok, normed, cot, att, q_in, k_in, v_in, p_in, wq, wk, wv, wo,
                     ngm, cos_ref, low_ref, high_ref,
                     ng_out, keep, send, small, ng, stage, dk_acc, dv_acc, sems):
    rows = tok.shape[0]
    nq = rows // QB
    g = pl.program_id(0)
    npos = stage.shape[0]
    unit_rows = rows_of = normed.shape[1] // npos
    gao_rows = (GROUP * 2) // npos
    start = off[0]
    stop = start + leng[0]
    place = lax.broadcasted_iota(jnp.int32, (rows, GROUP), 0)
    live = (place >= start) & (place < stop)
    x = normed[...]
    c = cot[...]
    do = jnp.where(live, dot(c, wo[...], NT), 0.0)
    cosine, low, high = cos_ref[...], low_ref[...], high_ref[...]
    dqs, dks, dvs = [], [], []
    for pr in range(GROUP // PAIR):
        cols = slice(pr * PAIR, (pr + 1) * PAIR)
        q, k, v = q_in[:, cols], k_in[:, cols], v_in[:, cols]
        dob = do[:, cols].astype(BF)
        prod = dob.astype(F32) * att[:, cols].astype(F32)
        zero = jnp.zeros((), BF)
        qh, kh, doh, delta = [], [], [], []
        for h in range(2):
            mine = head_lanes((rows, PAIR), h)
            qh.append(jnp.where(mine, q, zero))
            kh.append(jnp.where(mine, k, zero))
            doh.append(jnp.where(mine, dob, zero))
            delta.append(jnp.sum(jnp.where(mine, prod, 0.0), axis=-1, keepdims=True))
        dq_parts = [None] * nq
        for i in reversed(range(nq)):
            base = i * (i + 1) // 2 * QB
            ext = (i + 1) * QB
            blk = slice(i * QB, ext)
            dq_i, dk_i, dv_i = None, None, None
            for h in range(2):
                p = jnp.concatenate(
                    [p_in[2 * pr + h, base + kb * QB : base + (kb + 1) * QB, :] for kb in range(i + 1)], axis=1)
                dp = dot(doh[h][blk], v[:ext], NT)
                ds = (p.astype(F32) * (dp - delta[h][blk])).astype(BF)
                dv_h = dot(doh[h][blk], p, TN)
                dk_h = dot(qh[h][blk], ds, TN)
                dq_h = dot(ds, kh[h][:ext])
                dv_i = dv_h if dv_i is None else dv_i + dv_h
                dk_i = dk_h if dk_i is None else dk_i + dk_h
                dq_i = dq_h if dq_i is None else dq_i + dq_h
            dq_parts[i] = dq_i
            if i == nq - 1:
                dk_acc[...] = dk_i
                dv_acc[...] = dv_i
            else:
                dk_acc[:, :ext] += dk_i
                dv_acc[:, :ext] += dv_i
        dq = jnp.concatenate(dq_parts, axis=0) * 0.125
        dqs.append(turn_back(dq, cosine, low, high).astype(BF))
        dks.append(turn_back(dk_acc[...].T, cosine, low, high).astype(BF))
        dvs.append(dv_acc[...].T.astype(BF))
    dq, dk, dv = [jnp.concatenate(t, axis=1) for t in (dqs, dks, dvs)]
    part = dot(dq, wq[...], NT) + dot(dk, wk[...], NT) + dot(dv, wv[...], NT)
    for n, d in enumerate((dq, dk, dv)):
        grad = dot(x, d, TN).astype(BF)
        for i in range(npos):
            stage[tab[16 + i], n * unit_rows : (n + 1) * unit_rows, pl.ds(pl.multiple_of(g * GROUP, GROUP), GROUP)] = (
                grad[i * unit_rows : (i + 1) * unit_rows])
    gao = dot(att[...], c, TN).astype(BF)
    base_row = 3 * unit_rows
    per = GROUP // gao_rows
    for i in range(per):
        pos = tab[32 + g * per + i]
        for half in range(2):
            stage[pos, base_row + half * gao_rows : base_row + (half + 1) * gao_rows, :] = (
                gao[i * gao_rows : (i + 1) * gao_rows, half * 512 : (half + 1) * 512])

    @pl.when(g == 0)
    def _():
        ng[...] = ngm[...] + part

    @pl.when(g == pl.num_programs(0) - 1)
    def _():
        half = npos // 2
        one = pltpu.make_async_copy(stage.at[pl.ds(half, half)], send, sems.at[0])
        two = pltpu.make_async_copy(stage.at[pl.ds(0, half)], keep, sems.at[1])
        one.start()
        two.start()
        gsum = jnp.zeros((1, normed.shape[1]), F32)
        bsum = jnp.zeros((1, normed.shape[1]), F32)
        for r in range(0, rows, QB):
            unit, _ = norm_stats(tok[r : r + QB])
            full = ng[r : r + QB] + part[r : r + QB]
            ng_out[r : r + QB] = full.astype(BF)
            gsum = gsum + jnp.sum(full * unit, axis=0, keepdims=True)
            bsum = bsum + jnp.sum(full, axis=0, keepdims=True)
        small[0:1] = gsum
        small[1:2] = bsum
        small[2:3] = jnp.sum(c.astype(F32), axis=0, keepdims=True)
        small[3:8] = jnp.zeros((5, normed.shape[1]), F32)
        one.wait()
        two.wait()


def mlp_fwd_kernel(tab, *refs):
    normed = refs[0]
    w_in = refs[1 : 1 + SPLIT]
    b_in = refs[1 + SPLIT : 1 + 2 * SPLIT]
    w_out = refs[1 + 2 * SPLIT : 1 + 3 * SPLIT]
    att, wo, hid_out, dg_out, act_out, acc = refs[1 + 3 * SPLIT :]
    j = pl.program_id(0)
    last = pl.num_programs(0) - 1
    wi = jnp.concatenate([r[...] for r in w_in], axis=1)
    bi = jnp.concatenate([r[...] for r in b_in], axis=1)
    wout = jnp.concatenate([r[...] for r in w_out], axis=0)
    pre = dot(normed[...], wi) + bi
    hid, dg = gelu_both(pre)
    hid = hid.astype(BF)
    hid_out[...] = hid
    dg_out[...] = dg.astype(BF)
    out = dot(hid, wout)

    @pl.when(j == 0)
    def _():
        acc[...] = out + dot(att[...], wo[...])

    @pl.when((j > 0) & (j < last))
    def _():
        acc[...] += out

    @pl.when(j == last)
    def _():
        act_out[...] = (acc[...] + out).astype(BF)


def mlp_back_kernel(tab, *refs):
    normed, cot, hid, dg = refs[:4]
    w_in = refs[4 : 4 + SPLIT]
    w_out = refs[4 + SPLIT : 4 + 2 * SPLIT]
    gb_out, ng_out, keep, send, stage, sems = refs[4 + 2 * SPLIT :]
    j = pl.program_id(0)
    steps = pl.num_programs(0)
    npos = stage.shape[0]
    half = npos // 2
    unit_rows = normed.shape[1] // npos
    wi = jnp.concatenate([r[...] for r in w_in], axis=1)
    wout = jnp.concatenate([r[...] for r in w_out], axis=0)
    x, c = normed[...], cot[...]
    pg = dot(c, wout, NT) * dg[...].astype(F32)
    gb_out[...] = jnp.sum(pg, axis=0, keepdims=True)
    pg = pg.astype(BF)
    part = dot(pg, wi, NT)
    go = dot(hid[...], c, TN).astype(BF)
    for s in range(SPLIT):
        for n in range(2):
            stage[j * SPLIT + s, n * UNIT : (n + 1) * UNIT, :] = (
                go[s * UNIT : (s + 1) * UNIT, n * 512 : (n + 1) * 512])
    gi = dot(x, pg, TN).astype(BF)
    for s in range(SPLIT):
        place = tab[64 + j * SPLIT + s]
        row = pl.multiple_of(2 * UNIT + place // SPLIT * unit_rows, unit_rows)
        lane = pl.multiple_of(place % SPLIT * UNIT, UNIT)
        for i in range(npos):
            stage[tab[16 + i], pl.ds(row, unit_rows), pl.ds(lane, UNIT)] = (
                gi[i * unit_rows : (i + 1) * unit_rows, s * UNIT : (s + 1) * UNIT])

    @pl.when(j == 0)
    def _():
        ng_out[...] = part

    @pl.when(j > 0)
    def _():
        ng_out[...] += part

    def out_copies(step):
        at = step * SPLIT
        to, at_to = (keep, at) if at < half else (send, at - half)
        return [pltpu.make_async_copy(stage.at[pl.ds(at, SPLIT), pl.ds(0, 2 * UNIT)],
                                      to.at[pl.ds(at_to, SPLIT), pl.ds(0, 2 * UNIT)], sems.at[step])]

    def in_copies():
        low = pl.ds(2 * UNIT, stage.shape[1] - 2 * UNIT)
        return [pltpu.make_async_copy(stage.at[pl.ds(half, half), low], send.at[:, low], sems.at[total]),
                pltpu.make_async_copy(stage.at[pl.ds(0, half), low], keep.at[:, low], sems.at[total + 1])]

    total = npos // SPLIT
    for step in range(total):
        @pl.when(j == step)
        def _():
            for one in out_copies(step):
                one.start()

    @pl.when(j == steps - 1)
    def _():
        for one in in_copies():
            one.start()
        for step in range(total):
            for one in out_copies(step):
                one.wait()
        for one in in_copies():
            one.wait()


def finish_kernel(tok, cot, ng_a, ng_b, gain, out):
    unit, inv = norm_stats(tok[...])
    scaled = (ng_a[...].astype(F32) + ng_b[...].astype(F32)) * gain[...]
    mean = jnp.mean(scaled, axis=-1, keepdims=True)
    lean = jnp.mean(scaled * unit, axis=-1, keepdims=True)
    out[...] = (cot[...].astype(F32) + inv * (scaled - mean - unit * lean)).astype(BF)


def const_spec(shape):
    zeros = (0,) * len(shape)
    return pl.BlockSpec(shape, lambda g, *tabs: zeros, pipeline_mode=pl.Buffered(1))


def params():
    return pltpu.CompilerParams(vmem_limit_bytes=LIMIT)


def rotary_tables(rows):
    lane = np.arange(PAIR) % HEAD
    half = ROT // 2
    angle = np.arange(rows)[:, None] * np.power(10000.0, (lane % half) * (-2.0 / ROT))[None, :]
    inside = (lane < ROT)[None, :]
    cosine = np.where(inside, np.cos(angle), 1.0)
    low = np.where((lane < half)[None, :], -np.sin(angle), 0.0)
    high = np.where(inside & (lane >= half)[None, :], np.sin(angle), 0.0)
    return [jnp.asarray(t, F32) for t in (cosine, low, high)]


def attn_forward(tab, off, leng, tokens, gain, bias, w_qkv, tables, b_tab):
    rows, width = tokens.shape
    groups = width // 2 // GROUP
    wspec = lambda n: pl.BlockSpec((width, GROUP), lambda g, t, o, l: (0, n * 2 * groups + t[0] * groups + g))
    ospec = pl.BlockSpec((rows, GROUP), lambda g, *t: (0, g))
    tri = (rows // QB) * (rows // QB + 1) // 2 * QB
    half = jax.ShapeDtypeStruct((rows, width // 2), BF)
    return pl.pallas_call(
        attn_fwd_kernel,
        grid_spec=pltpu.PrefetchScalarGridSpec(
            num_scalar_prefetch=3,
            grid=(groups,),
            in_specs=[const_spec((rows, width)), const_spec((1, width)), const_spec((1, width)),
                      wspec(0), wspec(1), wspec(2)] + [const_spec((rows, PAIR))] * 3,
            out_specs=[const_spec((rows, width)), ospec, ospec, ospec,
                       pl.BlockSpec((GROUP // HEAD, tri, QB), lambda g, *t: (g, 0, 0)), ospec],
        ),
        out_shape=[jax.ShapeDtypeStruct((rows, width), BF), half, half, half,
                   jax.ShapeDtypeStruct((HEADS // 2, tri, QB), BF), half],
        compiler_params=params(),
        cost_estimate=pl.CostEstimate(flops=12 * 10**9, bytes_accessed=25 * 10**6, transcendentals=5 * 10**6),
        name="attention_forward",
    )(b_tab, off, leng, tokens, gain, bias, w_qkv, w_qkv, w_qkv, *tables)


def attn_backward(tab, off, leng, tokens, normed, cot, att, q, k, v, p, w_qkv, w_ao, ngm, tables, npos):
    rows, width = tokens.shape
    groups = width // 2 // GROUP
    unit_rows = width // npos
    gao_rows = GROUP * 2 // npos
    wspec = lambda n: pl.BlockSpec((width, GROUP), lambda g, t, o, l: (0, n * 2 * groups + t[48] * groups + g))
    ospec = pl.BlockSpec((rows, GROUP), lambda g, *t: (0, g))
    tri = p.shape[1]
    ublock = 3 * unit_rows + 2 * gao_rows
    anyspec = pl.BlockSpec(memory_space=pl.ANY)
    part = jax.ShapeDtypeStruct((npos // 2, ublock, 512), BF)
    return pl.pallas_call(
        attn_back_kernel,
        grid_spec=pltpu.PrefetchScalarGridSpec(
            num_scalar_prefetch=3,
            grid=(groups,),
            in_specs=[const_spec((rows, width))] * 3 + [ospec] * 4
            + [pl.BlockSpec((GROUP // HEAD, tri, QB), lambda g, *t: (g, 0, 0)), wspec(0), wspec(1), wspec(2),
               pl.BlockSpec((GROUP, width), lambda g, t, o, l: (t[48] * groups + g, 0)),
               const_spec((rows, width))] + [const_spec((rows, PAIR))] * 3,
            out_specs=[const_spec((rows, width)), anyspec, anyspec, const_spec((8, width))],
            scratch_shapes=[pltpu.VMEM((rows, width), F32), pltpu.VMEM((npos, ublock, 512), BF),
                            pltpu.VMEM((PAIR, rows), F32), pltpu.VMEM((PAIR, rows), F32),
                            pltpu.SemaphoreType.DMA((2,))],
        ),
        out_shape=[jax.ShapeDtypeStruct((rows, width), BF), part, part, jax.ShapeDtypeStruct((8, width), F32)],
        compiler_params=params(),
        cost_estimate=pl.CostEstimate(flops=30 * 10**9, bytes_accessed=30 * 10**6, transcendentals=0),
        name="attention_backward",
    )(tab, off, leng, tokens, normed, cot, att, q, k, v, p, w_qkv, w_qkv, w_qkv, w_ao, ngm, *tables)


def mlp_specs(width):
    w_in = [pl.BlockSpec((width, UNIT), lambda j, t, s=s: (0, t[j * SPLIT + s])) for s in range(SPLIT)]
    b_in = [pl.BlockSpec((1, UNIT), lambda j, t, s=s: (0, t[j * SPLIT + s])) for s in range(SPLIT)]
    w_out = [pl.BlockSpec((UNIT, width), lambda j, t, s=s: (t[j * SPLIT + s], 0)) for s in range(SPLIT)]
    return w_in, b_in, w_out


def mlp_forward(tab, normed, w_in, b_in, w_out, att, w_ao, npos):
    rows, width = normed.shape
    wi, bi, wo = mlp_specs(width)
    wide = SPLIT * UNIT
    hspec = pl.BlockSpec((rows, wide), lambda j, t: (0, j))
    hid = jax.ShapeDtypeStruct((rows, npos * UNIT), BF)
    return pl.pallas_call(
        mlp_fwd_kernel,
        grid_spec=pltpu.PrefetchScalarGridSpec(
            num_scalar_prefetch=1,
            grid=(npos // SPLIT,),
            in_specs=[const_spec((rows, width))] + wi + bi + wo
            + [const_spec((rows, width // 2)),
               pl.BlockSpec((width // 2, width), lambda j, t: (t[48], 0))],
            out_specs=[hspec, hspec, const_spec((rows, width))],
            scratch_shapes=[pltpu.VMEM((rows, width), F32)],
        ),
        out_shape=[hid, hid, jax.ShapeDtypeStruct((rows, width), BF)],
        compiler_params=params(),
        cost_estimate=pl.CostEstimate(flops=10 * 10**9, bytes_accessed=25 * 10**6, transcendentals=2 * 10**6),
        name="mlp_forward",
    )(tab, normed, *([w_in] * SPLIT), *([b_in] * SPLIT), *([w_out] * SPLIT), att, w_ao)


def mlp_backward(tab, normed, cot, hid, dg, w_in, w_out, npos):
    rows, width = normed.shape
    wi, _, wo = mlp_specs(width)
    wide = SPLIT * UNIT
    hspec = pl.BlockSpec((rows, wide), lambda j, t: (0, j))
    unit_rows = width // npos
    ublock = 2 * UNIT + npos // SPLIT * unit_rows
    part = jax.ShapeDtypeStruct((npos // 2, ublock, 512), BF)
    anyspec = pl.BlockSpec(memory_space=pl.ANY)
    return pl.pallas_call(
        mlp_back_kernel,
        grid_spec=pltpu.PrefetchScalarGridSpec(
            num_scalar_prefetch=1,
            grid=(npos // SPLIT,),
            in_specs=[const_spec((rows, width)), const_spec((rows, width)), hspec, hspec] + wi + wo,
            out_specs=[pl.BlockSpec((1, wide), lambda j, t: (0, j)), const_spec((rows, width)), anyspec, anyspec],
            scratch_shapes=[pltpu.VMEM((npos, ublock, 512), BF), pltpu.SemaphoreType.DMA((npos // SPLIT + 2,))],
        ),
        out_shape=[jax.ShapeDtypeStruct((1, npos * UNIT), F32), jax.ShapeDtypeStruct((rows, width), F32), part, part],
        compiler_params=params(),
        cost_estimate=pl.CostEstimate(flops=18 * 10**9, bytes_accessed=30 * 10**6, transcendentals=0),
        name="mlp_backward",
    )(tab, normed, cot, hid, dg, *([w_in] * SPLIT), *([w_out] * SPLIT))


def finish(tokens, cot, ng_a, ng_b, gain):
    rows, width = tokens.shape
    row = pl.BlockSpec((QB, width), lambda r: (r, 0))
    return pl.pallas_call(
        finish_kernel,
        grid=(rows // QB,),
        in_specs=[row, row, row, row, pl.BlockSpec((1, width), lambda r: (0, 0))],
        out_specs=row,
        out_shape=jax.ShapeDtypeStruct((rows, width), BF),
        compiler_params=params(),
        cost_estimate=pl.CostEstimate(flops=10**7, bytes_accessed=10**7, transcendentals=0),
        name="norm_backward",
    )(tokens, cot, ng_a, ng_b, gain)


def bit_reverse(value, bits):
    out = 0
    for n in range(bits):
        out |= (value >> n & 1) << (bits - 1 - n)
    return out


NPOS = 16


def place_tables(ndp):
    bits = NPOS.bit_length() - 1
    table = np.zeros((ndp, 2, 80), np.int32)
    for d in range(ndp):
        for b in range(2):
            for n in range(NPOS):
                if ndp == NPOS:
                    table[d, b, n] = 2 * (bit_reverse(n, bits) ^ d) + b
                    table[d, b, 64 + n] = bit_reverse(n, bits) ^ d
                    table[d, b, 16 + n] = bit_reverse(n ^ d, bits)
                    rel = 0
                    for k in range(bits - 1):
                        rel |= ((n >> (k + 1) & 1) ^ (d >> k & 1)) << (bits - 1 - k)
                    rel |= (n & 1) ^ (d >> (bits - 1) & 1)
                    table[d, b, 32 + n] = rel
                else:
                    table[d, b, n] = b * NPOS + n
                    table[d, b, 64 + n] = n
                    table[d, b, 16 + n] = n
                    table[d, b, 32 + n] = n
            table[d, b, 48] = b
    return table


def add_halves(keep, recv):
    half = keep.shape[0] // 2
    mine = (keep[:half].astype(F32) + recv[:half].astype(F32)).astype(BF)
    other = (keep[half:].astype(F32) + recv[half:].astype(F32)).astype(BF)
    return mine, other


def ring_sum(keep, send, ndp):
    bit = 1
    while True:
        recv = lax.ppermute(send, "dp", [(d, d ^ bit) for d in range(ndp)])
        bit *= 2
        if bit == ndp:
            return keep[0].astype(F32) + recv[0].astype(F32)
        keep, send = add_halves(keep, recv)


def place_columns_kernel(tab, own, recv, out):
    b = tab[48]
    for n in range(NPOS):
        step, s = n // SPLIT, n % SPLIT
        col = slice(s * UNIT, (s + 1) * UNIT)
        mine = (2 * n + b) * UNIT
        theirs = (2 * n + 1 - b) * UNIT
        out[:, pl.ds(pl.multiple_of(mine, UNIT), UNIT)] = own[step, :, col].astype(F32)
        out[:, pl.ds(pl.multiple_of(theirs, UNIT), UNIT)] = recv[step, :, col].astype(F32)


def shards(ndp, tokens, offsets, lengths, cotangent, ln_gain, ln_bias, w_qkv, w_attn_out, w_in, b_in, w_out, b_out):
    rows, width = tokens.shape
    dp = lax.axis_index("dp")
    b = lax.axis_index("branch")
    hidden = w_in.shape[1]
    tables = rotary_tables(rows)
    all_tab = jnp.asarray(place_tables(ndp))
    tab = lax.dynamic_slice(all_tab, (dp, b, 0), (1, 1, 80)).reshape(80)
    b_tab = lax.dynamic_slice(all_tab, (dp, b, 48), (1, 1, 1)).reshape(1)
    gain = ln_gain.reshape(1, width)
    bias = ln_bias.reshape(1, width)
    swap = [(0, 1), (1, 0)]

    normed, q, k, v, p, att = attn_forward(tab, offsets, lengths, tokens, gain, bias, w_qkv, tables, b_tab)
    hid, dg, act_own = mlp_forward(tab, normed, w_in, b_in.reshape(1, hidden), w_out, att, w_attn_out, NPOS)
    act_recv = lax.ppermute(act_own, "branch", swap)
    gb_in, ngm, mlp_keep, mlp_send = mlp_backward(tab, normed, cotangent, hid, dg, w_in, w_out, NPOS)
    ng_own, att_keep, att_send, small = attn_backward(
        tab, offsets, lengths, tokens, normed, cotangent, att, q, k, v, p, w_qkv, w_attn_out, ngm, tables, NPOS)
    ng_recv = lax.ppermute(ng_own, "branch", swap)
    activations = (tokens.astype(F32) + (act_own.astype(F32) + act_recv.astype(F32)) + b_out).astype(BF)
    input_grad = finish(tokens, cotangent, ng_own, ng_recv, gain)

    if ndp != NPOS:
        return (activations, input_grad) + natural_sums(
            ndp, b, mlp_keep, mlp_send, att_keep, att_send, small, gb_in, width, hidden)

    mlp = ring_sum(mlp_keep, mlp_send, ndp)
    attn = ring_sum(att_keep, att_send, ndp)
    unit_rows = width // NPOS
    sub = unit_rows // 2
    g_out = mlp[: 2 * UNIT].reshape(2, UNIT, 512).transpose(1, 0, 2).reshape(UNIT, width)
    gi = mlp[2 * UNIT :].reshape(NPOS // SPLIT, unit_rows, 512)
    gq = attn[: 3 * unit_rows].reshape(3, unit_rows, 512)
    both = jnp.concatenate([gi, gq], axis=0)
    own = lax.dynamic_slice_in_dim(both, b * sub, sub, 1)
    away = lax.dynamic_slice_in_dim(both, (1 - b) * sub, sub, 1).astype(BF)
    recv = lax.ppermute(away, "branch", swap)
    steps = NPOS // SPLIT
    g_in = pl.pallas_call(
        place_columns_kernel,
        grid_spec=pltpu.PrefetchScalarGridSpec(
            num_scalar_prefetch=1, grid=(1,),
            in_specs=[const_spec((steps, sub, 512))] * 2,
            out_specs=const_spec((sub, hidden)),
        ),
        out_shape=jax.ShapeDtypeStruct((sub, hidden), F32),
        compiler_params=params(),
        name="place_columns",
    )(tab, own[:steps], recv[:steps])
    mine, theirs = own[steps:], recv[steps:].astype(F32)
    first = jnp.where(b == 0, mine, theirs)
    second = jnp.where(b == 0, theirs, mine)
    g_qkv = jnp.concatenate(sum([[first[n], second[n]] for n in range(3)], []), axis=1)
    gao_rows = GROUP * 2 // NPOS
    ga = attn[3 * unit_rows :].reshape(2, gao_rows, 512).transpose(1, 0, 2).reshape(gao_rows, width)
    top = ndp // 2
    pairs = [(d * 2 + c, (d ^ top) * 2 + 1 - c) for d in range(ndp) for c in range(2) if d // top != c]
    moved = lax.ppermute(ga.astype(BF), ("dp", "branch"), pairs).astype(F32)
    g_ao = jnp.where(dp // top == b, ga, moved)

    vec = small[:3]
    hb = gb_in.reshape(NPOS, UNIT)
    bit = 1
    count = NPOS
    while bit < ndp:
        count //= 2
        out = jnp.concatenate([hb[count:].reshape(-1), vec.reshape(-1)])
        got = lax.ppermute(out, "dp", [(d, d ^ bit) for d in range(ndp)])
        hb = hb[:count] + got[: count * UNIT].reshape(count, UNIT)
        vec = vec + got[count * UNIT :].reshape(vec.shape)
        bit *= 2
    pair = vec[:2] + lax.ppermute(vec[:2], "branch", swap)
    vec = jnp.concatenate([pair, vec[2:]], axis=0)
    per = width // (2 * ndp)
    cut = lax.dynamic_slice(vec, (0, (dp * 2 + b) * per), (3, per))
    return (activations, input_grad, cut[0], cut[1], g_qkv, g_ao, g_in, hb.reshape(UNIT), g_out, cut[2])


def natural_sums(ndp, b, mlp_keep, mlp_send, att_keep, att_send, small, gb_in, width, hidden):
    axes = ("dp", "branch")
    steps = NPOS // SPLIT
    unit_rows = width // NPOS
    mlp = jnp.concatenate([mlp_keep, mlp_send], axis=0).astype(F32)
    att = jnp.concatenate([att_keep, att_send], axis=0).astype(F32)
    go = mlp[:, : 2 * UNIT].reshape(NPOS, 2, UNIT, 512).transpose(0, 2, 1, 3).reshape(NPOS * UNIT, width)
    gi = mlp[:, 2 * UNIT :].reshape(NPOS, steps, unit_rows, 512).transpose(0, 2, 1, 3).reshape(width, hidden // 2)
    gq = att[:, : 3 * unit_rows].reshape(NPOS, 3, unit_rows, 512).transpose(0, 2, 1, 3).reshape(width, 3, 512)
    gao_rows = GROUP * 2 // NPOS
    ga = att[:, 3 * unit_rows :].reshape(NPOS, 2, gao_rows, 512).transpose(0, 2, 1, 3).reshape(NPOS * gao_rows, width)

    def scatter(part, full, dim):
        starts = [0] * part.ndim
        starts[dim] = b * part.shape[dim]
        whole = lax.dynamic_update_slice(jnp.zeros(full, F32), part, starts)
        return lax.psum_scatter(whole, axes, scatter_dimension=0, tiled=True)

    total = lambda t: lax.psum_scatter(t, axes, scatter_dimension=0, tiled=True)
    g_qkv = scatter(gq, (width, 3, width), 2)
    return (
        total(small[0]),
        total(small[1]),
        g_qkv.reshape(g_qkv.shape[0], 3 * width),
        scatter(ga, (width, width), 0),
        scatter(gi, (width, hidden), 1),
        scatter(gb_in.reshape(-1), (hidden,), 0),
        scatter(go, (hidden, width), 0),
        total(jnp.where(b == 0, small[2], 0.0)),
    )


def solution(mesh):
    return jax.shard_map(
        functools.partial(shards, mesh.shape["dp"]),
        mesh=mesh,
        in_specs=(P("dp", None), P("dp"), P("dp"), P("dp", None)) + (P(),) * 8,
        out_specs=(
            P("dp", None),
            P("dp", None),
            P(("dp", "branch")),
            P(("dp", "branch")),
            P(("dp", "branch"), None),
            P(("dp", "branch"), None),
            P(("dp", "branch"), None),
            P(("dp", "branch")),
            P(("dp", "branch"), None),
            P(("dp", "branch")),
        ),
        check_vma=False,
    )
```

```python
import functools

import jax
import jax.numpy as jnp
import numpy as np
from jax import lax
from jax.experimental import pallas as pl
from jax.experimental.pallas import tpu as pltpu
from jax.sharding import PartitionSpec as P

HEADS = 16
HEAD = 64
ROT = 32
EPSILON = 1e-05
MASKED = -1e30
BF = jnp.bfloat16
F32 = jnp.float32
QB = 256
PAIR = 128
GROUP = 256
UNIT = 128
SPLIT = 4
LIMIT = 60 * 2**20

NN = (((1,), (0,)), ((), ()))
NT = (((1,), (1,)), ((), ()))
TN = (((0,), (0,)), ((), ()))


def dot(left, right, dims=NN):
    return lax.dot_general(left, right, dims, preferred_element_type=F32)


def norm_stats(rows):
    x = rows.astype(F32)
    mean = jnp.mean(x, axis=-1, keepdims=True)
    centred = x - mean
    inv = lax.rsqrt(jnp.mean(centred * centred, axis=-1, keepdims=True) + EPSILON)
    return centred * inv, inv


def gelu_both(u):
    c = 0.7978845608028654
    u2 = u * u
    t = jnp.tanh(u * (c + (c * 0.044715) * u2))
    half = 0.5 + 0.5 * t
    slope = u * (c + (3 * c * 0.044715) * u2)
    return u * half, half + 0.5 * slope * (1.0 - t * t)


def lanes(shape):
    return lax.broadcasted_iota(jnp.int32, shape, 1)


def head_lanes(shape, h):
    lane = lanes(shape)
    return (lane < HEAD) if h == 0 else (lane >= HEAD)


def turn(part, cosine, low, high):
    return part * cosine + pltpu.roll(part, PAIR - ROT // 2, 1) * low + pltpu.roll(part, ROT // 2, 1) * high


def turn_back(grad, cosine, low, high):
    return grad * cosine + pltpu.roll(grad * low, ROT // 2, 1) + pltpu.roll(grad * high, PAIR - ROT // 2, 1)


def mlp_fwd_kernel(tab, *refs):
    tok, gain, bias = refs[:3]
    w_in = refs[3 : 3 + SPLIT]
    b_in = refs[3 + SPLIT : 3 + 2 * SPLIT]
    w_out = refs[3 + 2 * SPLIT : 3 + 3 * SPLIT]
    normed, unit_out, inv_out, hid_out, dg_out, out_ref, acc = refs[3 + 3 * SPLIT :]
    j = pl.program_id(0)
    last = pl.num_programs(0) - 1

    @pl.when(j == 0)
    def _():
        for r in range(0, tok.shape[0], QB):
            unit, inv = norm_stats(tok[r : r + QB])
            unit_out[r : r + QB] = unit.astype(BF)
            inv_out[r : r + QB] = jnp.broadcast_to(inv, (QB, PAIR))
            normed[r : r + QB] = (unit * gain[...] + bias[...]).astype(BF)

    wi = jnp.concatenate([r[...] for r in w_in], axis=1)
    bi = jnp.concatenate([r[...] for r in b_in], axis=1)
    wout = jnp.concatenate([r[...] for r in w_out], axis=0)
    hid, dg = gelu_both(dot(normed[...], wi) + bi)
    hid = hid.astype(BF)
    hid_out[...] = hid
    dg_out[...] = dg.astype(BF)
    out = dot(hid, wout)

    @pl.when(j == 0)
    def _():
        acc[...] = out

    @pl.when((j > 0) & (j < last))
    def _():
        acc[...] += out

    @pl.when(j == last)
    def _():
        out_ref[...] = (acc[...] + out).astype(BF)


def out_grad_kernel(hid, cot, keep, send):
    j = pl.program_id(0)
    go = dot(hid[...], cot[...], TN).astype(BF)

    def store(to):
        for s in range(SPLIT):
            for n in range(2):
                to[s, n * UNIT : (n + 1) * UNIT, :] = go[s * UNIT : (s + 1) * UNIT, n * 512 : (n + 1) * 512]

    @pl.when(j < pl.num_programs(0) // 2)
    def _():
        store(send)

    @pl.when(j >= pl.num_programs(0) // 2)
    def _():
        store(keep)


def attn_fwd_kernel(b_tab, off, leng, x_ref, wq, wk, wv, wo, mlp, cos_ref, low_ref, high_ref,
                    q_out, k_out, v_out, p_out, att_out, act_low, act_high, acc):
    rows = x_ref.shape[0]
    nq = rows // QB
    x = x_ref[...]
    start = off[0]
    stop = start + leng[0]
    place = lax.broadcasted_iota(jnp.int32, (rows, PAIR), 0)
    live = (place >= start) & (place < stop)
    kbias = jnp.where(live, 0.0, MASKED)
    live_f = jnp.where(live, 1.0, 0.0)
    lane = lanes((rows, PAIR))
    diag = lax.broadcasted_iota(jnp.int32, (QB, QB), 0) >= lax.broadcasted_iota(jnp.int32, (QB, QB), 1)
    qa = dot(x, wq[...])
    ka = dot(x, wk[...])
    va = dot(x, wv[...])
    cosine, low, high = cos_ref[...], low_ref[...], high_ref[...]
    for pr in range(GROUP // PAIR):
        cols = slice(pr * PAIR, (pr + 1) * PAIR)
        q = turn(qa[:, cols], cosine, low, high).astype(BF).astype(F32) * 0.125
        k = turn(ka[:, cols], cosine, low, high)
        v = va[:, cols]
        q_out[:, cols] = q.astype(BF)
        k_out[:, cols] = k.astype(BF)
        v_out[:, cols] = v.astype(BF)
        qh, kh, vh = [], [], []
        for h in range(2):
            mine = head_lanes((rows, PAIR), h)
            spare = lane == (HEAD if h == 0 else 0)
            qh.append(jnp.where(mine, q, jnp.where(spare, 1.0, 0.0)).astype(BF))
            kh.append(jnp.where(mine, k, jnp.where(spare, kbias, 0.0)).astype(BF))
            vh.append(jnp.where(mine, v, 0.0).astype(BF))
        for i in range(nq):
            base = i * (i + 1) // 2 * QB
            ext = (i + 1) * QB
            mixed = None
            for h in range(2):
                s = dot(qh[h][i * QB : ext], kh[h][:ext], NT)
                tail = jnp.where(diag, s[:, i * QB :], MASKED)
                s = tail if i == 0 else jnp.concatenate([s[:, : i * QB], tail], axis=1)
                e = jnp.exp(s - jnp.max(s, axis=-1, keepdims=True))
                p = (e * (1.0 / jnp.sum(e, axis=-1, keepdims=True))).astype(BF)
                for kb in range(i + 1):
                    p_out[2 * pr + h, base + kb * QB : base + (kb + 1) * QB, :] = p[:, kb * QB : (kb + 1) * QB]
                part = dot(p, vh[h][:ext])
                mixed = part if mixed is None else mixed + part
            att_out[i * QB : ext, cols] = (mixed * live_f[i * QB : ext]).astype(BF)
    out = dot(att_out[...], wo[...])

    @pl.when(pl.program_id(0) == 0)
    def _():
        acc[...] = mlp[...].astype(F32) + out

    @pl.when(pl.program_id(0) > 0)
    def _():
        act_low[...] = (acc[: rows // 2] + out[: rows // 2]).astype(BF)
        act_high[...] = (acc[rows // 2 :] + out[rows // 2 :]).astype(BF)


def mlp_back_kernel(tab, *refs):
    normed, cot, dg = refs[:3]
    w_in = refs[3 : 3 + SPLIT]
    w_out = refs[3 + SPLIT : 3 + 2 * SPLIT]
    gb_out, ng_out, keep, send, stage, sems = refs[3 + 2 * SPLIT :]
    j = pl.program_id(0)
    steps = pl.num_programs(0)
    npos = stage.shape[0]
    half = npos // 2
    unit_rows = normed.shape[1] // npos
    wi = jnp.concatenate([r[...] for r in w_in], axis=1)
    wout = jnp.concatenate([r[...] for r in w_out], axis=0)
    x, c = normed[...], cot[...]
    pg = dot(c, wout, NT) * dg[...].astype(F32)
    gb_out[...] = jnp.sum(pg, axis=0, keepdims=True)
    pg = pg.astype(BF)
    part = dot(pg, wi, NT)
    gi = dot(x, pg, TN).astype(BF)
    for s in range(SPLIT):
        place = tab[64 + j * SPLIT + s]
        row = pl.multiple_of(place // SPLIT * unit_rows, unit_rows)
        lane = pl.multiple_of(place % SPLIT * UNIT, UNIT)
        for i in range(npos):
            stage[tab[16 + i], pl.ds(row, unit_rows), pl.ds(lane, UNIT)] = (
                gi[i * unit_rows : (i + 1) * unit_rows, s * UNIT : (s + 1) * UNIT])

    @pl.when(j == 0)
    def _():
        ng_out[...] = part

    @pl.when(j > 0)
    def _():
        ng_out[...] += part

    @pl.when(j == steps - 1)
    def _():
        one = pltpu.make_async_copy(stage.at[pl.ds(half, half)], send, sems.at[0])
        two = pltpu.make_async_copy(stage.at[pl.ds(0, half)], keep, sems.at[1])
        one.start()
        two.start()
        one.wait()
        two.wait()


def attn_back_kernel(g, last, tab, off, leng, cot, att, q_in, k_in, v_in, wo, cos_ref, low_ref, high_ref,
                     p_hbm, x_hbm, w_hbm, ng_hbm, *refs):
    ng_out = refs[:-10]
    keep, send, stage, dk_acc, dv_acc, p_in, x_in, w_in, ng_in, sems = refs[-10:]
    rows = cot.shape[0]
    width = cot.shape[1]
    nq = rows // QB
    npos = stage.shape[0]
    half = npos // 2
    unit_rows = width // npos
    pairs = GROUP // PAIR
    loads = []
    for pr in range(pairs):
        loads.append(pltpu.make_async_copy(
            p_hbm.at[pl.ds(g * 2 * pairs + 2 * pr, 2)], p_in.at[pl.ds(2 * pr, 2)], sems.at[pr]))
    loads.append(pltpu.make_async_copy(x_hbm, x_in, sems.at[pairs]))
    for n in range(3):
        col = pl.multiple_of(n * width + tab[48] * (width // 2) + g * GROUP, GROUP)
        loads.append(pltpu.make_async_copy(w_hbm.at[:, pl.ds(col, GROUP)], w_in.at[n], sems.at[pairs + 1 + n]))
    loads.append(pltpu.make_async_copy(ng_hbm, ng_in, sems.at[pairs + 4]))
    for one in loads:
        one.start()
    start = off[0]
    stop = start + leng[0]
    place = lax.broadcasted_iota(jnp.int32, (rows, GROUP), 0)
    live = (place >= start) & (place < stop)
    do = jnp.where(live, dot(cot[...], wo[...], NT), 0.0)
    cosine, low, high = cos_ref[...], low_ref[...], high_ref[...]
    dqs, dks, dvs = [], [], []
    zero = jnp.zeros((), BF)
    for pr in range(pairs):
        loads[pr].wait()
        cols = slice(pr * PAIR, (pr + 1) * PAIR)
        q, k, v = q_in[:, cols], k_in[:, cols], v_in[:, cols]
        dob = do[:, cols].astype(BF)
        prod = dob.astype(F32) * att[:, g * GROUP + pr * PAIR : g * GROUP + (pr + 1) * PAIR].astype(F32)
        qh, kh, doh, delta = [], [], [], []
        for h in range(2):
            mine = head_lanes((rows, PAIR), h)
            qh.append(jnp.where(mine, q, zero))
            kh.append(jnp.where(mine, k, zero))
            doh.append(jnp.where(mine, dob, zero))
            delta.append(jnp.sum(jnp.where(mine, prod, 0.0), axis=-1, keepdims=True))
        dq_parts = [None] * nq
        for i in reversed(range(nq)):
            base = i * (i + 1) // 2 * QB
            ext = (i + 1) * QB
            blk = slice(i * QB, ext)
            dq_i, dk_i, dv_i = None, None, None
            for h in range(2):
                p = jnp.concatenate(
                    [p_in[2 * pr + h, base + kb * QB : base + (kb + 1) * QB, :] for kb in range(i + 1)], axis=1)
                dp = dot(doh[h][blk], v[:ext], NT)
                ds = (p.astype(F32) * (dp - delta[h][blk])).astype(BF)
                dv_h = dot(doh[h][blk], p, TN)
                dk_h = dot(qh[h][blk], ds, TN)
                dq_h = dot(ds, kh[h][:ext])
                dv_i = dv_h if dv_i is None else dv_i + dv_h
                dk_i = dk_h if dk_i is None else dk_i + dk_h
                dq_i = dq_h if dq_i is None else dq_i + dq_h
            dq_parts[i] = dq_i
            if i == nq - 1:
                dk_acc[...] = dk_i
                dv_acc[...] = dv_i
            else:
                dk_acc[:, :ext] += dk_i
                dv_acc[:, :ext] += dv_i
        dq = jnp.concatenate(dq_parts, axis=0) * 0.125
        dqs.append(turn_back(dq, cosine, low, high).astype(BF))
        dks.append(turn_back(dk_acc[...].T, cosine, low, high).astype(BF))
        dvs.append(dv_acc[...].T.astype(BF))
    grads = [jnp.concatenate(t, axis=1) for t in (dqs, dks, dvs)]
    for one in loads[pairs:]:
        one.wait()
    total = ng_in[...]
    for n in range(3):
        total = total + dot(grads[n], w_in[n], NT)
    per = rows // len(ng_out)
    for n, to in enumerate(ng_out):
        to[...] = total[n * per : (n + 1) * per].astype(to.dtype)
    x = x_in[...]
    for n, d in enumerate(grads):
        grad = dot(x, d, TN).astype(BF)
        for i in range(npos):
            stage[tab[16 + i], n * unit_rows : (n + 1) * unit_rows, :] = grad[i * unit_rows : (i + 1) * unit_rows]
    if not last:
        gao = dot(att[...], cot[...], TN).astype(BF)
        gao_rows = gao.shape[0] // npos
        for i in range(npos):
            for n in range(width // GROUP):
                at = 3 * unit_rows + n * gao_rows
                stage[tab[32 + i], at : at + gao_rows, :] = (
                    gao[i * gao_rows : (i + 1) * gao_rows, n * GROUP : (n + 1) * GROUP])
    one = pltpu.make_async_copy(stage.at[pl.ds(half, half)], send, sems.at[0])
    two = pltpu.make_async_copy(stage.at[pl.ds(0, half)], keep, sems.at[1])
    one.start()
    two.start()
    one.wait()
    two.wait()


def small_kernel(unit_ref, cot, *refs):
    parts, out = refs[:-1], refs[-1]

    @pl.when(pl.program_id(0) == 0)
    def _():
        out[...] = jnp.zeros_like(out)

    unit = unit_ref[...].astype(F32)
    out[2:3] += jnp.sum(cot[...].astype(F32), axis=0, keepdims=True)
    for n, part in enumerate(parts):
        @pl.when(pl.program_id(0) == n)
        def _():
            full = part[...].astype(F32)
            out[0:1] += jnp.sum(full * unit, axis=0, keepdims=True)
            out[1:2] += jnp.sum(full, axis=0, keepdims=True)


def act_kernel(tok, bias, own_low, own_high, recv_low, recv_high, out):
    base = tok[...].astype(F32) + bias[...]
    steps = pl.num_programs(0)

    @pl.when(pl.program_id(0) < steps // 2)
    def _():
        out[...] = (base + (own_low[...].astype(F32) + recv_low[...].astype(F32))).astype(BF)

    @pl.when(pl.program_id(0) >= steps // 2)
    def _():
        out[...] = (base + (own_high[...].astype(F32) + recv_high[...].astype(F32))).astype(BF)


def finish_kernel(unit_ref, inv, cot, ng_a, ng_b, gain, *refs):
    out = refs[-1]
    unit = unit_ref[...].astype(F32)
    scaled = (ng_a[...].astype(F32) + ng_b[...].astype(F32)) * gain[...]
    mean = jnp.mean(scaled, axis=-1, keepdims=True)
    lean = jnp.mean(scaled * unit, axis=-1, keepdims=True)
    out[...] = (cot[...].astype(F32) + inv[:, :1] * (scaled - mean - unit * lean)).astype(BF)


def const_spec(shape):
    zeros = (0,) * len(shape)
    return pl.BlockSpec(shape, lambda g, *tabs: zeros, pipeline_mode=pl.Buffered(1))


def params():
    return pltpu.CompilerParams(vmem_limit_bytes=LIMIT)


def rotary_tables(rows):
    lane = np.arange(PAIR) % HEAD
    half = ROT // 2
    angle = np.arange(rows)[:, None] * np.power(10000.0, (lane % half) * (-2.0 / ROT))[None, :]
    inside = (lane < ROT)[None, :]
    cosine = np.where(inside, np.cos(angle), 1.0)
    low = np.where((lane < half)[None, :], -np.sin(angle), 0.0)
    high = np.where(inside & (lane >= half)[None, :], np.sin(angle), 0.0)
    return [jnp.asarray(t, F32) for t in (cosine, low, high)]


def mlp_specs(width):
    w_in = [pl.BlockSpec((width, UNIT), lambda j, t, s=s: (0, t[j * SPLIT + s])) for s in range(SPLIT)]
    b_in = [pl.BlockSpec((1, UNIT), lambda j, t, s=s: (0, t[j * SPLIT + s])) for s in range(SPLIT)]
    w_out = [pl.BlockSpec((UNIT, width), lambda j, t, s=s: (t[j * SPLIT + s], 0)) for s in range(SPLIT)]
    return w_in, b_in, w_out


def mlp_forward(tab, tokens, gain, bias, w_in, b_in, w_out, npos):
    rows, width = tokens.shape
    wi, bi, wo = mlp_specs(width)
    wide = SPLIT * UNIT
    hspec = pl.BlockSpec((rows, wide), lambda j, t: (0, j))
    hid = jax.ShapeDtypeStruct((rows, npos * UNIT), BF)
    full = jax.ShapeDtypeStruct((rows, width), BF)
    return pl.pallas_call(
        mlp_fwd_kernel,
        grid_spec=pltpu.PrefetchScalarGridSpec(
            num_scalar_prefetch=1,
            grid=(npos // SPLIT,),
            in_specs=[const_spec((rows, width)), const_spec((1, width)), const_spec((1, width))] + wi + bi + wo,
            out_specs=[const_spec((rows, width)), const_spec((rows, width)), const_spec((rows, PAIR)), hspec, hspec,
                       const_spec((rows, width))],
            scratch_shapes=[pltpu.VMEM((rows, width), F32)],
        ),
        out_shape=[full, full, jax.ShapeDtypeStruct((rows, PAIR), F32), hid, hid, full],
        compiler_params=params(),
        cost_estimate=pl.CostEstimate(flops=20 * 10**9, bytes_accessed=10**7, transcendentals=0),
        name="mlp_forward",
    )(tab, tokens, gain, bias, *([w_in] * SPLIT), *([b_in] * SPLIT), *([w_out] * SPLIT))


def out_grad(hid, cot, npos):
    rows, width = cot.shape
    wide = SPLIT * UNIT
    steps = npos // SPLIT
    part = jax.ShapeDtypeStruct((npos // 2, 2 * UNIT, 512), BF)
    block = (SPLIT, 2 * UNIT, 512)
    return pl.pallas_call(
        out_grad_kernel,
        grid=(steps,),
        in_specs=[pl.BlockSpec((rows, wide), lambda j: (0, (j + steps // 2) % steps)),
                  pl.BlockSpec((rows, width), lambda j: (0, 0), pipeline_mode=pl.Buffered(1))],
        out_specs=[pl.BlockSpec(block, lambda j: (jnp.maximum(j - steps // 2, 0), 0, 0)),
                   pl.BlockSpec(block, lambda j: (jnp.minimum(j, steps // 2 - 1), 0, 0))],
        out_shape=[part, part],
        compiler_params=params(),
        cost_estimate=pl.CostEstimate(flops=20 * 10**9, bytes_accessed=10**7, transcendentals=0),
        name="out_grad",
    )(hid, cot)


def attn_forward(b_tab, off, leng, normed, mlp_out, w_qkv, w_ao, tables):
    rows, width = normed.shape
    groups = width // 2 // GROUP
    wspec = lambda n: pl.BlockSpec((width, GROUP), lambda g, t, o, l: (0, n * 2 * groups + t[0] * groups + g))
    ospec = pl.BlockSpec((rows, GROUP), lambda g, *t: (0, g))
    tri = (rows // QB) * (rows // QB + 1) // 2 * QB
    half = jax.ShapeDtypeStruct((rows, width // 2), BF)
    return pl.pallas_call(
        attn_fwd_kernel,
        grid_spec=pltpu.PrefetchScalarGridSpec(
            num_scalar_prefetch=3,
            grid=(groups,),
            in_specs=[const_spec((rows, width)), wspec(0), wspec(1), wspec(2),
                      pl.BlockSpec((GROUP, width), lambda g, t, o, l: (t[0] * groups + g, 0)),
                      const_spec((rows, width))] + [const_spec((rows, PAIR))] * 3,
            out_specs=[ospec, ospec, ospec,
                       pl.BlockSpec((GROUP // HEAD, tri, QB), lambda g, *t: (g, 0, 0)), ospec,
                       const_spec((rows // 2, width)), const_spec((rows // 2, width))],
            scratch_shapes=[pltpu.VMEM((rows, width), F32)],
        ),
        out_shape=[half, half, half,
                   jax.ShapeDtypeStruct((HEADS // 2, tri, QB), BF), half]
        + [jax.ShapeDtypeStruct((rows // 2, width), BF)] * 2,
        compiler_params=params(),
        cost_estimate=pl.CostEstimate(flops=20 * 10**9, bytes_accessed=10**7, transcendentals=0),
        name="attention_forward",
    )(b_tab, off, leng, normed, w_qkv, w_qkv, w_qkv, w_ao, mlp_out, *tables)


def mlp_backward(tab, normed, cot, dg, w_in, w_out, npos):
    rows, width = normed.shape
    wi, _, wo = mlp_specs(width)
    wide = SPLIT * UNIT
    unit_rows = width // npos
    ublock = npos // SPLIT * unit_rows
    part = jax.ShapeDtypeStruct((npos // 2, ublock, 512), BF)
    anyspec = pl.BlockSpec(memory_space=pl.ANY)
    return pl.pallas_call(
        mlp_back_kernel,
        grid_spec=pltpu.PrefetchScalarGridSpec(
            num_scalar_prefetch=1,
            grid=(npos // SPLIT,),
            in_specs=[const_spec((rows, width)), const_spec((rows, width)),
                      pl.BlockSpec((rows, wide), lambda j, t: (0, j))] + wi + wo,
            out_specs=[pl.BlockSpec((1, wide), lambda j, t: (0, j)), const_spec((rows, width)), anyspec, anyspec],
            scratch_shapes=[pltpu.VMEM((npos, ublock, 512), BF), pltpu.SemaphoreType.DMA((2,))],
        ),
        out_shape=[jax.ShapeDtypeStruct((1, npos * UNIT), F32), jax.ShapeDtypeStruct((rows, width), F32), part, part],
        compiler_params=params(),
        cost_estimate=pl.CostEstimate(flops=20 * 10**9, bytes_accessed=10**7, transcendentals=0),
        name="mlp_backward",
    )(tab, normed, cot, dg, *([w_in] * SPLIT), *([w_out] * SPLIT))


def attn_backward(g, last, tab, off, leng, normed, cot, att, q, k, v, p, w_qkv, w_ao, ng, tables, npos):
    rows, width = normed.shape
    groups = width // 2 // GROUP
    ospec = pl.BlockSpec((rows, GROUP), lambda i, *t: (0, g))
    tri = p.shape[1]
    ublock = 3 * (width // npos) + (0 if last else width // GROUP * (width // 2 // npos))
    anyspec = pl.BlockSpec(memory_space=pl.ANY)
    part = jax.ShapeDtypeStruct((npos // 2, ublock, GROUP), BF)
    parts = CHUNKS if last else 1
    return pl.pallas_call(
        functools.partial(attn_back_kernel, g, last),
        grid_spec=pltpu.PrefetchScalarGridSpec(
            num_scalar_prefetch=3,
            grid=(1,),
            in_specs=[const_spec((rows, width)), const_spec((rows, width // 2))] + [ospec] * 3
            + [pl.BlockSpec((GROUP, width), lambda i, t, o, l: (t[48] * groups + g, 0))]
            + [const_spec((rows, PAIR))] * 3 + [anyspec] * 4,
            out_specs=[const_spec((rows // parts, width))] * parts + [anyspec, anyspec],
            scratch_shapes=[pltpu.VMEM((npos, ublock, GROUP), BF),
                            pltpu.VMEM((PAIR, rows), F32), pltpu.VMEM((PAIR, rows), F32),
                            pltpu.VMEM((GROUP // HEAD, tri, QB), BF), pltpu.VMEM((rows, width), BF),
                            pltpu.VMEM((3, width, GROUP), BF), pltpu.VMEM((rows, width), F32),
                            pltpu.SemaphoreType.DMA((7,))],
        ),
        out_shape=[jax.ShapeDtypeStruct((rows // parts, width), BF if last else F32)] * parts + [part, part],
        compiler_params=params(),
        cost_estimate=pl.CostEstimate(flops=20 * 10**9, bytes_accessed=10**7, transcendentals=0),
        name="attention_backward",
    )(tab, off, leng, cot, att, q, k, v, w_ao, *tables, p, normed, w_qkv, ng)


def small_sums(unit, cot, parts):
    rows, width = unit.shape
    step = rows // len(parts)
    row = pl.BlockSpec((step, width), lambda r: (r, 0))
    return pl.pallas_call(
        small_kernel,
        grid=(len(parts),),
        in_specs=[row] * 2 + [pl.BlockSpec((step, width), lambda r: (0, 0))] * len(parts),
        out_specs=pl.BlockSpec((8, width), lambda r: (0, 0)),
        out_shape=jax.ShapeDtypeStruct((8, width), F32),
        compiler_params=params(),
        cost_estimate=pl.CostEstimate(flops=10**7, bytes_accessed=6 * 10**6, transcendentals=0),
        name="small_sums",
    )(unit, cot, *parts)


def act_sum(tokens, bias, own, recv):
    rows, width = tokens.shape
    steps = rows // QB
    row = pl.BlockSpec((QB, width), lambda r: (r, 0))
    low = pl.BlockSpec((QB, width), lambda r: (jnp.minimum(r, steps // 2 - 1), 0))
    high = pl.BlockSpec((QB, width), lambda r: (jnp.maximum(r - steps // 2, 0), 0))
    return pl.pallas_call(
        act_kernel,
        grid=(steps,),
        in_specs=[row, pl.BlockSpec((1, width), lambda r: (0, 0)), low, high, low, high],
        out_specs=row,
        out_shape=jax.ShapeDtypeStruct((rows, width), BF),
        compiler_params=params(),
        cost_estimate=pl.CostEstimate(flops=10**7, bytes_accessed=10**7, transcendentals=0),
        name="activations",
    )(tokens, bias, *own, *recv)


def finish(n, unit, inv, cot, ng_a, ng_b, gain, done):
    rows, width = unit.shape
    total = ng_a.shape[0]
    step = min(128, total)
    at = n * total // step
    row = pl.BlockSpec((step, width), lambda r: (at + r, 0))
    part = pl.BlockSpec((step, width), lambda r: (r, 0))
    return pl.pallas_call(
        finish_kernel,
        grid=(total // step,),
        in_specs=[row, pl.BlockSpec((step, PAIR), lambda r: (at + r, 0)), row, part, part,
                  pl.BlockSpec((1, width), lambda r: (0, 0))]
        + [pl.BlockSpec(memory_space=pl.ANY)] * len(done),
        out_specs=row,
        out_shape=jax.ShapeDtypeStruct((rows, width), BF),
        input_output_aliases={6: 0} if done else {},
        compiler_params=params(),
        cost_estimate=pl.CostEstimate(flops=10**7, bytes_accessed=10**7, transcendentals=0),
        name="norm_backward",
    )(unit, inv, cot, ng_a, ng_b, gain, *done)


def bit_reverse(value, bits):
    out = 0
    for n in range(bits):
        out |= (value >> n & 1) << (bits - 1 - n)
    return out


NPOS = 16
CHUNKS = 4


def place_tables(ndp):
    bits = NPOS.bit_length() - 1
    table = np.zeros((ndp, 2, 80), np.int32)
    for d in range(ndp):
        for b in range(2):
            for n in range(NPOS):
                if ndp == NPOS:
                    table[d, b, n] = 2 * (bit_reverse(n, bits) ^ d) + b
                    table[d, b, 64 + n] = bit_reverse(n, bits) ^ d
                    table[d, b, 16 + n] = bit_reverse(n ^ d, bits)
                    rel = 0
                    for k in range(bits - 1):
                        rel |= ((n >> (k + 1) & 1) ^ (d >> k & 1)) << (bits - 1 - k)
                    rel |= (n & 1) ^ (d >> (bits - 1) & 1)
                    table[d, b, 32 + n] = rel
                else:
                    table[d, b, n] = b * NPOS + n
                    table[d, b, 64 + n] = n
                    table[d, b, 16 + n] = n
                    table[d, b, 32 + n] = n
            table[d, b, 48] = b
    return table


def after(values, *others):
    out = lax.optimization_barrier((values,) + others)
    return out[0]


def trade(send, bit, ndp):
    return lax.ppermute(send, "dp", [(d, d ^ bit) for d in range(ndp)])


def add_halves(keep, recv):
    half = keep.shape[0] // 2
    mine = (keep[:half].astype(F32) + recv[:half].astype(F32)).astype(BF)
    other = (keep[half:].astype(F32) + recv[half:].astype(F32)).astype(BF)
    return mine, other


def place_columns_kernel(tab, own, recv, out):
    b = tab[48]
    for n in range(NPOS):
        step, s = n // SPLIT, n % SPLIT
        col = slice(s * UNIT, (s + 1) * UNIT)
        mine = (2 * n + b) * UNIT
        theirs = (2 * n + 1 - b) * UNIT
        out[:, pl.ds(pl.multiple_of(mine, UNIT), UNIT)] = own[step, :, col].astype(F32)
        out[:, pl.ds(pl.multiple_of(theirs, UNIT), UNIT)] = recv[step, :, col].astype(F32)


def shards(ndp, tokens, offsets, lengths, cotangent, ln_gain, ln_bias, w_qkv, w_attn_out, w_in, b_in, w_out, b_out):
    rows, width = tokens.shape
    dp = lax.axis_index("dp")
    b = lax.axis_index("branch")
    hidden = w_in.shape[1]
    tables = rotary_tables(rows)
    all_tab = jnp.asarray(place_tables(ndp))
    tab = lax.dynamic_slice(all_tab, (dp, b, 0), (1, 1, 80)).reshape(80)
    b_tab = lax.dynamic_slice(all_tab, (dp, b, 48), (1, 1, 1)).reshape(1)
    gain = ln_gain.reshape(1, width)
    bias = ln_bias.reshape(1, width)
    swap = [(0, 1), (1, 0)]
    halving = ndp == NPOS

    normed, unit, inv, hid, dg, mlp_out = mlp_forward(tab, tokens, gain, bias, w_in, b_in.reshape(1, hidden), w_out, NPOS)
    a_keep, a_send = out_grad(hid, cotangent, NPOS)
    a_part = (a_keep, a_send)
    a_recv = trade(a_send, 1, ndp) if halving else a_send
    q, k, v, p, att, *act_own = attn_forward(
        b_tab, offsets, lengths, after(normed, a_send), mlp_out, w_qkv, w_attn_out, tables)
    act_recv = [lax.ppermute(part, "branch", swap) for part in act_own]
    barrier = lax.optimization_barrier
    a_recv, att = barrier((a_recv, att))
    if halving:
        a_keep, a_send = add_halves(a_keep, a_recv)
        a_recv = trade(a_send, 2, ndp)
    gb_in, ng, b_keep, b_send = mlp_backward(tab, normed, cotangent, after(dg, att, a_send), w_in, w_out, NPOS)
    b_part = (b_keep, b_send)
    a_recv, b_send, ng, act_recv[0] = barrier((a_recv, b_send, ng, act_recv[0]))
    if halving:
        b_recv = trade(b_send, 1, ndp)
        a_keep, a_send = add_halves(a_keep, a_recv)
        a_recv = trade(a_send, 4, ndp)
        b_keep, b_send = add_halves(b_keep, b_recv)
        b_recv = trade(b_send, 2, ndp)
    else:
        b_recv = b_send
    ng, c_keep, c_send = attn_backward(0, False, tab, offsets, lengths, normed, cotangent, after(att, a_send, b_send),
                                       q, k, v, p, w_qkv, w_attn_out, ng, tables, NPOS)
    c_part = (c_keep, c_send)
    a_recv, b_recv, c_send, ng, act_recv[1] = barrier((a_recv, b_recv, c_send, ng, act_recv[1]))
    c_recv = trade(c_send, 1, ndp) if halving else c_send
    activations = act_sum(tokens, b_out.reshape(1, width), act_own, act_recv)
    activations, c_recv, ng = barrier((activations, c_recv, ng))
    if halving:
        c_keep, c_send = add_halves(c_keep, c_recv)
        c_recv = trade(c_send, 2, ndp)
        a_keep, a_send = add_halves(a_keep, a_recv)
        a_recv = trade(a_send, 8, ndp)
        b_keep, b_send = add_halves(b_keep, b_recv)
        b_recv = trade(b_send, 4, ndp)
    *ng_own, d_keep, d_send = attn_backward(
        1, True, tab, offsets, lengths, normed, cotangent, after(att, a_send, b_send, c_send),
        q, k, v, p, w_qkv, w_attn_out, ng, tables, NPOS)
    if halving:
        a_recv, b_recv, c_recv, d_send = barrier((a_recv, b_recv, c_recv, d_send))
    ng_recv = [lax.ppermute(part, "branch", swap) for part in ng_own]
    small = small_sums(unit, cotangent, ng_own)
    if not halving:
        input_grad = ()
        for n in range(CHUNKS):
            input_grad = (finish(n, unit, inv, cotangent, ng_own[n], ng_recv[n], gain, input_grad),)
        return (activations,) + input_grad + natural_sums(
            b, a_part, b_part, c_part, (d_keep, d_send), small, gb_in, width, hidden)

    vec = small[:3]
    hb = gb_in.reshape(NPOS, UNIT)

    def vec_out(hb, vec, bit):
        count = hb.shape[0] // 2
        return trade(jnp.concatenate([hb[count:].reshape(-1), vec.reshape(-1)]), bit, ndp)

    def vec_add(hb, vec, got):
        count = hb.shape[0] // 2
        return (hb[:count] + got[: count * UNIT].reshape(count, UNIT), vec + got[count * UNIT :].reshape(vec.shape))

    d_recv = trade(d_send, 1, ndp)
    c_keep, c_send = add_halves(c_keep, c_recv)
    c_recv = trade(c_send, 4, ndp)
    b_keep, b_send = add_halves(b_keep, b_recv)
    b_recv = trade(b_send, 8, ndp)
    got = vec_out(hb, vec, 1)
    d_recv, c_recv, b_recv, got, ng_recv[0] = barrier((d_recv, c_recv, b_recv, got, ng_recv[0]))
    d_keep, d_send = add_halves(d_keep, d_recv)
    d_recv = trade(d_send, 2, ndp)
    c_keep, c_send = add_halves(c_keep, c_recv)
    c_recv = trade(c_send, 8, ndp)
    hb, vec = vec_add(hb, vec, got)
    got = vec_out(hb, vec, 2)
    grad = finish(0, unit, inv, cotangent, ng_own[0], after(ng_recv[0], d_send, c_send), gain, ())
    d_recv, c_recv, got, ng_recv[1], grad = barrier((d_recv, c_recv, got, ng_recv[1], grad))
    d_keep, d_send = add_halves(d_keep, d_recv)
    d_recv = trade(d_send, 4, ndp)
    hb, vec = vec_add(hb, vec, got)
    got = vec_out(hb, vec, 4)
    grad = finish(1, unit, inv, cotangent, ng_own[1], after(ng_recv[1], d_send), gain, (grad,))
    d_recv, got, ng_recv[2], grad = barrier((d_recv, got, ng_recv[2], grad))
    d_keep, d_send = add_halves(d_keep, d_recv)
    d_recv = trade(d_send, 8, ndp)
    hb, vec = vec_add(hb, vec, got)
    got = vec_out(hb, vec, 8)
    grad = finish(2, unit, inv, cotangent, ng_own[2], after(ng_recv[2], d_send), gain, (grad,))
    d_recv, got, grad = barrier((d_recv, got, grad))
    hb, vec = vec_add(hb, vec, got)
    input_grad = finish(3, unit, inv, cotangent, ng_own[3], ng_recv[3], gain, (grad,))
    ga, gb, gc, gd = [keep[0].astype(F32) + recv[0].astype(F32)
                      for keep, recv in ((a_keep, a_recv), (b_keep, b_recv), (c_keep, c_recv), (d_keep, d_recv))]

    unit_rows = width // NPOS
    sub = unit_rows // 2
    steps = NPOS // SPLIT
    g_out = ga.reshape(2, UNIT, 512).transpose(1, 0, 2).reshape(UNIT, width)
    gi = gb.reshape(steps, unit_rows, 512)
    gq = jnp.concatenate([gc[: 3 * unit_rows].reshape(3, unit_rows, GROUP), gd.reshape(3, unit_rows, GROUP)], axis=2)
    both = jnp.concatenate([gi, gq], axis=0)
    own = lax.dynamic_slice_in_dim(both, b * sub, sub, 1)
    away = lax.dynamic_slice_in_dim(both, (1 - b) * sub, sub, 1).astype(BF)
    recv = lax.ppermute(away, "branch", swap)
    g_in = pl.pallas_call(
        place_columns_kernel,
        grid_spec=pltpu.PrefetchScalarGridSpec(
            num_scalar_prefetch=1, grid=(1,),
            in_specs=[const_spec((steps, sub, 512))] * 2,
            out_specs=const_spec((sub, hidden)),
        ),
        out_shape=jax.ShapeDtypeStruct((sub, hidden), F32),
        compiler_params=params(),
        name="place_columns",
    )(tab, own[:steps], recv[:steps])
    mine, theirs = own[steps:], recv[steps:].astype(F32)
    first = jnp.where(b == 0, mine, theirs)
    second = jnp.where(b == 0, theirs, mine)
    g_qkv = jnp.concatenate(sum([[first[n], second[n]] for n in range(3)], []), axis=1)
    gao_rows = width // 2 // NPOS
    gao = gc[3 * unit_rows :].reshape(width // GROUP, gao_rows, GROUP).transpose(1, 0, 2).reshape(gao_rows, width)
    top = ndp // 2
    pairs = [(d * 2 + c, (d ^ top) * 2 + 1 - c) for d in range(ndp) for c in range(2) if d // top != c]
    moved = lax.ppermute(gao.astype(BF), ("dp", "branch"), pairs).astype(F32)
    g_ao = jnp.where(dp // top == b, gao, moved)

    pair = vec[:2] + lax.ppermute(vec[:2], "branch", swap)
    vec = jnp.concatenate([pair, vec[2:]], axis=0)
    per = width // (2 * ndp)
    cut = lax.dynamic_slice(vec, (0, (dp * 2 + b) * per), (3, per))
    return (activations, input_grad, cut[0], cut[1], g_qkv, g_ao, g_in, hb.reshape(UNIT), g_out, cut[2])


def natural_sums(b, a_part, b_part, c_part, d_part, small, gb_in, width, hidden):
    axes = ("dp", "branch")
    steps = NPOS // SPLIT
    unit_rows = width // NPOS
    wa, wb, wc, wd = [jnp.concatenate(part, axis=0).astype(F32) for part in (a_part, b_part, c_part, d_part)]
    go = wa.reshape(NPOS, 2, UNIT, 512).transpose(0, 2, 1, 3).reshape(NPOS * UNIT, width)
    gi = wb.reshape(NPOS, steps, unit_rows, 512).transpose(0, 2, 1, 3)
    gi = gi.reshape(width, hidden // 2)
    gq = jnp.concatenate([w[:, : 3 * unit_rows].reshape(NPOS, 3, unit_rows, GROUP) for w in (wc, wd)], axis=3)
    gq = gq.transpose(0, 2, 1, 3).reshape(width, 3, 2 * GROUP)
    gao_rows = width // 2 // NPOS
    ga = wc[:, 3 * unit_rows :].reshape(NPOS, width // GROUP, gao_rows, GROUP).transpose(0, 2, 1, 3)
    ga = ga.reshape(NPOS * gao_rows, width)

    def scatter(part, full, dim):
        starts = [0] * part.ndim
        starts[dim] = b * part.shape[dim]
        whole = lax.dynamic_update_slice(jnp.zeros(full, F32), part, starts)
        return lax.psum_scatter(whole, axes, scatter_dimension=0, tiled=True)

    total = lambda t: lax.psum_scatter(t, axes, scatter_dimension=0, tiled=True)
    g_qkv = scatter(gq, (width, 3, width), 2)
    return (
        total(small[0]),
        total(small[1]),
        g_qkv.reshape(g_qkv.shape[0], 3 * width),
        scatter(ga, (width, width), 0),
        scatter(gi, (width, hidden), 1),
        scatter(gb_in.reshape(-1), (hidden,), 0),
        scatter(go, (hidden, width), 0),
        total(jnp.where(b == 0, small[2], 0.0)),
    )


def solution(mesh):
    return jax.shard_map(
        functools.partial(shards, mesh.shape["dp"]),
        mesh=mesh,
        in_specs=(P("dp", None), P("dp"), P("dp"), P("dp", None)) + (P(),) * 8,
        out_specs=(
            P("dp", None),
            P("dp", None),
            P(("dp", "branch")),
            P(("dp", "branch")),
            P(("dp", "branch"), None),
            P(("dp", "branch"), None),
            P(("dp", "branch"), None),
            P(("dp", "branch")),
            P(("dp", "branch"), None),
            P(("dp", "branch")),
        ),
        check_vma=False,
    )
```

```python
import functools

import jax
import jax.numpy as jnp
import numpy as np
from jax import lax
from jax.experimental import pallas as pl
from jax.experimental.pallas import tpu as pltpu
from jax.sharding import PartitionSpec as P

HEADS = 16
HEAD = 64
ROT = 32
EPSILON = 1e-05
MASKED = -1e30
BF = jnp.bfloat16
F32 = jnp.float32
QB = 256
PAIR = 128
GROUP = 256
UNIT = 128
SPLIT = 4
LIMIT = 60 * 2**20
MAIN = 36 * 2**20

NN = (((1,), (0,)), ((), ()))
NT = (((1,), (1,)), ((), ()))
TN = (((0,), (0,)), ((), ()))


def dot(left, right, dims=NN):
    return lax.dot_general(left, right, dims, preferred_element_type=F32)


def norm_stats(rows):
    x = rows.astype(F32)
    mean = jnp.mean(x, axis=-1, keepdims=True)
    centred = x - mean
    inv = lax.rsqrt(jnp.mean(centred * centred, axis=-1, keepdims=True) + EPSILON)
    return centred * inv, inv


def gelu_both(u):
    c = 0.7978845608028654
    u2 = u * u
    t = jnp.tanh(u * (c + (c * 0.044715) * u2))
    half = 0.5 + 0.5 * t
    slope = u * (c + (3 * c * 0.044715) * u2)
    return u * half, half + 0.5 * slope * (1.0 - t * t)


def lanes(shape):
    return lax.broadcasted_iota(jnp.int32, shape, 1)


def head_lanes(shape, h):
    lane = lanes(shape)
    return (lane < HEAD) if h == 0 else (lane >= HEAD)


def turn(part, cosine, low, high):
    return part * cosine + pltpu.roll(part, PAIR - ROT // 2, 1) * low + pltpu.roll(part, ROT // 2, 1) * high


def turn_back(grad, cosine, low, high):
    return grad * cosine + pltpu.roll(grad * low, ROT // 2, 1) + pltpu.roll(grad * high, PAIR - ROT // 2, 1)


def mlp_fwd_kernel(tab, *refs):
    tok, gain, bias, cot = refs[:4]
    w_in = refs[4 : 4 + SPLIT]
    b_in = refs[4 + SPLIT : 4 + 2 * SPLIT]
    w_out = refs[4 + 2 * SPLIT : 4 + 3 * SPLIT]
    normed, unit_out, inv_out, dg_out, out_ref, keep, send, acc = refs[4 + 3 * SPLIT :]
    j = pl.program_id(0)
    last = pl.num_programs(0) - 1

    @pl.when(j == 0)
    def _():
        for r in range(0, tok.shape[0], QB):
            unit, inv = norm_stats(tok[r : r + QB])
            unit_out[r : r + QB] = unit.astype(BF)
            inv_out[r : r + QB] = jnp.broadcast_to(inv, (QB, PAIR))
            normed[r : r + QB] = (unit * gain[...] + bias[...]).astype(BF)

    wi = jnp.concatenate([r[...] for r in w_in], axis=1)
    bi = jnp.concatenate([r[...] for r in b_in], axis=1)
    wout = jnp.concatenate([r[...] for r in w_out], axis=0)
    hid, dg = gelu_both(dot(normed[...], wi) + bi)
    hid = hid.astype(BF)
    dg_out[...] = dg.astype(BF)
    out = dot(hid, wout)

    @pl.when(j == 0)
    def _():
        acc[...] = out

    @pl.when((j > 0) & (j < last))
    def _():
        acc[...] += out

    @pl.when(j == last)
    def _():
        out_ref[...] = (acc[...] + out).astype(BF)
    go = dot(hid, cot[...], TN).astype(BF)

    def store(to):
        for s in range(SPLIT):
            for n in range(2):
                to[s, n * UNIT : (n + 1) * UNIT, :] = go[s * UNIT : (s + 1) * UNIT, n * 512 : (n + 1) * 512]

    @pl.when(j <= last // 2)
    def _():
        store(send)

    @pl.when(j > last // 2)
    def _():
        store(keep)


def attn_fwd_kernel(b_tab, off, leng, x_ref, wq, wk, wv, wo, mlp, cos_ref, low_ref, high_ref,
                    q_out, k_out, v_out, p_out, att_out, act_low, act_high, acc):
    rows = x_ref.shape[0]
    nq = rows // QB
    x = x_ref[...]
    start = off[0]
    stop = start + leng[0]
    place = lax.broadcasted_iota(jnp.int32, (rows, PAIR), 0)
    live = (place >= start) & (place < stop)
    kbias = jnp.where(live, 0.0, MASKED)
    live_f = jnp.where(live, 1.0, 0.0)
    lane = lanes((rows, PAIR))
    diag = lax.broadcasted_iota(jnp.int32, (QB, QB), 0) >= lax.broadcasted_iota(jnp.int32, (QB, QB), 1)
    qa = dot(x, wq[...])
    ka = dot(x, wk[...])
    va = dot(x, wv[...])
    cosine, low, high = cos_ref[...], low_ref[...], high_ref[...]
    for pr in range(GROUP // PAIR):
        cols = slice(pr * PAIR, (pr + 1) * PAIR)
        q = turn(qa[:, cols], cosine, low, high).astype(BF).astype(F32) * 0.125
        k = turn(ka[:, cols], cosine, low, high)
        v = va[:, cols]
        q_out[:, cols] = q.astype(BF)
        k_out[:, cols] = k.astype(BF)
        v_out[:, cols] = v.astype(BF)
        qh, kh, vh = [], [], []
        for h in range(2):
            mine = head_lanes((rows, PAIR), h)
            spare = lane == (HEAD if h == 0 else 0)
            qh.append(jnp.where(mine, q, jnp.where(spare, 1.0, 0.0)).astype(BF))
            kh.append(jnp.where(mine, k, jnp.where(spare, kbias, 0.0)).astype(BF))
            vh.append(jnp.where(mine, v, 0.0).astype(BF))
        for i in range(nq):
            base = i * (i + 1) // 2 * QB
            ext = (i + 1) * QB
            mixed = None
            for h in range(2):
                s = dot(qh[h][i * QB : ext], kh[h][:ext], NT)
                tail = jnp.where(diag, s[:, i * QB :], MASKED)
                s = tail if i == 0 else jnp.concatenate([s[:, : i * QB], tail], axis=1)
                e = jnp.exp(s - jnp.max(s, axis=-1, keepdims=True))
                p = (e * (1.0 / jnp.sum(e, axis=-1, keepdims=True))).astype(BF)
                for kb in range(i + 1):
                    p_out[2 * pr + h, base + kb * QB : base + (kb + 1) * QB, :] = p[:, kb * QB : (kb + 1) * QB]
                part = dot(p, vh[h][:ext])
                mixed = part if mixed is None else mixed + part
            att_out[i * QB : ext, cols] = (mixed * live_f[i * QB : ext]).astype(BF)
    out = dot(att_out[...], wo[...])

    @pl.when(pl.program_id(0) == 0)
    def _():
        acc[...] = mlp[...].astype(F32) + out

    cut = act_low.shape[0]

    @pl.when(pl.program_id(0) > 0)
    def _():
        act_low[...] = (acc[:cut] + out[:cut]).astype(BF)
        act_high[...] = (acc[cut:] + out[cut:]).astype(BF)


def mlp_back_kernel(tab, *refs):
    normed, cot, dg = refs[:3]
    w_in = refs[3 : 3 + SPLIT]
    w_out = refs[3 + SPLIT : 3 + 2 * SPLIT]
    gb_out, ng_out, keep, send, stage, sems = refs[3 + 2 * SPLIT :]
    j = pl.program_id(0)
    steps = pl.num_programs(0)
    npos = stage.shape[0]
    half = npos // 2
    unit_rows = normed.shape[1] // npos
    wi = jnp.concatenate([r[...] for r in w_in], axis=1)
    wout = jnp.concatenate([r[...] for r in w_out], axis=0)
    x, c = normed[...], cot[...]
    pg = dot(c, wout, NT) * dg[...].astype(F32)
    gb = jnp.sum(pg, axis=0, keepdims=True)
    pg = pg.astype(BF)
    part = dot(pg, wi, NT)
    gi = dot(x, pg, TN).astype(BF)
    first = (j + steps // 2) % steps * SPLIT
    for s in range(SPLIT):
        place = tab[64 + first + s]
        gb_out[:, pl.ds(pl.multiple_of(place * UNIT, UNIT), UNIT)] = gb[:, s * UNIT : (s + 1) * UNIT]
        row = pl.multiple_of(place // SPLIT * unit_rows, unit_rows)
        lane = pl.multiple_of(place % SPLIT * UNIT, UNIT)
        for i in range(npos):
            stage[tab[16 + i], pl.ds(row, unit_rows), pl.ds(lane, UNIT)] = (
                gi[i * unit_rows : (i + 1) * unit_rows, s * UNIT : (s + 1) * UNIT])

    @pl.when(j == 0)
    def _():
        ng_out[...] = part

    @pl.when(j > 0)
    def _():
        ng_out[...] += part

    @pl.when(j == steps - 1)
    def _():
        one = pltpu.make_async_copy(stage.at[pl.ds(half, half)], send, sems.at[0])
        two = pltpu.make_async_copy(stage.at[pl.ds(0, half)], keep, sems.at[1])
        one.start()
        two.start()
        one.wait()
        two.wait()


def store_small(stage, at, tab, total, unit, cot, hid_bias):
    npos = stage.shape[0]
    width = total.shape[1]
    gain = jnp.sum(total * unit.astype(F32), axis=0, keepdims=True)
    bias = jnp.sum(total, axis=0, keepdims=True)
    out_bias = jnp.sum(cot.astype(F32), axis=0, keepdims=True)
    fill = jnp.zeros((14, 2 * UNIT), F32)
    for i in range(npos):
        tile = slice(i * width // npos // UNIT * UNIT, i * width // npos // UNIT * UNIT + UNIT)
        first = jnp.concatenate([gain[:, tile], bias[:, tile]], axis=1)
        second = jnp.concatenate([out_bias[:, tile], hid_bias[:, i * UNIT : (i + 1) * UNIT]], axis=1)
        stage[tab[16 + i], at : at + 16, :] = jnp.concatenate([first, second, fill], axis=0).astype(BF)


def attn_back_kernel(g, last, tab, off, leng, cot, att, q_in, k_in, v_in, wo, cos_ref, low_ref, high_ref,
                     p_hbm, x_hbm, w_hbm, ng_hbm, *refs):
    if last:
        (unit_hbm, hid_bias), refs = refs[:2], refs[2:]
        unit_in, refs = refs[-1], refs[:-1]
    ng_out = refs[:-10]
    keep, send, stage, dk_acc, dv_acc, p_in, x_in, w_in, ng_in, sems = refs[-10:]
    rows = cot.shape[0]
    width = cot.shape[1]
    nq = rows // QB
    npos = stage.shape[0]
    half = npos // 2
    unit_rows = width // npos
    pairs = GROUP // PAIR
    loads = []
    for pr in range(pairs):
        loads.append(pltpu.make_async_copy(
            p_hbm.at[pl.ds(g * 2 * pairs + 2 * pr, 2)], p_in.at[pl.ds(2 * pr, 2)], sems.at[pr]))
    loads.append(pltpu.make_async_copy(x_hbm, x_in, sems.at[pairs]))
    for n in range(3):
        col = pl.multiple_of(n * width + tab[48] * (width // 2) + g * GROUP, GROUP)
        loads.append(pltpu.make_async_copy(w_hbm.at[:, pl.ds(col, GROUP)], w_in.at[n], sems.at[pairs + 1 + n]))
    loads.append(pltpu.make_async_copy(ng_hbm, ng_in, sems.at[pairs + 4]))
    if last:
        loads.append(pltpu.make_async_copy(unit_hbm, unit_in, sems.at[pairs + 5]))
    for one in loads:
        one.start()
    start = off[0]
    stop = start + leng[0]
    place = lax.broadcasted_iota(jnp.int32, (rows, GROUP), 0)
    live = (place >= start) & (place < stop)
    do = jnp.where(live, dot(cot[...], wo[...], NT), 0.0)
    cosine, low, high = cos_ref[...], low_ref[...], high_ref[...]
    dqs, dks, dvs = [], [], []
    zero = jnp.zeros((), BF)
    for pr in range(pairs):
        loads[pr].wait()
        cols = slice(pr * PAIR, (pr + 1) * PAIR)
        q, k, v = q_in[:, cols], k_in[:, cols], v_in[:, cols]
        dob = do[:, cols].astype(BF)
        prod = dob.astype(F32) * att[:, g * GROUP + pr * PAIR : g * GROUP + (pr + 1) * PAIR].astype(F32)
        qh, kh, doh, delta = [], [], [], []
        for h in range(2):
            mine = head_lanes((rows, PAIR), h)
            qh.append(jnp.where(mine, q, zero))
            kh.append(jnp.where(mine, k, zero))
            doh.append(jnp.where(mine, dob, zero))
            delta.append(jnp.sum(jnp.where(mine, prod, 0.0), axis=-1, keepdims=True))
        dq_parts = [None] * nq
        for i in reversed(range(nq)):
            base = i * (i + 1) // 2 * QB
            ext = (i + 1) * QB
            blk = slice(i * QB, ext)
            dq_i, dk_i, dv_i = None, None, None
            for h in range(2):
                p = jnp.concatenate(
                    [p_in[2 * pr + h, base + kb * QB : base + (kb + 1) * QB, :] for kb in range(i + 1)], axis=1)
                dp = dot(doh[h][blk], v[:ext], NT)
                ds = (p.astype(F32) * (dp - delta[h][blk])).astype(BF)
                dv_h = dot(doh[h][blk], p, TN)
                dk_h = dot(qh[h][blk], ds, TN)
                dq_h = dot(ds, kh[h][:ext])
                dv_i = dv_h if dv_i is None else dv_i + dv_h
                dk_i = dk_h if dk_i is None else dk_i + dk_h
                dq_i = dq_h if dq_i is None else dq_i + dq_h
            dq_parts[i] = dq_i
            if i == nq - 1:
                dk_acc[...] = dk_i
                dv_acc[...] = dv_i
            else:
                dk_acc[:, :ext] += dk_i
                dv_acc[:, :ext] += dv_i
        dq = jnp.concatenate(dq_parts, axis=0) * 0.125
        dqs.append(turn_back(dq, cosine, low, high).astype(BF))
        dks.append(turn_back(dk_acc[...].T, cosine, low, high).astype(BF))
        dvs.append(dv_acc[...].T.astype(BF))
    grads = [jnp.concatenate(t, axis=1) for t in (dqs, dks, dvs)]
    for one in loads[pairs:]:
        one.wait()
    total = ng_in[...]
    for n in range(3):
        total = total + dot(grads[n], w_in[n], NT)
    at = 0
    for to in ng_out:
        to[...] = total[at : at + to.shape[0]].astype(to.dtype)
        at += to.shape[0]
    if last:
        store_small(stage, 3 * unit_rows, tab, total, unit_in[...], cot[...], hid_bias[...])
    x = x_in[...]
    for n, d in enumerate(grads):
        grad = dot(x, d, TN).astype(BF)
        for i in range(npos):
            stage[tab[16 + i], n * unit_rows : (n + 1) * unit_rows, :] = grad[i * unit_rows : (i + 1) * unit_rows]
    if not last:
        gao = dot(att[...], cot[...], TN).astype(BF)
        gao_rows = gao.shape[0] // npos
        for i in range(npos):
            for n in range(width // GROUP):
                at = 3 * unit_rows + n * gao_rows
                stage[tab[32 + i], at : at + gao_rows, :] = (
                    gao[i * gao_rows : (i + 1) * gao_rows, n * GROUP : (n + 1) * GROUP])
    one = pltpu.make_async_copy(stage.at[pl.ds(half, half)], send, sems.at[0])
    two = pltpu.make_async_copy(stage.at[pl.ds(0, half)], keep, sems.at[1])
    one.start()
    two.start()
    one.wait()
    two.wait()


def act_kernel(cut, tok, bias, own_low, own_high, recv_low, recv_high, out):
    base = tok[...].astype(F32) + bias[...]

    @pl.when(pl.program_id(0) < cut)
    def _():
        out[...] = (base + (own_low[...].astype(F32) + recv_low[...].astype(F32))).astype(BF)

    @pl.when(pl.program_id(0) >= cut)
    def _():
        out[...] = (base + (own_high[...].astype(F32) + recv_high[...].astype(F32))).astype(BF)


def finish_kernel(unit_ref, inv, cot, ng_a, ng_b, gain, *refs):
    out = refs[-1]
    unit = unit_ref[...].astype(F32)
    scaled = (ng_a[...].astype(F32) + ng_b[...].astype(F32)) * gain[...]
    mean = jnp.mean(scaled, axis=-1, keepdims=True)
    lean = jnp.mean(scaled * unit, axis=-1, keepdims=True)
    out[...] = (cot[...].astype(F32) + inv[:, :1] * (scaled - mean - unit * lean)).astype(BF)


def const_spec(shape):
    zeros = (0,) * len(shape)
    return pl.BlockSpec(shape, lambda g, *tabs: zeros, pipeline_mode=pl.Buffered(1))


def in_hbm(value):
    return pltpu.with_memory_space_constraint(value, pltpu.HBM)


def params(limit=LIMIT):
    return pltpu.CompilerParams(vmem_limit_bytes=limit)


def rotary_tables(rows):
    lane = np.arange(PAIR) % HEAD
    half = ROT // 2
    angle = np.arange(rows)[:, None] * np.power(10000.0, (lane % half) * (-2.0 / ROT))[None, :]
    inside = (lane < ROT)[None, :]
    cosine = np.where(inside, np.cos(angle), 1.0)
    low = np.where((lane < half)[None, :], -np.sin(angle), 0.0)
    high = np.where(inside & (lane >= half)[None, :], np.sin(angle), 0.0)
    return [jnp.asarray(t, F32) for t in (cosine, low, high)]


def mlp_specs(width, npos):
    steps = npos // SPLIT
    turn_of = lambda j: (j + steps // 2) % steps
    w_in = [pl.BlockSpec((width, UNIT), lambda j, t, s=s: (0, t[turn_of(j) * SPLIT + s])) for s in range(SPLIT)]
    b_in = [pl.BlockSpec((1, UNIT), lambda j, t, s=s: (0, t[turn_of(j) * SPLIT + s])) for s in range(SPLIT)]
    w_out = [pl.BlockSpec((UNIT, width), lambda j, t, s=s: (t[turn_of(j) * SPLIT + s], 0)) for s in range(SPLIT)]
    return w_in, b_in, w_out, lambda rows: pl.BlockSpec((rows, SPLIT * UNIT), lambda j, t: (0, turn_of(j)))


def mlp_forward(tab, tokens, gain, bias, cot, w_in, b_in, w_out, npos):
    rows, width = tokens.shape
    wi, bi, wo, wide = mlp_specs(width, npos)
    steps = npos // SPLIT
    full = jax.ShapeDtypeStruct((rows, width), BF)
    part = jax.ShapeDtypeStruct((npos // 2, 2 * UNIT, 512), BF)
    block = (SPLIT, 2 * UNIT, 512)
    return pl.pallas_call(
        mlp_fwd_kernel,
        grid_spec=pltpu.PrefetchScalarGridSpec(
            num_scalar_prefetch=1,
            grid=(steps,),
            in_specs=[const_spec((rows, width)), const_spec((1, width)), const_spec((1, width)),
                      const_spec((rows, width))] + wi + bi + wo,
            out_specs=[const_spec((rows, width)), const_spec((rows, width)), const_spec((rows, PAIR)), wide(rows),
                       const_spec((rows, width)),
                       pl.BlockSpec(block, lambda j, t: (jnp.maximum(j - steps // 2, 0), 0, 0)),
                       pl.BlockSpec(block, lambda j, t: (jnp.minimum(j, steps // 2 - 1), 0, 0))],
            scratch_shapes=[pltpu.VMEM((rows, width), F32)],
        ),
        out_shape=[full, full, jax.ShapeDtypeStruct((rows, PAIR), F32),
                   jax.ShapeDtypeStruct((rows, npos * UNIT), BF), full, part, part],
        compiler_params=params(MAIN),
        cost_estimate=pl.CostEstimate(flops=20 * 10**9, bytes_accessed=10**7, transcendentals=0),
        name="mlp_forward",
    )(tab, tokens, gain, bias, cot, *([w_in] * SPLIT), *([b_in] * SPLIT), *([w_out] * SPLIT))


def attn_forward(b_tab, off, leng, normed, mlp_out, w_qkv, w_ao, tables):
    rows, width = normed.shape
    groups = width // 2 // GROUP
    wspec = lambda n: pl.BlockSpec((width, GROUP), lambda g, t, o, l: (0, n * 2 * groups + t[48] * groups + g))
    ospec = pl.BlockSpec((rows, GROUP), lambda g, *t: (0, g))
    tri = (rows // QB) * (rows // QB + 1) // 2 * QB
    half = jax.ShapeDtypeStruct((rows, width // 2), BF)
    return pl.pallas_call(
        attn_fwd_kernel,
        grid_spec=pltpu.PrefetchScalarGridSpec(
            num_scalar_prefetch=3,
            grid=(groups,),
            in_specs=[const_spec((rows, width)), wspec(0), wspec(1), wspec(2),
                      pl.BlockSpec((GROUP, width), lambda g, t, o, l: (t[48] * groups + g, 0)),
                      const_spec((rows, width))] + [const_spec((rows, PAIR))] * 3,
            out_specs=[ospec, ospec, ospec,
                       pl.BlockSpec((GROUP // HEAD, tri, QB), lambda g, *t: (g, 0, 0)), ospec,
                       const_spec((rows * ACT_LOW // 16, width)), const_spec((rows - rows * ACT_LOW // 16, width))],
            scratch_shapes=[pltpu.VMEM((rows, width), F32)],
        ),
        out_shape=[half, half, half,
                   jax.ShapeDtypeStruct((HEADS // 2, tri, QB), BF), half]
        + [jax.ShapeDtypeStruct((n, width), BF) for n in (rows * ACT_LOW // 16, rows - rows * ACT_LOW // 16)],
        compiler_params=params(MAIN),
        cost_estimate=pl.CostEstimate(flops=20 * 10**9, bytes_accessed=10**7, transcendentals=0),
        name="attention_forward",
    )(b_tab, off, leng, normed, w_qkv, w_qkv, w_qkv, w_ao, mlp_out, *tables)


def mlp_backward(tab, normed, cot, dg, w_in, w_out, npos):
    rows, width = normed.shape
    wi, _, wo, wide = mlp_specs(width, npos)
    unit_rows = width // npos
    ublock = npos // SPLIT * unit_rows
    part = jax.ShapeDtypeStruct((npos // 2, ublock, 512), BF)
    anyspec = pl.BlockSpec(memory_space=pl.ANY)
    return pl.pallas_call(
        mlp_back_kernel,
        grid_spec=pltpu.PrefetchScalarGridSpec(
            num_scalar_prefetch=1,
            grid=(npos // SPLIT,),
            in_specs=[const_spec((rows, width)), const_spec((rows, width)),
                      wide(rows)] + wi + wo,
            out_specs=[const_spec((1, npos * UNIT)), const_spec((rows, width)), anyspec, anyspec],
            scratch_shapes=[pltpu.VMEM((npos, ublock, 512), BF), pltpu.SemaphoreType.DMA((2,))],
        ),
        out_shape=[jax.ShapeDtypeStruct((1, npos * UNIT), F32), jax.ShapeDtypeStruct((rows, width), F32), part, part],
        compiler_params=params(MAIN),
        cost_estimate=pl.CostEstimate(flops=20 * 10**9, bytes_accessed=10**7, transcendentals=0),
        name="mlp_backward",
    )(tab, normed, cot, dg, *([w_in] * SPLIT), *([w_out] * SPLIT))


def attn_backward(g, last, tab, off, leng, normed, cot, att, q, k, v, p, w_qkv, w_ao, ng, tables, npos, *extra):
    rows, width = normed.shape
    groups = width // 2 // GROUP
    ospec = pl.BlockSpec((rows, GROUP), lambda i, *t: (0, g))
    tri = p.shape[1]
    ublock = 3 * (width // npos) + (16 if last else width // GROUP * (width // 2 // npos))
    anyspec = pl.BlockSpec(memory_space=pl.ANY)
    part = jax.ShapeDtypeStruct((npos // 2, ublock, GROUP), BF)
    cuts = NG_CUTS if last else (0, 16)
    sizes = [(hi - lo) * rows // 16 for lo, hi in zip(cuts, cuts[1:])]
    return pl.pallas_call(
        functools.partial(attn_back_kernel, g, last),
        grid_spec=pltpu.PrefetchScalarGridSpec(
            num_scalar_prefetch=3,
            grid=(1,),
            in_specs=[const_spec((rows, width)), const_spec((rows, width // 2))] + [ospec] * 3
            + [pl.BlockSpec((GROUP, width), lambda i, t, o, l: (t[48] * groups + g, 0))]
            + [const_spec((rows, PAIR))] * 3 + [anyspec] * 4
            + ([anyspec, const_spec((1, npos * UNIT))] if last else []),
            out_specs=[const_spec((n, width)) for n in sizes] + [anyspec, anyspec],
            scratch_shapes=[pltpu.VMEM((npos, ublock, GROUP), BF),
                            pltpu.VMEM((PAIR, rows), F32), pltpu.VMEM((PAIR, rows), F32),
                            pltpu.VMEM((GROUP // HEAD, tri, QB), BF), pltpu.VMEM((rows, width), BF),
                            pltpu.VMEM((3, width, GROUP), BF), pltpu.VMEM((rows, width), F32),
                            pltpu.SemaphoreType.DMA((8,))] + ([pltpu.VMEM((rows, width), BF)] if last else []),
        ),
        out_shape=[jax.ShapeDtypeStruct((n, width), BF if last else F32) for n in sizes] + [part, part],
        compiler_params=params(MAIN),
        cost_estimate=pl.CostEstimate(flops=20 * 10**9, bytes_accessed=10**7, transcendentals=0),
        name="attention_backward",
    )(tab, off, leng, cot, att, *[in_hbm(t) for t in (q, k, v)], w_ao, *tables, p, normed, w_qkv, ng, *extra)


def act_sum(tokens, bias, own, recv):
    rows, width = tokens.shape
    step = rows // 4
    cut = own[0].shape[0] // step
    row = pl.BlockSpec((step, width), lambda r: (r, 0))
    low = pl.BlockSpec((step, width), lambda r: (jnp.minimum(r, cut - 1), 0))
    high = pl.BlockSpec((step, width), lambda r: (jnp.maximum(r - cut, 0), 0))
    return pl.pallas_call(
        functools.partial(act_kernel, cut),
        grid=(4,),
        in_specs=[row, pl.BlockSpec((1, width), lambda r: (0, 0)), low, high, low, high],
        out_specs=row,
        out_shape=jax.ShapeDtypeStruct((rows, width), BF),
        compiler_params=params(),
        cost_estimate=pl.CostEstimate(flops=10**6, bytes_accessed=10**6, transcendentals=0),
        name="activations",
    )(tokens, bias, *own, *recv)


def finish(n, unit, inv, cot, ng_a, ng_b, gain, done):
    rows, width = unit.shape
    step = rows // 8
    at, end = NG_CUTS[n] // 2, NG_CUTS[n + 1] // 2
    row = pl.BlockSpec((step, width), lambda r: (at + r, 0))
    part = pl.BlockSpec((step, width), lambda r: (r, 0))
    return pl.pallas_call(
        finish_kernel,
        grid=(end - at,),
        in_specs=[row, pl.BlockSpec((step, PAIR), lambda r: (at + r, 0)), row, part, part,
                  pl.BlockSpec((1, width), lambda r: (0, 0))]
        + [pl.BlockSpec(memory_space=pl.ANY)] * len(done),
        out_specs=row,
        out_shape=jax.ShapeDtypeStruct((rows, width), BF),
        input_output_aliases={6: 0} if done else {},
        compiler_params=params(),
        cost_estimate=pl.CostEstimate(flops=10**7, bytes_accessed=10**6, transcendentals=0),
        name="norm_backward",
    )(*[in_hbm(t) for t in (unit, inv, cot, ng_a, ng_b)], gain, *done)


def bit_reverse(value, bits):
    out = 0
    for n in range(bits):
        out |= (value >> n & 1) << (bits - 1 - n)
    return out


NPOS = 16
CHUNKS = 4
ACT_LOW = 8
NG_CUTS = (0, 6, 10, 14, 16)


def place_tables(ndp):
    bits = NPOS.bit_length() - 1
    table = np.zeros((ndp, 2, 80), np.int32)
    for d in range(ndp):
        for b in range(2):
            for n in range(NPOS):
                if ndp == NPOS:
                    table[d, b, n] = 2 * (bit_reverse(n, bits) ^ d) + b
                    table[d, b, 64 + n] = bit_reverse(n, bits) ^ d
                    table[d, b, 16 + n] = bit_reverse(n ^ d, bits)
                    rel = 0
                    for k in range(bits - 1):
                        rel |= ((n >> (k + 1) & 1) ^ (d >> k & 1)) << (bits - 1 - k)
                    rel |= (n & 1) ^ (d >> (bits - 1) & 1)
                    table[d, b, 32 + n] = rel
                else:
                    table[d, b, n] = b * NPOS + n
                    table[d, b, 64 + n] = n
                    table[d, b, 16 + n] = n
                    table[d, b, 32 + n] = n
            table[d, b, 48] = b
    return table


def after(values, *others):
    out = lax.optimization_barrier((values,) + others)
    return out[0]


def trade(send, bit, ndp):
    return lax.ppermute(send, "dp", [(d, d ^ bit) for d in range(ndp)])


def add_halves(keep, recv):
    half = keep.shape[0] // 2
    mine = (keep[:half].astype(F32) + recv[:half].astype(F32)).astype(BF)
    other = (keep[half:].astype(F32) + recv[half:].astype(F32)).astype(BF)
    return mine, other


def add_quarters(keep, recv):
    parts = [keep[n].astype(F32) + recv[n].astype(F32) for n in range(4)]
    return parts[0], [part.astype(BF) for part in parts[1:]]


def trade_quarters(parts, ndp):
    return [trade(part, bit, ndp) for part, bit in zip(parts, (8, 4, 12))]


def add_all(mine, recvs):
    for recv in recvs:
        mine = mine + recv.astype(F32)
    return mine


def place_columns_kernel(tab, own, recv, out):
    b = tab[48]
    for n in range(NPOS):
        step, s = n // SPLIT, n % SPLIT
        col = slice(s * UNIT, (s + 1) * UNIT)
        mine = (2 * n + b) * UNIT
        theirs = (2 * n + 1 - b) * UNIT
        out[:, pl.ds(pl.multiple_of(mine, UNIT), UNIT)] = own[step, :, col].astype(F32)
        out[:, pl.ds(pl.multiple_of(theirs, UNIT), UNIT)] = recv[step, :, col].astype(F32)


def shards(ndp, tokens, offsets, lengths, cotangent, ln_gain, ln_bias, w_qkv, w_attn_out, w_in, b_in, w_out, b_out):
    rows, width = tokens.shape
    dp = lax.axis_index("dp")
    b = lax.axis_index("branch")
    hidden = w_in.shape[1]
    tables = rotary_tables(rows)
    all_tab = jnp.asarray(place_tables(ndp))
    tab = lax.dynamic_slice(all_tab, (dp, b, 0), (1, 1, 80)).reshape(80)
    gain = ln_gain.reshape(1, width)
    bias = ln_bias.reshape(1, width)
    swap = [(0, 1), (1, 0)]
    halving = ndp == NPOS

    normed, unit, inv, dg, mlp_out, a_keep, a_send = mlp_forward(
        tab, tokens, gain, bias, cotangent, w_in, b_in.reshape(1, hidden), w_out, NPOS)
    barrier = lax.optimization_barrier
    a_part = (a_keep, a_send)
    if halving:
        a_recv = trade(a_send, 1, ndp)
        a_keep, a_send = add_halves(a_keep, a_recv)
        a_recv = trade(a_send, 2, ndp)
    else:
        a_recv = a_send
    q, k, v, p, att, *act_own = attn_forward(
        tab, offsets, lengths, after(normed, a_send), mlp_out, w_qkv, w_attn_out, tables)
    a_recv, att, *act_own = barrier((a_recv, att, *act_own))
    act_recv = [lax.ppermute(part, "branch", swap) for part in act_own]
    if halving:
        a_keep, a_send = add_halves(a_keep, a_recv)
        a_recv = trade(a_send, 4, ndp)
    gb_in, ng, b_keep, b_send = mlp_backward(tab, normed, cotangent, after(dg, att, a_send), w_in, w_out, NPOS)
    b_part = (b_keep, b_send)
    a_recv, b_send, ng, act_recv[0] = barrier((a_recv, b_send, ng, act_recv[0]))
    if halving:
        b_recv = trade(b_send, 1, ndp)
        a_keep, a_send = add_halves(a_keep, a_recv)
        a_recv = trade(a_send, 8, ndp)
        b_keep, b_send = add_halves(b_keep, b_recv)
        b_recv = trade(b_send, 2, ndp)
    else:
        b_recv = b_send
    ng, c_keep, c_send = attn_backward(0, False, tab, offsets, lengths, normed, cotangent, after(att, a_send, b_send),
                                       q, k, v, p, w_qkv, w_attn_out, ng, tables, NPOS)
    c_part = (c_keep, c_send)
    a_recv, c_send, ng, act_recv[1] = barrier((a_recv, c_send, ng, act_recv[1]))
    activations = act_sum(tokens, b_out.reshape(1, width), act_own, act_recv)
    activations, c_send, b_recv, ng = barrier((activations, c_send, b_recv, ng))
    c_recv = c_send
    if halving:
        c_recv = trade(c_send, 1, ndp)
        b_keep, b_send = add_halves(b_keep, b_recv)
        b_recv = trade(b_send, 4, ndp)
        c_keep, c_send = add_halves(c_keep, c_recv)
        c_recv = trade(c_send, 2, ndp)
    *ng_own, d_keep, d_send = attn_backward(
        1, True, tab, offsets, lengths, normed, cotangent, after(att, b_send, c_send),
        q, k, v, p, w_qkv, w_attn_out, ng, tables, NPOS, unit, gb_in)
    if halving:
        b_recv, c_recv, d_send = barrier((b_recv, c_recv, d_send))
    ng_recv = [lax.ppermute(part, "branch", swap) for part in ng_own]
    if not halving:
        input_grad = ()
        for n in range(CHUNKS):
            input_grad = (finish(n, unit, inv, cotangent, ng_own[n], ng_recv[n], gain, input_grad),)
        return (activations,) + input_grad + natural_sums(
            b, a_part, b_part, c_part, (d_keep, d_send), width, hidden)

    unit_rows = width // NPOS
    sub = unit_rows // 2
    steps = NPOS // SPLIT
    gao_rows = width // 2 // NPOS
    total = lambda keep, recv: keep[0].astype(F32) + recv[0].astype(F32)

    def halves(parts):
        return (lax.dynamic_slice_in_dim(parts, b * sub, sub, 1),
                lax.dynamic_slice_in_dim(parts, (1 - b) * sub, sub, 1).astype(BF))

    d_recv = trade(d_send, 1, ndp)
    c_keep, c_send = add_halves(c_keep, c_recv)
    c_recv = trade(c_send, 4, ndp)
    b_keep, b_send = add_halves(b_keep, b_recv)
    b_recv = trade(b_send, 8, ndp)
    d_recv, b_send, c_send = barrier((d_recv, b_send, c_send))
    d_keep, d_send = add_halves(d_keep, d_recv)
    d_recv = trade(d_send, 2, ndp)
    g_out = total(a_keep, a_recv).reshape(2, UNIT, 512).transpose(1, 0, 2).reshape(UNIT, width)
    d_recv, c_recv, b_recv, ng_recv[0] = barrier((d_recv, c_recv, b_recv, ng_recv[0]))
    d_keep, d_send = add_halves(d_keep, d_recv)
    d_recv = trade(d_send, 4, ndp)
    c_keep, c_send = add_halves(c_keep, after(c_recv, d_send))
    c_recv = trade(c_send, 8, ndp)
    gi_own, gi_away = halves(total(b_keep, after(b_recv, c_send)).reshape(steps, unit_rows, 512))
    gi_recv = lax.ppermute(gi_away, "branch", swap)
    grad = finish(0, unit, inv, cotangent, ng_own[0], after(ng_recv[0], gi_away), gain, ())
    d_recv, c_recv, ng_recv[1], gi_recv, grad = barrier((d_recv, c_recv, ng_recv[1], gi_recv, grad))
    d_keep, d_send = add_halves(d_keep, d_recv)
    d_recv = trade(d_send, 8, ndp)
    gc = total(c_keep, after(c_recv, d_send))
    gc_own, gc_away = halves(gc[: 3 * unit_rows].reshape(3, unit_rows, GROUP))
    gao = gc[3 * unit_rows :].reshape(width // GROUP, gao_rows, GROUP).transpose(1, 0, 2).reshape(gao_rows, width)
    top = ndp // 2
    pairs = [(d * 2 + c, (d ^ top) * 2 + 1 - c) for d in range(ndp) for c in range(2) if d // top != c]
    moved = lax.ppermute(gao.astype(BF), ("dp", "branch"), pairs)
    grad = finish(1, unit, inv, cotangent, ng_own[1], after(ng_recv[1], gc_away), gain, (grad,))
    g_in = pl.pallas_call(
        place_columns_kernel,
        grid_spec=pltpu.PrefetchScalarGridSpec(
            num_scalar_prefetch=1, grid=(1,),
            in_specs=[const_spec((steps, sub, 512))] * 2,
            out_specs=const_spec((sub, hidden)),
        ),
        out_shape=jax.ShapeDtypeStruct((sub, hidden), F32),
        compiler_params=params(),
        name="place_columns",
    )(tab, gi_own, after(gi_recv, gc_away))
    d_recv, ng_recv[2], moved, grad, g_in = barrier((d_recv, ng_recv[2], moved, grad, g_in))
    gd = total(d_keep, d_recv)
    gd_own, gd_away = halves(gd[: 3 * unit_rows].reshape(3, unit_rows, GROUP))
    small = gd[3 * unit_rows : 3 * unit_rows + 2]
    both = jnp.concatenate([gc_away, gd_away, jnp.broadcast_to(small[:1].astype(BF)[None], (3, sub, GROUP))], axis=2)
    both_recv = lax.ppermute(both, "branch", swap).astype(F32)
    g_ao = jnp.where(dp // top == b, gao, moved.astype(F32))
    grad = finish(2, unit, inv, cotangent, ng_own[2], after(ng_recv[2], both), gain, (grad,))
    input_grad = finish(3, unit, inv, cotangent, ng_own[3], ng_recv[3], gain, (grad,))
    own = jnp.concatenate([gc_own, gd_own], axis=2)
    recv = both_recv[:, :, : 2 * GROUP]
    first = jnp.where(b == 0, own, recv)
    second = jnp.where(b == 0, recv, own)
    g_qkv = jnp.concatenate(sum([[first[n], second[n]] for n in range(3)], []), axis=1)
    per = width // (2 * ndp)
    lane = dp % (UNIT // (2 * per)) * 2 * per + b * per
    row = small[0] + both_recv[0, 0, 2 * GROUP :]
    cut = lambda values, start: lax.dynamic_slice(values, (start,), (per,))
    return (activations, input_grad, cut(row, lane), cut(row, UNIT + lane), g_qkv, g_ao, g_in,
            small[1, UNIT:], g_out, cut(small[1], lane))


def natural_sums(b, a_part, b_part, c_part, d_part, width, hidden):
    axes = ("dp", "branch")
    steps = NPOS // SPLIT
    unit_rows = width // NPOS
    wa, wb, wc, wd = [jnp.concatenate(part, axis=0).astype(F32) for part in (a_part, b_part, c_part, d_part)]
    go = wa.reshape(NPOS, 2, UNIT, 512).transpose(0, 2, 1, 3).reshape(NPOS * UNIT, width)
    gi = wb.reshape(NPOS, steps, unit_rows, 512).transpose(0, 2, 1, 3)
    gi = gi.reshape(width, hidden // 2)
    gq = jnp.concatenate([w[:, : 3 * unit_rows].reshape(NPOS, 3, unit_rows, GROUP) for w in (wc, wd)], axis=3)
    gq = gq.transpose(0, 2, 1, 3).reshape(width, 3, 2 * GROUP)
    gao_rows = width // 2 // NPOS
    ga = wc[:, 3 * unit_rows :].reshape(NPOS, width // GROUP, gao_rows, GROUP).transpose(0, 2, 1, 3)
    ga = ga.reshape(NPOS * gao_rows, width)

    tiles = wd[:, 3 * unit_rows : 3 * unit_rows + 2]
    per_tile = UNIT // unit_rows

    def vector(row, lane):
        split = tiles[:, row, lane : lane + UNIT].reshape(NPOS // per_tile, per_tile, per_tile, unit_rows)
        return jnp.stack([split[:, n, n] for n in range(per_tile)], axis=1).reshape(width)

    def scatter(part, full, dim):
        starts = [0] * part.ndim
        starts[dim] = b * part.shape[dim]
        whole = lax.dynamic_update_slice(jnp.zeros(full, F32), part, starts)
        return lax.psum_scatter(whole, axes, scatter_dimension=0, tiled=True)

    total = lambda t: lax.psum_scatter(t, axes, scatter_dimension=0, tiled=True)
    g_qkv = scatter(gq, (width, 3, width), 2)
    return (
        total(vector(0, 0)),
        total(vector(0, UNIT)),
        g_qkv.reshape(g_qkv.shape[0], 3 * width),
        scatter(ga, (width, width), 0),
        scatter(gi, (width, hidden), 1),
        scatter(tiles[:, 1, UNIT:].reshape(-1), (hidden,), 0),
        scatter(go, (hidden, width), 0),
        total(jnp.where(b == 0, vector(1, 0), 0.0)),
    )


def solution(mesh):
    return jax.shard_map(
        functools.partial(shards, mesh.shape["dp"]),
        mesh=mesh,
        in_specs=(P("dp", None), P("dp"), P("dp"), P("dp", None)) + (P(),) * 8,
        out_specs=(
            P("dp", None),
            P("dp", None),
            P(("dp", "branch")),
            P(("dp", "branch")),
            P(("dp", "branch"), None),
            P(("dp", "branch"), None),
            P(("dp", "branch"), None),
            P(("dp", "branch")),
            P(("dp", "branch"), None),
            P(("dp", "branch")),
        ),
        check_vma=False,
    )
```

```python
import functools

import jax
import jax.numpy as jnp
import numpy as np
from jax import lax
from jax.experimental import pallas as pl
from jax.experimental.pallas import tpu as pltpu
from jax.sharding import PartitionSpec as P

HEADS = 16
HEAD = 64
ROT = 32
EPSILON = 1e-05
MASKED = -1e30
BF = jnp.bfloat16
F32 = jnp.float32
QB = 256
PAIR = 128
GROUP = 256
UNIT = 128
SPLIT = 4
LIMIT = 60 * 2**20
MAIN = 36 * 2**20
BACK = 48 * 2**20

NN = (((1,), (0,)), ((), ()))
NT = (((1,), (1,)), ((), ()))
TN = (((0,), (0,)), ((), ()))


def dot(left, right, dims=NN):
    return lax.dot_general(left, right, dims, preferred_element_type=F32)


def norm_stats(rows):
    x = rows.astype(F32)
    mean = jnp.mean(x, axis=-1, keepdims=True)
    centred = x - mean
    inv = lax.rsqrt(jnp.mean(centred * centred, axis=-1, keepdims=True) + EPSILON)
    return centred * inv, inv


def gelu_both(u):
    c = 0.7978845608028654
    u2 = u * u
    t = jnp.tanh(u * (c + (c * 0.044715) * u2))
    half = 0.5 + 0.5 * t
    slope = u * (c + (3 * c * 0.044715) * u2)
    return u * half, half + 0.5 * slope * (1.0 - t * t)


def lanes(shape):
    return lax.broadcasted_iota(jnp.int32, shape, 1)


def head_lanes(shape, h):
    lane = lanes(shape)
    return (lane < HEAD) if h == 0 else (lane >= HEAD)


def turn(part, cosine, low, high):
    return part * cosine + pltpu.roll(part, PAIR - ROT // 2, 1) * low + pltpu.roll(part, ROT // 2, 1) * high


def turn_back(grad, cosine, low, high):
    return grad * cosine + pltpu.roll(grad * low, ROT // 2, 1) + pltpu.roll(grad * high, PAIR - ROT // 2, 1)


def mlp_fwd_kernel(tab, *refs):
    tok, gain, bias, cot = refs[:4]
    w_in = refs[4 : 4 + SPLIT]
    b_in = refs[4 + SPLIT : 4 + 2 * SPLIT]
    w_out = refs[4 + 2 * SPLIT : 4 + 3 * SPLIT]
    normed, unit_out, inv_out, dg_out, out_ref, keep, send, acc = refs[4 + 3 * SPLIT :]
    j = pl.program_id(0)
    last = pl.num_programs(0) - 1

    @pl.when(j == 0)
    def _():
        for r in range(0, tok.shape[0], QB):
            unit, inv = norm_stats(tok[r : r + QB])
            unit_out[r : r + QB] = unit.astype(BF)
            inv_out[r : r + QB] = jnp.broadcast_to(inv, (QB, PAIR))
            normed[r : r + QB] = (unit * gain[...] + bias[...]).astype(BF)

    wi = jnp.concatenate([r[...] for r in w_in], axis=1)
    bi = jnp.concatenate([r[...] for r in b_in], axis=1)
    wout = jnp.concatenate([r[...] for r in w_out], axis=0)
    hid, dg = gelu_both(dot(normed[...], wi) + bi)
    hid = hid.astype(BF)
    dg_out[...] = dg.astype(BF)
    out = dot(hid, wout)

    @pl.when(j == 0)
    def _():
        acc[...] = out

    @pl.when((j > 0) & (j < last))
    def _():
        acc[...] += out

    @pl.when(j == last)
    def _():
        out_ref[...] = (acc[...] + out).astype(BF)
    go = dot(hid, cot[...], TN).astype(BF)

    def store(to):
        for s in range(SPLIT):
            for n in range(2):
                to[s, n * UNIT : (n + 1) * UNIT, :] = go[s * UNIT : (s + 1) * UNIT, n * 512 : (n + 1) * 512]

    @pl.when(j <= last // 2)
    def _():
        store(send)

    @pl.when(j > last // 2)
    def _():
        store(keep)


def attn_fwd_kernel(b_tab, off, leng, x_ref, wq, wk, wv, wo, mlp, cos_ref, low_ref, high_ref,
                    q_out, k_out, v_out, p_out, att_out, act_low, act_high, acc):
    rows = x_ref.shape[0]
    nq = rows // QB
    x = x_ref[...]
    start = off[0]
    stop = start + leng[0]
    place = lax.broadcasted_iota(jnp.int32, (rows, PAIR), 0)
    live = (place >= start) & (place < stop)
    kbias = jnp.where(live, 0.0, MASKED)
    live_f = jnp.where(live, 1.0, 0.0)
    lane = lanes((rows, PAIR))
    diag = lax.broadcasted_iota(jnp.int32, (QB, QB), 0) >= lax.broadcasted_iota(jnp.int32, (QB, QB), 1)
    qa = dot(x, wq[...])
    ka = dot(x, wk[...])
    va = dot(x, wv[...])
    cosine, low, high = cos_ref[...], low_ref[...], high_ref[...]
    for pr in range(GROUP // PAIR):
        cols = slice(pr * PAIR, (pr + 1) * PAIR)
        q = turn(qa[:, cols], cosine, low, high).astype(BF).astype(F32) * 0.125
        k = turn(ka[:, cols], cosine, low, high)
        v = va[:, cols]
        q_out[:, cols] = q.astype(BF)
        k_out[:, cols] = k.astype(BF)
        v_out[:, cols] = v.astype(BF)
        qh, kh, vh = [], [], []
        for h in range(2):
            mine = head_lanes((rows, PAIR), h)
            spare = lane == (HEAD if h == 0 else 0)
            qh.append(jnp.where(mine, q, jnp.where(spare, 1.0, 0.0)).astype(BF))
            kh.append(jnp.where(mine, k, jnp.where(spare, kbias, 0.0)).astype(BF))
            vh.append(jnp.where(mine, v, 0.0).astype(BF))
        for i in range(nq):
            base = i * (i + 1) // 2 * QB
            ext = (i + 1) * QB
            mixed = None
            for h in range(2):
                s = dot(qh[h][i * QB : ext], kh[h][:ext], NT)
                tail = jnp.where(diag, s[:, i * QB :], MASKED)
                s = tail if i == 0 else jnp.concatenate([s[:, : i * QB], tail], axis=1)
                e = jnp.exp(s - jnp.max(s, axis=-1, keepdims=True))
                p = (e * (1.0 / jnp.sum(e, axis=-1, keepdims=True))).astype(BF)
                for kb in range(i + 1):
                    p_out[2 * pr + h, base + kb * QB : base + (kb + 1) * QB, :] = p[:, kb * QB : (kb + 1) * QB]
                part = dot(p, vh[h][:ext])
                mixed = part if mixed is None else mixed + part
            att_out[i * QB : ext, cols] = (mixed * live_f[i * QB : ext]).astype(BF)
    out = dot(att_out[...], wo[...])

    @pl.when(pl.program_id(0) == 0)
    def _():
        acc[...] = mlp[...].astype(F32) + out

    cut = act_low.shape[0]

    @pl.when(pl.program_id(0) > 0)
    def _():
        act_low[...] = (acc[:cut] + out[:cut]).astype(BF)
        act_high[...] = (acc[cut:] + out[cut:]).astype(BF)


def mlp_back_kernel(tab, *refs):
    normed, cot, dg = refs[:3]
    w_in = refs[3 : 3 + SPLIT]
    w_out = refs[3 + SPLIT : 3 + 2 * SPLIT]
    gb_out, ng_out, keep, send, stage, ng_acc, sems = refs[3 + 2 * SPLIT :]
    j = pl.program_id(0)
    steps = pl.num_programs(0)
    npos = stage.shape[0]
    half = npos // 2
    unit_rows = normed.shape[1] // npos
    wi = jnp.concatenate([r[...] for r in w_in], axis=1)
    wout = jnp.concatenate([r[...] for r in w_out], axis=0)
    x, c = normed[...], cot[...]
    pg = dot(c, wout, NT) * dg[...].astype(F32)
    gb = jnp.sum(pg, axis=0, keepdims=True)
    pg = pg.astype(BF)
    part = dot(pg, wi, NT)
    gi = dot(x, pg, TN).astype(BF)
    first = (j + steps // 2) % steps * SPLIT
    for s in range(SPLIT):
        place = tab[64 + first + s]
        gb_out[:, pl.ds(pl.multiple_of(place * UNIT, UNIT), UNIT)] = gb[:, s * UNIT : (s + 1) * UNIT]
        row = pl.multiple_of(place // SPLIT * unit_rows, unit_rows)
        lane = pl.multiple_of(place % SPLIT * UNIT, UNIT)
        for i in range(npos):
            stage[tab[16 + i], pl.ds(row, unit_rows), pl.ds(lane, UNIT)] = (
                gi[i * unit_rows : (i + 1) * unit_rows, s * UNIT : (s + 1) * UNIT])

    @pl.when(j == 0)
    def _():
        ng_acc[...] = part

    @pl.when((j > 0) & (j < steps - 1))
    def _():
        ng_acc[...] += part

    @pl.when(j == steps - 1)
    def _():
        ng_out[...] = (ng_acc[...] + part).astype(BF)

    def copies(step):
        lane = tab[64 + (step + steps // 2) % steps * SPLIT] % SPLIT * UNIT
        cols = pl.ds(pl.multiple_of(lane, UNIT), UNIT)
        return [pltpu.make_async_copy(stage.at[pl.ds(half, half), :, cols], send.at[:, :, cols], sems.at[2 * step]),
                pltpu.make_async_copy(stage.at[pl.ds(0, half), :, cols], keep.at[:, :, cols], sems.at[2 * step + 1])]

    for one in copies(j):
        one.start()

    @pl.when(j == steps - 1)
    def _():
        for step in range(npos // SPLIT):
            for one in copies(step):
                one.wait()


def store_small(stage, at, tab, sums, hid_bias):
    npos = stage.shape[0]
    width = sums.shape[1]
    fill = jnp.zeros((14, 2 * UNIT), F32)
    for i in range(npos):
        tile = slice(i * width // npos // UNIT * UNIT, i * width // npos // UNIT * UNIT + UNIT)
        first = jnp.concatenate([sums[0:1, tile], sums[1:2, tile]], axis=1)
        second = jnp.concatenate([sums[2:3, tile], hid_bias[:, i * UNIT : (i + 1) * UNIT]], axis=1)
        stage[tab[16 + i], at : at + 16, :] = jnp.concatenate([first, second, fill], axis=0).astype(BF)


def gain_sums(total, unit):
    return [jnp.sum(total * unit.astype(F32), axis=0, keepdims=True), jnp.sum(total, axis=0, keepdims=True)]


def pair_back(pr, blocks, do, att, q_in, k_in, v_in, p_in, dk_acc, dv_acc, first, base_col=0):
    cols = slice(base_col + pr * PAIR, base_col + (pr + 1) * PAIR)
    top = (blocks[0] + 1) * QB
    start = blocks[-1] * QB
    q, k, v = q_in[:, cols], k_in[:, cols], v_in[:, cols]
    dob = do[:, cols].astype(BF)
    prod = dob.astype(F32) * att[:, cols].astype(F32)
    zero = jnp.zeros((), BF)
    skip = blocks[-1] * (blocks[-1] + 1) // 2 * QB
    qh, kh, doh, delta = [], [], [], []
    for h in range(2):
        mine = head_lanes((top - start, PAIR), h)
        qh.append(jnp.where(mine, q, zero))
        kh.append(jnp.where(head_lanes((top, PAIR), h), k, zero))
        doh.append(jnp.where(mine, dob, zero))
        delta.append(jnp.sum(jnp.where(mine, prod, 0.0), axis=-1, keepdims=True))
    parts = []
    for i in blocks:
        base = i * (i + 1) // 2 * QB - skip
        ext = (i + 1) * QB
        blk = slice(i * QB - start, ext - start)
        sums = [None, None, None]
        for h in range(2):
            p = jnp.concatenate(
                [p_in[2 * pr + h, base + kb * QB : base + (kb + 1) * QB, :] for kb in range(i + 1)], axis=1)
            dp = dot(doh[h][blk], v[:ext], NT)
            ds = (p.astype(F32) * (dp - delta[h][blk])).astype(BF)
            new = [dot(ds, kh[h][:ext]), dot(qh[h][blk], ds, TN), dot(doh[h][blk], p, TN)]
            sums = [n if old is None else old + n for old, n in zip(sums, new)]
        parts.append(sums[0])
        if first and i == blocks[0]:
            dk_acc[pr], dv_acc[pr] = sums[1], sums[2]
        else:
            dk_acc[pr, :, :ext] += sums[1]
            dv_acc[pr, :, :ext] += sums[2]
    return jnp.concatenate(parts[::-1], axis=0) * 0.125


def out_grads(rows, base, off, leng, cot, wo):
    place = base + lax.broadcasted_iota(jnp.int32, (rows, wo.shape[0]), 0)
    live = (place >= off[0]) & (place < off[0] + leng[0])
    return jnp.where(live, dot(cot, wo[...], NT), 0.0)


def start_all(copies):
    for one in copies:
        one.start()
    return copies


def wait_all(copies):
    for one in copies:
        one.wait()


def weight_columns(tab, w_hbm, w_in, sem):
    width = w_hbm.shape[0]
    col = lambda n: pl.multiple_of(n * width + tab[48] * (width // 2), width // 2)
    return pltpu.make_async_copy(w_hbm.at[:, pl.ds(col(0), width // 2)], w_in.at[0], sem.at[0]), \
        pltpu.make_async_copy(w_hbm.at[:, pl.ds(col(1), width // 2)], w_in.at[1], sem.at[1]), \
        pltpu.make_async_copy(w_hbm.at[:, pl.ds(col(2), width // 2)], w_in.at[2], sem.at[2])


def store_block(stage, tab, at, grad, gao):
    npos = stage.shape[0]
    rows = grad[0].shape[0] // npos
    for n in range(3):
        for i in range(npos):
            stage[tab[16 + i], at + n * rows : at + (n + 1) * rows, :] = grad[n][i * rows : (i + 1) * rows]
    at += 3 * rows
    rows = gao.shape[0] // npos
    for i in range(npos):
        for n in range(2):
            stage[tab[32 + i], at + n * rows : at + (n + 1) * rows, :] = (
                gao[i * rows : (i + 1) * rows, n * GROUP : (n + 1) * GROUP])


def send_out(stage, keep, send, sems):
    part = stage.shape[0] // 2
    copy = pltpu.make_async_copy
    wait_all(start_all([copy(stage.at[pl.ds(part, part)], send, sems.at[0]),
                        copy(stage.at[pl.ds(0, part)], keep, sems.at[1])]))


def attn_wide_kernel(tab, off, leng, cot, wo, cos_ref, low_ref, high_ref,
                     att_hbm, q_hbm, k_hbm, v_hbm, p_hbm, x_hbm, unit_hbm, ng_hbm, w_hbm, *refs):
    ng_out = refs[:-27]
    (first_out, dqkv_out, dka_out, dva_out, gao_out, sums, keep, send,
     att_in, q_in, k_in, v_in, p_in, p_hi, x_in, unit_in, ng_in, w_in, first, dqkv, dk_acc, dv_acc, dk_hi, dv_hi,
     gao, stage, sems) = refs[-27:]
    rows, width = cot.shape
    half = rows // 2
    nq = rows // QB
    pairs = GROUP // PAIR
    skip = nq // 2 * (nq // 2 + 1) // 2 * QB
    count = p_hi.shape[1]
    lo, hi, group = pl.ds(0, half), pl.ds(half, half), pl.ds(GROUP, GROUP)
    copy = pltpu.make_async_copy
    early = start_all([copy(q_hbm, q_in, sems.at[0]), copy(k_hbm, k_in, sems.at[1]),
                       copy(v_hbm, v_in, sems.at[2]), copy(att_hbm, att_in, sems.at[3])])
    loads = start_all([copy(p_hbm.at[pl.ds(2 * pr, 2)], p_in.at[pl.ds(2 * pr, 2)], sems.at[4 + pr])
                       for pr in range(pairs)])
    loads += start_all([copy(p_hbm.at[pl.ds(2 * (pairs + pr), 2), pl.ds(skip, count)], p_hi.at[pl.ds(2 * pr, 2)],
                             sems.at[4 + pairs + pr]) for pr in range(pairs)])
    at = 4 + 2 * pairs
    late = start_all([copy(x_hbm, x_in, sems.at[at]), *weight_columns(tab, w_hbm, w_in, sems.at[pl.ds(at + 1, 3)]),
                      copy(ng_hbm.at[hi], ng_in, sems.at[at + 4]), copy(unit_hbm.at[hi], unit_in, sems.at[at + 5])])
    cosine, low, high = cos_ref[...], low_ref[...], high_ref[...]
    do = out_grads(rows, 0, off, leng, cot[...], wo)
    blocks = list(reversed(range(nq)))
    wait_all(early)
    for pr in range(pairs):
        loads[pr].wait()
        cols = slice(pr * PAIR, (pr + 1) * PAIR)
        dq = pair_back(pr, blocks, do, att_in, q_in, k_in, v_in, p_in, dk_acc, dv_acc, True)
        first[0, :, cols] = turn_back(dq, cosine, low, high).astype(BF)
        first[1, :, cols] = turn_back(dk_acc[pr].T, cosine, low, high).astype(BF)
        first[2, :, cols] = dv_acc[pr].T.astype(BF)
    outs = start_all([copy(first, first_out, sems.at[0])])
    do = do[half:]
    blocks = list(reversed(range(nq // 2, nq)))
    cosine, low, high = cosine[half:], low[half:], high[half:]
    for pr in range(pairs):
        loads[pairs + pr].wait()
        cols = slice(GROUP + pr * PAIR, GROUP + (pr + 1) * PAIR)
        dq = pair_back(pr, blocks, do, att_in.at[hi], q_in.at[hi], k_in, v_in, p_hi, dk_hi, dv_hi, True, GROUP)
        dqkv[0, :, cols] = turn_back(dq, cosine, low, high).astype(BF)
        dqkv[1, :, cols] = turn_back(dk_hi[pr, :, half:].T, cosine, low, high).astype(BF)
        dqkv[2, :, cols] = dv_hi[pr, :, half:].T.astype(BF)
    outs += start_all([copy(dqkv.at[:, :, group], dqkv_out, sems.at[1]), copy(dk_hi.at[:, :, lo], dka_out, sems.at[2]),
                       copy(dv_hi.at[:, :, lo], dva_out, sems.at[3])])
    all_gao = dot(att_in[...], cot[...], TN).astype(BF)
    gao[...] = all_gao[:, width // 2 :]
    outs += start_all([copy(gao, gao_out, sems.at[4])])
    wait_all(late)
    x = x_in[...]
    store_block(stage, tab, 0, [dot(x, first[n], TN).astype(BF) for n in range(3)], all_gao[:, : width // 2])
    part = stage.shape[0] // 2
    outs += start_all([copy(stage.at[pl.ds(part, part)], send, sems.at[5]), copy(stage.at[pl.ds(0, part)], keep, sems.at[6])])
    total = ng_in[...].astype(F32)
    for n in range(3):
        total = total + dot(first[n, half:], w_in[n, :, :GROUP], NT) + dot(dqkv[n, :, GROUP:], w_in[n, :, GROUP:], NT)
    at = 0
    for to in ng_out:
        to[...] = total[at : at + to.shape[0]].astype(BF)
        at += to.shape[0]
    sums[...] = jnp.concatenate(
        gain_sums(total, unit_in[...]) + [jnp.sum(cot[...].astype(F32), axis=0, keepdims=True), jnp.zeros((5, width), F32)],
        axis=0)
    wait_all(outs)


def attn_low_kernel(tab, off, leng, cot, wo, cos_ref, low_ref, high_ref, hid_bias, sums_in,
                    att_hbm, q_hbm, k_hbm, v_hbm, p_hbm, unit_hbm, ng_hbm, w_hbm, x_hbm, first_hbm, dqkv_hbm, dka_hbm,
                    dva_hbm, gao_hbm, *refs):
    ng_out = refs[:-18]
    (keep, send, stage, att_in, q_in, k_in, v_in, p_in, unit_in, ng_in, w_in, x_in, dqkv, dqkv_hi, dk_acc, dv_acc, gao,
     sems) = refs[-18:]
    half, width = cot.shape
    nq = 2 * half // QB
    pairs = GROUP // PAIR
    count = p_in.shape[1]
    lo, group = pl.ds(0, half), pl.ds(GROUP, GROUP)
    copy = pltpu.make_async_copy
    early = start_all([copy(q_hbm.at[lo, group], q_in, sems.at[0]), copy(k_hbm.at[lo, group], k_in, sems.at[1]),
                       copy(v_hbm.at[lo, group], v_in, sems.at[2]), copy(att_hbm.at[lo, group], att_in, sems.at[3]),
                       copy(dka_hbm, dk_acc, sems.at[4]), copy(dva_hbm, dv_acc, sems.at[5])])
    loads = start_all([copy(p_hbm.at[pl.ds(4 + 2 * pr, 2), pl.ds(0, count)], p_in.at[pl.ds(2 * pr, 2)], sems.at[6 + pr])
                       for pr in range(pairs)])
    at = 6 + pairs
    late = start_all([copy(dqkv_hbm, dqkv_hi, sems.at[at]), copy(x_hbm, x_in, sems.at[at + 1]),
                      *weight_columns(tab, w_hbm, w_in, sems.at[pl.ds(at + 2, 3)]),
                      copy(ng_hbm.at[lo], ng_in, sems.at[at + 5]), copy(unit_hbm.at[lo], unit_in, sems.at[at + 6]),
                      copy(gao_hbm, gao, sems.at[at + 7]),
                      copy(first_hbm.at[:, lo], dqkv.at[:, :, pl.ds(0, GROUP)], sems.at[at + 8])])
    do = out_grads(half, 0, off, leng, cot[...], wo)
    cosine, low, high = cos_ref[...], low_ref[...], high_ref[...]
    blocks = list(reversed(range(nq // 2)))
    wait_all(early)
    for pr in range(pairs):
        loads[pr].wait()
        cols = slice(GROUP + pr * PAIR, GROUP + (pr + 1) * PAIR)
        dq = pair_back(pr, blocks, do, att_in, q_in, k_in, v_in, p_in, dk_acc, dv_acc, False)
        dqkv[0, :, cols] = turn_back(dq, cosine, low, high).astype(BF)
        dqkv[1, :, cols] = turn_back(dk_acc[pr].T, cosine, low, high).astype(BF)
        dqkv[2, :, cols] = dv_acc[pr].T.astype(BF)
    wait_all(late)
    x = x_in[...]
    grad = [(dot(x[:half], dqkv[n, :, GROUP:], TN) + dot(x[half:], dqkv_hi[n], TN)).astype(BF) for n in range(3)]
    store_block(stage, tab, 0, grad, gao[...])
    total = ng_in[...].astype(F32)
    for n in range(3):
        total = total + dot(dqkv[n], w_in[n], NT)
    at = 0
    for to in ng_out:
        to[...] = total[at : at + to.shape[0]].astype(BF)
        at += to.shape[0]
    sums = sums_in[...]
    new = gain_sums(total, unit_in[...])
    store_small(stage, stage.shape[1] - 16, tab,
                jnp.concatenate([sums[0:1] + new[0], sums[1:2] + new[1], sums[2:3]], axis=0), hid_bias[...])
    send_out(stage, keep, send, sems)


def act_kernel(tok, bias, own_low, own_high, recv_low, recv_high, out):
    cut = own_low.shape[0]
    for rows, own, recv in ((slice(0, cut), own_low, recv_low), (slice(cut, tok.shape[0]), own_high, recv_high)):
        base = tok[rows].astype(F32) + bias[...]
        out[rows] = (base + (own[...].astype(F32) + recv[...].astype(F32))).astype(BF)


def finish_kernel(unit_ref, inv, cot, ng_a, ng_b, gain, *refs):
    out = refs[-1]
    unit = unit_ref[...].astype(F32)
    scaled = (ng_a[...].astype(F32) + ng_b[...].astype(F32)) * gain[...]
    mean = jnp.mean(scaled, axis=-1, keepdims=True)
    lean = jnp.mean(scaled * unit, axis=-1, keepdims=True)
    out[...] = (cot[...].astype(F32) + inv[:, :1] * (scaled - mean - unit * lean)).astype(BF)


def const_spec(shape):
    zeros = (0,) * len(shape)
    return pl.BlockSpec(shape, lambda g, *tabs: zeros, pipeline_mode=pl.Buffered(1))


def in_hbm(value):
    return pltpu.with_memory_space_constraint(value, pltpu.HBM)


def params(limit=LIMIT):
    return pltpu.CompilerParams(vmem_limit_bytes=limit)


def rotary_tables(rows):
    lane = np.arange(PAIR) % HEAD
    half = ROT // 2
    angle = np.arange(rows)[:, None] * np.power(10000.0, (lane % half) * (-2.0 / ROT))[None, :]
    inside = (lane < ROT)[None, :]
    cosine = np.where(inside, np.cos(angle), 1.0)
    low = np.where((lane < half)[None, :], -np.sin(angle), 0.0)
    high = np.where(inside & (lane >= half)[None, :], np.sin(angle), 0.0)
    return [jnp.asarray(t, F32) for t in (cosine, low, high)]


def mlp_specs(width, npos):
    steps = npos // SPLIT
    turn_of = lambda j: (j + steps // 2) % steps
    w_in = [pl.BlockSpec((width, UNIT), lambda j, t, s=s: (0, t[turn_of(j) * SPLIT + s])) for s in range(SPLIT)]
    b_in = [pl.BlockSpec((1, UNIT), lambda j, t, s=s: (0, t[turn_of(j) * SPLIT + s])) for s in range(SPLIT)]
    w_out = [pl.BlockSpec((UNIT, width), lambda j, t, s=s: (t[turn_of(j) * SPLIT + s], 0)) for s in range(SPLIT)]
    return w_in, b_in, w_out, lambda rows: pl.BlockSpec((rows, SPLIT * UNIT), lambda j, t: (0, turn_of(j)))


def mlp_forward(tab, tokens, gain, bias, cot, w_in, b_in, w_out, npos):
    rows, width = tokens.shape
    wi, bi, wo, wide = mlp_specs(width, npos)
    steps = npos // SPLIT
    full = jax.ShapeDtypeStruct((rows, width), BF)
    part = jax.ShapeDtypeStruct((npos // 2, 2 * UNIT, 512), BF)
    block = (SPLIT, 2 * UNIT, 512)
    return pl.pallas_call(
        mlp_fwd_kernel,
        grid_spec=pltpu.PrefetchScalarGridSpec(
            num_scalar_prefetch=1,
            grid=(steps,),
            in_specs=[const_spec((rows, width)), const_spec((1, width)), const_spec((1, width)),
                      const_spec((rows, width))] + wi + bi + wo,
            out_specs=[const_spec((rows, width)), const_spec((rows, width)), const_spec((rows, PAIR)), wide(rows),
                       const_spec((rows, width)),
                       pl.BlockSpec(block, lambda j, t: (jnp.maximum(j - steps // 2, 0), 0, 0)),
                       pl.BlockSpec(block, lambda j, t: (jnp.minimum(j, steps // 2 - 1), 0, 0))],
            scratch_shapes=[pltpu.VMEM((rows, width), F32)],
        ),
        out_shape=[full, full, jax.ShapeDtypeStruct((rows, PAIR), F32),
                   jax.ShapeDtypeStruct((rows, npos * UNIT), BF), full, part, part],
        compiler_params=params(MAIN),
        cost_estimate=pl.CostEstimate(flops=20 * 10**9, bytes_accessed=10**7, transcendentals=0),
        name="mlp_forward",
    )(tab, *[in_hbm(t) for t in (tokens, gain, bias, cot)], *([w_in] * SPLIT), *([in_hbm(b_in)] * SPLIT),
      *([w_out] * SPLIT))


def attn_forward(b_tab, off, leng, normed, mlp_out, w_qkv, w_ao, tables):
    rows, width = normed.shape
    groups = width // 2 // GROUP
    wspec = lambda n: pl.BlockSpec((width, GROUP), lambda g, t, o, l: (0, n * 2 * groups + t[48] * groups + g))
    ospec = pl.BlockSpec((rows, GROUP), lambda g, *t: (0, g))
    tri = (rows // QB) * (rows // QB + 1) // 2 * QB
    half = pltpu.HBM((rows, width // 2), BF)
    return pl.pallas_call(
        attn_fwd_kernel,
        grid_spec=pltpu.PrefetchScalarGridSpec(
            num_scalar_prefetch=3,
            grid=(groups,),
            in_specs=[const_spec((rows, width)), wspec(0), wspec(1), wspec(2),
                      pl.BlockSpec((GROUP, width), lambda g, t, o, l: (t[48] * groups + g, 0)),
                      const_spec((rows, width))] + [const_spec((rows, PAIR))] * 3,
            out_specs=[ospec, ospec, ospec,
                       pl.BlockSpec((GROUP // HEAD, tri, QB), lambda g, *t: (g, 0, 0)), ospec,
                       const_spec((rows * ACT_LOW // 16, width)), const_spec((rows - rows * ACT_LOW // 16, width))],
            scratch_shapes=[pltpu.VMEM((rows, width), F32)],
        ),
        out_shape=[half, half, half,
                   jax.ShapeDtypeStruct((HEADS // 2, tri, QB), BF), jax.ShapeDtypeStruct((rows, width // 2), BF)]
        + [jax.ShapeDtypeStruct((n, width), BF) for n in (rows * ACT_LOW // 16, rows - rows * ACT_LOW // 16)],
        compiler_params=params(MAIN),
        cost_estimate=pl.CostEstimate(flops=20 * 10**9, bytes_accessed=10**7, transcendentals=0),
        name="attention_forward",
    )(b_tab, off, leng, normed, *[in_hbm(w_qkv)] * 3, w_ao, mlp_out, *tables)


def mlp_backward(tab, normed, cot, dg, w_in, w_out, npos):
    rows, width = normed.shape
    wi, _, wo, wide = mlp_specs(width, npos)
    unit_rows = width // npos
    ublock = npos // SPLIT * unit_rows
    part = jax.ShapeDtypeStruct((npos // 2, ublock, 512), BF)
    anyspec = pl.BlockSpec(memory_space=pl.ANY)
    return pl.pallas_call(
        mlp_back_kernel,
        grid_spec=pltpu.PrefetchScalarGridSpec(
            num_scalar_prefetch=1,
            grid=(npos // SPLIT,),
            in_specs=[const_spec((rows, width)), const_spec((rows, width)),
                      wide(rows)] + wi + wo,
            out_specs=[const_spec((1, npos * UNIT)), const_spec((rows, width)), anyspec, anyspec],
            scratch_shapes=[pltpu.VMEM((npos, ublock, 512), BF), pltpu.VMEM((rows, width), F32),
                            pltpu.SemaphoreType.DMA((2 * npos // SPLIT,))],
        ),
        out_shape=[jax.ShapeDtypeStruct((1, npos * UNIT), F32), jax.ShapeDtypeStruct((rows, width), BF), part, part],
        compiler_params=params(MAIN),
        cost_estimate=pl.CostEstimate(flops=20 * 10**9, bytes_accessed=10**7, transcendentals=0),
        name="mlp_backward",
    )(tab, normed, cot, dg, *([w_in] * SPLIT), *([w_out] * SPLIT))


def back_specs(width, half_rows, place, group, count):
    row = lambda n: pl.BlockSpec((half_rows, n), lambda i, *t: (place, 0), pipeline_mode=pl.Buffered(1))
    blocks = width // 2 // GROUP // count
    out = pl.BlockSpec((GROUP * count, width), lambda i, t, o, l: (t[48] * blocks + group, 0),
                       pipeline_mode=pl.Buffered(1))
    return [row(width), out] + [row(PAIR)] * 3


def back_call(kernel, name, cost, scratch, in_specs, out_specs, out_shape):
    return pl.pallas_call(
        kernel,
        grid_spec=pltpu.PrefetchScalarGridSpec(
            num_scalar_prefetch=3, grid=(1,), in_specs=in_specs, out_specs=out_specs, scratch_shapes=scratch),
        out_shape=out_shape,
        compiler_params=params(BACK),
        cost_estimate=pl.CostEstimate(flops=cost, bytes_accessed=10**5, transcendentals=0),
        name=name,
    )


def stage_rows(width, npos):
    return 3 * (width // npos) + 2 * (width // 2 // npos)


def attn_back_wide(tab, off, leng, cot, att, q, k, v, p, unit, w_qkv, w_ao, ng, tables, normed, npos):
    rows, width = cot.shape
    half = rows // 2
    nq = rows // QB
    count = p.shape[1] - nq // 2 * (nq // 2 + 1) // 2 * QB
    pairs = GROUP // PAIR
    anyspec = pl.BlockSpec(memory_space=pl.ANY)
    sizes = [size * UNIT for at, size in NG_PARTS if at * UNIT >= half]
    ublock = stage_rows(width, npos)
    part = jax.ShapeDtypeStruct((npos // 2, ublock, GROUP), BF)
    accs = pltpu.HBM((pairs, PAIR, half), F32)
    cols = pltpu.VMEM((rows, width // 2), BF)
    acc = pltpu.VMEM((pairs, PAIR, rows), F32)
    wide = pltpu.VMEM((half, width), BF)
    return back_call(
        attn_wide_kernel, "attention_back_wide", 20 * 10**9,
        [cols, cols, cols, cols, pltpu.VMEM((GROUP // HEAD, p.shape[1], QB), BF), pltpu.VMEM((GROUP // HEAD, count, QB), BF),
         pltpu.VMEM((rows, width), BF), wide, wide, pltpu.VMEM((3, width, width // 2), BF), pltpu.VMEM((3, rows, GROUP), BF),
         pltpu.VMEM((3, half, width // 2), BF), acc, acc, acc, acc, pltpu.VMEM((width // 2, width // 2), BF),
         pltpu.VMEM((npos, ublock, GROUP), BF), pltpu.SemaphoreType.DMA((2 * pairs + 10,))],
        back_specs(width, rows, 0, 0, 2) + [anyspec] * 9,
        [const_spec((n, width)) for n in sizes] + [anyspec] * 5 + [const_spec((8, width)), anyspec, anyspec],
        [jax.ShapeDtypeStruct((n, width), BF) for n in sizes]
        + [pltpu.HBM((3, rows, GROUP), BF), pltpu.HBM((3, half, GROUP), BF), accs, accs,
           pltpu.HBM((width // 2, width // 2), BF), jax.ShapeDtypeStruct((8, width), F32), part, part],
    )(tab, off, leng, cot, w_ao, *tables, att, q, k, v, p, normed, unit, ng, w_qkv)


def attn_back_low(tab, off, leng, cot, att, q, k, v, p, unit, w_qkv, w_ao, ng, tables, normed, hid_bias, first,
                  gao, carried, npos):
    rows, width = cot.shape
    half = rows // 2
    nq = rows // QB
    count = nq // 2 * (nq // 2 + 1) // 2 * QB
    pairs = GROUP // PAIR
    anyspec = pl.BlockSpec(memory_space=pl.ANY)
    sizes = [size * UNIT for at, size in NG_PARTS if at * UNIT < half]
    ublock = stage_rows(width, npos) + 16
    part = jax.ShapeDtypeStruct((npos // 2, ublock, GROUP), BF)
    dqkv, dk_acc, dv_acc, sums = carried
    cols = pltpu.VMEM((half, GROUP), BF)
    acc = pltpu.VMEM((pairs, PAIR, half), F32)
    wide = pltpu.VMEM((half, width), BF)
    return back_call(
        attn_low_kernel, "attention_back_low", 20 * 10**9,
        [pltpu.VMEM((npos, ublock, GROUP), BF), cols, cols, cols, cols, pltpu.VMEM((GROUP // HEAD, count, QB), BF),
         wide, wide, pltpu.VMEM((3, width, width // 2), BF), pltpu.VMEM((rows, width), BF),
         pltpu.VMEM((3, half, width // 2), BF), pltpu.VMEM((3, half, GROUP), BF), acc, acc,
         pltpu.VMEM((width // 2, width // 2), BF), pltpu.SemaphoreType.DMA((pairs + 15,))],
        back_specs(width, half, 0, 1, 1) + [const_spec((1, npos * UNIT)), const_spec((8, width))]
        + [anyspec] * 14,
        [const_spec((n, width)) for n in sizes] + [anyspec, anyspec],
        [jax.ShapeDtypeStruct((n, width), BF) for n in sizes] + [part, part],
    )(tab, off, leng, cot, w_ao, *tables, hid_bias, sums, att, q, k, v, p, unit, ng, w_qkv, normed, first, dqkv,
      dk_acc, dv_acc, gao)


def act_sum(tokens, bias, own, recv):
    return pl.pallas_call(
        act_kernel,
        grid=(1,),
        in_specs=[const_spec(t.shape) for t in (tokens, bias, *own, *recv)],
        out_specs=const_spec(tokens.shape),
        out_shape=jax.ShapeDtypeStruct(tokens.shape, BF),
        compiler_params=params(),
        cost_estimate=pl.CostEstimate(flops=10**6, bytes_accessed=10**6, transcendentals=0),
        name="activations",
    )(in_hbm(tokens), bias, *[in_hbm(t) for t in (*own, *recv)])


def finish(n, unit, inv, cot, ng_a, ng_b, gain, done):
    rows, width = unit.shape
    step = UNIT
    at, count = NG_PARTS[n]
    row = pl.BlockSpec((step, width), lambda r: (at + r, 0))
    part = pl.BlockSpec((step, width), lambda r: (r, 0))
    return pl.pallas_call(
        finish_kernel,
        grid=(count,),
        in_specs=[row, pl.BlockSpec((step, PAIR), lambda r: (at + r, 0)), row, part, part,
                  pl.BlockSpec((1, width), lambda r: (0, 0))]
        + [pl.BlockSpec(memory_space=pl.ANY)] * len(done),
        out_specs=row,
        out_shape=jax.ShapeDtypeStruct((rows, width), BF),
        input_output_aliases={6: 0} if done else {},
        compiler_params=params(),
        cost_estimate=pl.CostEstimate(flops=10**7, bytes_accessed=10**6, transcendentals=0),
        name="norm_backward",
    )(*[in_hbm(t) for t in (unit, inv, cot, ng_a, ng_b)], gain, *done)


def bit_reverse(value, bits):
    out = 0
    for n in range(bits):
        out |= (value >> n & 1) << (bits - 1 - n)
    return out


NPOS = 16
ACT_LOW = 7
NG_PARTS = ((4, 2), (6, 2), (0, 2), (2, 2))


def place_tables(ndp):
    bits = NPOS.bit_length() - 1
    table = np.zeros((ndp, 2, 80), np.int32)
    for d in range(ndp):
        for b in range(2):
            for n in range(NPOS):
                if ndp == NPOS:
                    table[d, b, n] = 2 * (bit_reverse(n, bits) ^ d) + b
                    table[d, b, 64 + n] = bit_reverse(n, bits) ^ d
                    table[d, b, 16 + n] = bit_reverse(n ^ d, bits)
                    rel = 0
                    for k in range(bits - 1):
                        rel |= ((n >> (k + 1) & 1) ^ (d >> k & 1)) << (bits - 1 - k)
                    rel |= (n & 1) ^ (d >> (bits - 1) & 1)
                    table[d, b, 32 + n] = rel
                else:
                    table[d, b, n] = b * NPOS + n
                    table[d, b, 64 + n] = n
                    table[d, b, 16 + n] = n
                    table[d, b, 32 + n] = n
            table[d, b, 48] = b
    return table


def after(values, *others):
    out = lax.optimization_barrier((values,) + others)
    return out[0]


def trade(send, bit, ndp):
    return lax.ppermute(send, "dp", [(d, d ^ bit) for d in range(ndp)])


def add_halves(keep, recv):
    half = keep.shape[0] // 2
    mine = (keep[:half].astype(F32) + recv[:half].astype(F32)).astype(BF)
    other = (keep[half:].astype(F32) + recv[half:].astype(F32)).astype(BF)
    return mine, other


def add_quarters(keep, recv):
    parts = [keep[n].astype(F32) + recv[n].astype(F32) for n in range(4)]
    return parts[0], [part.astype(BF) for part in parts[1:]]


def trade_quarters(parts, ndp):
    return [trade(part, bit, ndp) for part, bit in zip(parts, (8, 4, 12))]


def add_all(mine, recvs):
    for recv in recvs:
        mine = mine + recv.astype(F32)
    return mine


def place_columns_kernel(tab, own, recv, out):
    b = tab[48]
    for n in range(NPOS):
        step, s = n // SPLIT, n % SPLIT
        col = slice(s * UNIT, (s + 1) * UNIT)
        mine = (2 * n + b) * UNIT
        theirs = (2 * n + 1 - b) * UNIT
        out[:, pl.ds(pl.multiple_of(mine, UNIT), UNIT)] = own[step, :, col].astype(F32)
        out[:, pl.ds(pl.multiple_of(theirs, UNIT), UNIT)] = recv[step, :, col].astype(F32)


def shards(ndp, tokens, offsets, lengths, cotangent, ln_gain, ln_bias, w_qkv, w_attn_out, w_in, b_in, w_out, b_out):
    rows, width = tokens.shape
    dp = lax.axis_index("dp")
    b = lax.axis_index("branch")
    hidden = w_in.shape[1]
    tables = rotary_tables(rows)
    all_tab = jnp.asarray(place_tables(ndp))
    tab = lax.dynamic_slice(all_tab, (dp, b, 0), (1, 1, 80)).reshape(80)
    gain = ln_gain.reshape(1, width)
    bias = ln_bias.reshape(1, width)
    swap = [(0, 1), (1, 0)]
    halving = ndp == NPOS

    normed, unit, inv, dg, mlp_out, a_keep, a_send = mlp_forward(
        tab, tokens, gain, bias, cotangent, w_in, b_in.reshape(1, hidden), w_out, NPOS)
    barrier = lax.optimization_barrier
    a_part = (a_keep, a_send)
    a_recv = trade(a_send, 1, ndp) if halving else a_send
    q, k, v, p, att, *act_own = attn_forward(
        tab, offsets, lengths, after(normed, a_send), mlp_out, w_qkv, w_attn_out, tables)
    a_recv, att, *act_own = barrier((a_recv, att, *act_own))
    act_recv = [lax.ppermute(part, "branch", swap) for part in act_own]
    if halving:
        a_keep, a_send = add_halves(a_keep, a_recv)
        a_recv = trade(a_send, 2, ndp)
    gb_in, ng, b_keep, b_send = mlp_backward(tab, normed, cotangent, after(dg, att, a_send), w_in, w_out, NPOS)
    b_part = (b_keep, b_send)
    a_recv, b_send, ng, act_recv[0] = barrier((a_recv, b_send, ng, act_recv[0]))
    if halving:
        b_recv = trade(b_send, 1, ndp)
        a_keep, a_send = add_halves(a_keep, a_recv)
        a_recv = trade(a_send, 4, ndp)
        b_keep, b_send = add_halves(b_keep, b_recv)
        b_recv = trade(b_send, 2, ndp)
    else:
        b_recv = b_send
    *ng_own, first, dqkv, dk_acc, dv_acc, gao, sums, c_keep, c_send = attn_back_wide(
        tab, offsets, lengths, cotangent, after(att, a_send, b_send), q, k, v, p, unit, w_qkv, w_attn_out, ng, tables,
        normed, NPOS)
    c_part = (c_keep, c_send)
    b_recv, a_recv, act_recv[1], c_send, *ng_own = barrier((b_recv, a_recv, act_recv[1], c_send, *ng_own))
    ng_recv = [lax.ppermute(part, "branch", swap) for part in ng_own]
    c_recv = c_send
    if halving:
        c_recv = trade(c_send, 1, ndp)
        b_keep, b_send = add_halves(b_keep, b_recv)
        b_recv = trade(b_send, 4, ndp)
        a_keep, a_send = add_halves(a_keep, a_recv)
        a_recv = trade(a_send, 8, ndp)
        c_recv, b_send, a_send = barrier((c_recv, b_send, a_send))
        c_keep, c_send = add_halves(c_keep, c_recv)
        c_recv = trade(c_send, 2, ndp)
    *more, d_keep, d_send = attn_back_low(
        tab, offsets, lengths, cotangent, after(att, b_send, c_send, ng_own[0]), q, k, v, p, unit, w_qkv, w_attn_out, ng,
        tables, normed, gb_in, first, gao, (dqkv, dk_acc, dv_acc, sums), NPOS)
    ng_own = ng_own + more
    if not halving:
        ng_recv = [lax.ppermute(part, "branch", swap) for part in ng_own]
        activations = act_sum(tokens, b_out.reshape(1, width), act_own, act_recv)
        input_grad = ()
        for n in range(len(NG_PARTS)):
            input_grad = (finish(n, unit, inv, cotangent, ng_own[n], ng_recv[n], gain, input_grad),)
        return (activations,) + input_grad + natural_sums(b, a_part, b_part, c_part, (d_keep, d_send), width, hidden)

    unit_rows = width // NPOS
    sub = unit_rows // 2
    steps = NPOS // SPLIT
    gao_rows = width // 2 // NPOS
    second = 3 * unit_rows + 2 * gao_rows
    total = lambda keep, recv: keep[0].astype(F32) + recv[0].astype(F32)

    def halves(parts):
        return (lax.dynamic_slice_in_dim(parts, b * sub, sub, 1),
                lax.dynamic_slice_in_dim(parts, (1 - b) * sub, sub, 1).astype(BF))

    a_recv, b_recv, c_recv, ng_recv[0], d_send, *more = barrier((a_recv, b_recv, c_recv, ng_recv[0], d_send, *more))
    ng_recv += [lax.ppermute(part, "branch", swap) for part in more]
    d_recv = trade(d_send, 1, ndp)
    c_keep, c_send = add_halves(c_keep, c_recv)
    c_recv = trade(c_send, 4, ndp)
    b_keep, b_send = add_halves(b_keep, b_recv)
    b_recv = trade(b_send, 8, ndp)
    d_recv, c_send, b_send = barrier((d_recv, c_send, b_send))
    d_keep, d_send = add_halves(d_keep, d_recv)
    d_recv = trade(d_send, 2, ndp)
    g_out = total(a_keep, after(a_recv, d_send)).reshape(2, UNIT, 512).transpose(1, 0, 2).reshape(UNIT, width)
    act_recv[0] = after(act_recv[0], g_out)
    activations = act_sum(tokens, b_out.reshape(1, width), act_own, act_recv)
    c_recv, d_recv, b_recv, ng_recv[1], activations = barrier((c_recv, d_recv, b_recv, ng_recv[1], activations))
    d_keep, d_send = add_halves(d_keep, d_recv)
    d_recv = trade(d_send, 4, ndp)
    c_keep, c_send = add_halves(c_keep, after(c_recv, d_send))
    c_recv = trade(c_send, 8, ndp)
    gi_own, gi_away = halves(total(b_keep, after(b_recv, c_send)).reshape(steps, unit_rows, 512))
    gi_recv = lax.ppermute(gi_away, "branch", swap)
    grad = finish(0, unit, inv, cotangent, ng_own[0], after(ng_recv[0], gi_away), gain, ())
    c_recv, d_recv, ng_recv[2], gi_recv, grad = barrier((c_recv, d_recv, ng_recv[2], gi_recv, grad))
    d_keep, d_send = add_halves(d_keep, d_recv)
    d_recv = trade(d_send, 8, ndp)
    gc = total(c_keep, after(c_recv, d_send))
    grad = finish(1, unit, inv, cotangent, ng_own[1], after(ng_recv[1], d_send), gain, (grad,))
    g_in = pl.pallas_call(
        place_columns_kernel,
        grid_spec=pltpu.PrefetchScalarGridSpec(
            num_scalar_prefetch=1, grid=(1,),
            in_specs=[const_spec((steps, sub, 512))] * 2,
            out_specs=const_spec((sub, hidden)),
        ),
        out_shape=jax.ShapeDtypeStruct((sub, hidden), F32),
        compiler_params=params(),
        name="place_columns",
    )(tab, gi_own, after(gi_recv, d_send))
    d_recv, ng_recv[3], gc, grad, g_in = barrier((d_recv, ng_recv[3], gc, grad, g_in))
    gd = total(d_keep, d_recv)
    gq = jnp.concatenate([gc[: 3 * unit_rows].reshape(3, unit_rows, GROUP), gd[: 3 * unit_rows].reshape(3, unit_rows, GROUP)],
                         axis=2)
    gq_own, gq_away = halves(gq)
    gao = jnp.concatenate([g[3 * unit_rows + n * gao_rows : 3 * unit_rows + (n + 1) * gao_rows]
                           for g in (gc, gd) for n in range(2)], axis=1)
    small = gd[second : second + 2]
    both = jnp.concatenate([gq_away, jnp.broadcast_to(small[:1].astype(BF)[None], (3, sub, GROUP))], axis=2)
    both_recv = lax.ppermute(both, "branch", swap).astype(F32)
    top = ndp // 2
    pairs = [(d * 2 + c, (d ^ top) * 2 + 1 - c) for d in range(ndp) for c in range(2) if d // top != c]
    moved = lax.ppermute(gao.astype(BF), ("dp", "branch"), pairs)
    grad = finish(2, unit, inv, cotangent, ng_own[2], after(ng_recv[2], both), gain, (grad,))
    input_grad = finish(3, unit, inv, cotangent, ng_own[3], ng_recv[3], gain, (grad,))
    g_ao = jnp.where(dp // top == b, gao, moved.astype(F32))
    recv = both_recv[:, :, : 2 * GROUP]
    first = jnp.where(b == 0, gq_own, recv)
    second_half = jnp.where(b == 0, recv, gq_own)
    g_qkv = jnp.concatenate(sum([[first[n], second_half[n]] for n in range(3)], []), axis=1)
    per = width // (2 * ndp)
    lane = dp % (UNIT // (2 * per)) * 2 * per + b * per
    row = small[0] + both_recv[0, 0, 2 * GROUP :]
    cut = lambda values, start: lax.dynamic_slice(values, (start,), (per,))
    return (activations, input_grad, cut(row, lane), cut(row, UNIT + lane), g_qkv, g_ao, g_in,
            small[1, UNIT:], g_out, cut(small[1], lane))


def natural_sums(b, a_part, b_part, c_part, d_part, width, hidden):
    axes = ("dp", "branch")
    steps = NPOS // SPLIT
    unit_rows = width // NPOS
    gao_rows = width // 2 // NPOS
    second = 3 * unit_rows + 2 * gao_rows
    wa, wb, wc, wd = [jnp.concatenate(part, axis=0).astype(F32) for part in (a_part, b_part, c_part, d_part)]
    go = wa.reshape(NPOS, 2, UNIT, 512).transpose(0, 2, 1, 3).reshape(NPOS * UNIT, width)
    gi = wb.reshape(NPOS, steps, unit_rows, 512).transpose(0, 2, 1, 3)
    gi = gi.reshape(width, hidden // 2)
    gq = jnp.concatenate([w[:, : 3 * unit_rows].reshape(NPOS, 3, unit_rows, GROUP) for w in (wc, wd)], axis=3)
    gq = gq.transpose(0, 2, 1, 3).reshape(width, 3, 2 * GROUP)
    ga = jnp.concatenate([w[:, 3 * unit_rows : second].reshape(NPOS, 2, gao_rows, GROUP) for w in (wc, wd)], axis=1)
    ga = ga.transpose(0, 2, 1, 3).reshape(NPOS * gao_rows, width)
    tiles = wd[:, second : second + 2]
    per_tile = UNIT // unit_rows

    def vector(row, lane):
        split = tiles[:, row, lane : lane + UNIT].reshape(NPOS // per_tile, per_tile, per_tile, unit_rows)
        return jnp.stack([split[:, n, n] for n in range(per_tile)], axis=1).reshape(width)

    def scatter(part, full, dim):
        starts = [0] * part.ndim
        starts[dim] = b * part.shape[dim]
        whole = lax.dynamic_update_slice(jnp.zeros(full, F32), part, starts)
        return lax.psum_scatter(whole, axes, scatter_dimension=0, tiled=True)

    total = lambda t: lax.psum_scatter(t, axes, scatter_dimension=0, tiled=True)
    g_qkv = scatter(gq, (width, 3, width), 2)
    return (
        total(vector(0, 0)),
        total(vector(0, UNIT)),
        g_qkv.reshape(g_qkv.shape[0], 3 * width),
        scatter(ga, (width, width), 0),
        scatter(gi, (width, hidden), 1),
        scatter(tiles[:, 1, UNIT:].reshape(-1), (hidden,), 0),
        scatter(go, (hidden, width), 0),
        total(jnp.where(b == 0, vector(1, 0), 0.0)),
    )


def solution(mesh):
    return jax.shard_map(
        functools.partial(shards, mesh.shape["dp"]),
        mesh=mesh,
        in_specs=(P("dp", None), P("dp"), P("dp"), P("dp", None)) + (P(),) * 8,
        out_specs=(
            P("dp", None),
            P("dp", None),
            P(("dp", "branch")),
            P(("dp", "branch")),
            P(("dp", "branch"), None),
            P(("dp", "branch"), None),
            P(("dp", "branch"), None),
            P(("dp", "branch")),
            P(("dp", "branch"), None),
            P(("dp", "branch")),
        ),
        check_vma=False,
    )
```

```python
import functools

import jax
import jax.numpy as jnp
import numpy as np
from jax import lax
from jax.experimental import pallas as pl
from jax.experimental.pallas import tpu as pltpu
from jax.sharding import PartitionSpec as P

HEADS = 16
HEAD = 64
ROT = 32
EPSILON = 1e-05
MASKED = -1e30
BF = jnp.bfloat16
F32 = jnp.float32
QB = 256
PAIR = 128
GROUP = 256
UNIT = 128
SPLIT = 4
LIMIT = 60 * 2**20
MAIN = 36 * 2**20
BACK = 48 * 2**20
FORWARD = 44 * 2**20

NN = (((1,), (0,)), ((), ()))
NT = (((1,), (1,)), ((), ()))
TN = (((0,), (0,)), ((), ()))


def dot(left, right, dims=NN):
    return lax.dot_general(left, right, dims, preferred_element_type=F32)


def norm_stats(rows):
    x = rows.astype(F32)
    mean = jnp.mean(x, axis=-1, keepdims=True)
    centred = x - mean
    inv = lax.rsqrt(jnp.mean(centred * centred, axis=-1, keepdims=True) + EPSILON)
    return centred * inv, inv


def gelu_both(u):
    c = 0.7978845608028654
    u2 = u * u
    t = jnp.tanh(u * (c + (c * 0.044715) * u2))
    half = 0.5 + 0.5 * t
    slope = u * (c + (3 * c * 0.044715) * u2)
    return u * half, half + 0.5 * slope * (1.0 - t * t)


def lanes(shape):
    return lax.broadcasted_iota(jnp.int32, shape, 1)


def head_lanes(shape, h):
    lane = lanes(shape)
    return (lane < HEAD) if h == 0 else (lane >= HEAD)


def turn(part, cosine, low, high):
    return part * cosine + pltpu.roll(part, PAIR - ROT // 2, 1) * low + pltpu.roll(part, ROT // 2, 1) * high


def turn_back(grad, cosine, low, high):
    return grad * cosine + pltpu.roll(grad * low, ROT // 2, 1) + pltpu.roll(grad * high, PAIR - ROT // 2, 1)


def start_all(copies):
    for one in copies:
        one.start()
    return copies


def wait_all(copies):
    for one in copies:
        one.wait()


def mlp_fwd_kernel(tab, *refs):
    tok, gain, bias, cot = refs[:4]
    w_in = refs[4 : 4 + SPLIT]
    b_in = refs[4 + SPLIT : 4 + 2 * SPLIT]
    w_out = refs[4 + 2 * SPLIT]
    (normed_out, unit_out, inv_out, dg_out, out_ref, keep, send, hid_all, w_all, normed, unit_in, inv_in,
     sems) = refs[5 + 2 * SPLIT :]
    j = pl.program_id(0)
    last = pl.num_programs(0) - 1

    def norm_copies():
        return [pltpu.make_async_copy(src, dst, sems.at[n])
                for n, (src, dst) in enumerate(((normed, normed_out), (unit_in, unit_out), (inv_in, inv_out)))]

    def weight_copies():
        return [pltpu.make_async_copy(w_out.at[pl.ds(pl.multiple_of(tab[n] * UNIT, UNIT), UNIT)],
                                      w_all.at[pl.ds(n * UNIT, UNIT)], sems.at[3 + n]) for n in range(w_all.shape[0] // UNIT)]

    @pl.when(j == 0)
    def _():
        start_all(weight_copies())
        for r in range(0, tok.shape[0], QB):
            unit, inv = norm_stats(tok[r : r + QB])
            unit_in[r : r + QB] = unit.astype(BF)
            inv_in[r : r + QB] = jnp.broadcast_to(inv, (QB, PAIR))
            normed[r : r + QB] = (unit * gain[...] + bias[...]).astype(BF)
        start_all(norm_copies())

    wi = jnp.concatenate([r[...] for r in w_in], axis=1)
    bi = jnp.concatenate([r[...] for r in b_in], axis=1)
    hid, dg = gelu_both(dot(normed[...], wi) + bi)
    hid = hid.astype(BF)
    dg_out[...] = dg.astype(BF)
    steps = pl.num_programs(0)
    place = (j + steps // 2) % steps * (SPLIT * UNIT)
    hid_all[:, pl.ds(pl.multiple_of(place, SPLIT * UNIT), SPLIT * UNIT)] = hid
    go = dot(hid, cot[...], TN).astype(BF)

    def store(to):
        for s in range(SPLIT):
            for n in range(2):
                to[s, n * UNIT : (n + 1) * UNIT, :] = go[s * UNIT : (s + 1) * UNIT, n * 512 : (n + 1) * 512]

    @pl.when(j <= last // 2)
    def _():
        store(send)

    @pl.when(j > last // 2)
    def _():
        store(keep)

    @pl.when(j == last)
    def _():
        wait_all(weight_copies())
        out_ref[...] = dot(hid_all[...], w_all[...]).astype(BF)
        wait_all(norm_copies())


def attn_fwd_kernel(tab, off, leng, x_ref, cos_ref, low_ref, high_ref, w_hbm, wo_hbm, mlp_hbm,
                    q_out, k_out, v_out, p_out, att_out, act_low, act_high,
                    w_in, wo, mlp, q_in, k_in, v_in, p_in, att_in, sems):
    rows, width = x_ref.shape
    nq = rows // QB
    pairs = GROUP // PAIR
    groups = width // 2 // GROUP
    copy = pltpu.make_async_copy
    loads = []
    for g in range(groups):
        for n in range(3):
            col = pl.multiple_of(n * width + tab[48] * (width // 2) + g * GROUP, GROUP)
            loads.append(copy(w_hbm.at[:, pl.ds(col, GROUP)], w_in.at[g, n], sems.at[3 * g + n]))
    at = 3 * groups
    late = [copy(wo_hbm.at[pl.ds(pl.multiple_of(tab[48] * (width // 2), width // 2), width // 2)], wo, sems.at[at]),
            copy(mlp_hbm, mlp, sems.at[at + 1])]
    at += 2
    start_all(loads + late)
    x = x_ref[...]
    start = off[0]
    stop = start + leng[0]
    place = lax.broadcasted_iota(jnp.int32, (rows, PAIR), 0)
    live = (place >= start) & (place < stop)
    kbias = jnp.where(live, 0.0, MASKED)
    live_f = jnp.where(live, 1.0, 0.0)
    lane = lanes((rows, PAIR))
    diag = lax.broadcasted_iota(jnp.int32, (QB, QB), 0) >= lax.broadcasted_iota(jnp.int32, (QB, QB), 1)
    cosine, low, high = cos_ref[...], low_ref[...], high_ref[...]
    outs = []
    for g in range(groups):
        wait_all(loads[3 * g : 3 * g + 3])
        qa, ka, va = [dot(x, w_in[g, n]) for n in range(3)]
        for pr in range(pairs):
            cols = slice(pr * PAIR, (pr + 1) * PAIR)
            to = slice(g * GROUP + pr * PAIR, g * GROUP + (pr + 1) * PAIR)
            q = turn(qa[:, cols], cosine, low, high).astype(BF).astype(F32) * 0.125
            k = turn(ka[:, cols], cosine, low, high)
            v = va[:, cols]
            q_in[:, to] = q.astype(BF)
            k_in[:, to] = k.astype(BF)
            v_in[:, to] = v.astype(BF)
            qh, kh, vh = [], [], []
            for h in range(2):
                mine = head_lanes((rows, PAIR), h)
                spare = lane == (HEAD if h == 0 else 0)
                qh.append(jnp.where(mine, q, jnp.where(spare, 1.0, 0.0)).astype(BF))
                kh.append(jnp.where(mine, k, jnp.where(spare, kbias, 0.0)).astype(BF))
                vh.append(jnp.where(mine, v, 0.0).astype(BF))
            head = g * 2 * pairs + 2 * pr
            for i in range(nq):
                base = i * (i + 1) // 2 * QB
                ext = (i + 1) * QB
                mixed = None
                scores = [dot(qh[h][i * QB : ext], kh[h][:ext], NT) for h in range(2)]
                for h in range(2):
                    s = scores[h]
                    tail = jnp.where(diag, s[:, i * QB :], MASKED)
                    s = tail if i == 0 else jnp.concatenate([s[:, : i * QB], tail], axis=1)
                    e = jnp.exp(s - jnp.max(s, axis=-1, keepdims=True))
                    p = (e * (1.0 / jnp.sum(e, axis=-1, keepdims=True))).astype(BF)
                    for kb in range(i + 1):
                        p_in[head + h, base + kb * QB : base + (kb + 1) * QB, :] = p[:, kb * QB : (kb + 1) * QB]
                    part = dot(p, vh[h][:ext])
                    mixed = part if mixed is None else mixed + part
                att_in[i * QB : ext, to] = (mixed * live_f[i * QB : ext]).astype(BF)
            outs += start_all([copy(p_in.at[pl.ds(head, 2)], p_out.at[pl.ds(head, 2)], sems.at[at])])
            at += 1
        group = pl.ds(g * GROUP, GROUP)
        outs += start_all([copy(src.at[:, group], dst.at[:, group], sems.at[at + n])
                           for n, (src, dst) in enumerate(((q_in, q_out), (k_in, k_out), (v_in, v_out), (att_in, att_out)))])
        at += 4
    wait_all(late)
    out = mlp[...].astype(F32) + dot(att_in[...], wo[...])
    cut = act_low.shape[0]
    act_low[...] = out[:cut].astype(BF)
    act_high[...] = out[cut:].astype(BF)
    wait_all(outs)


def mlp_back_kernel(tab, *refs):
    normed, cot, dg = refs[:3]
    w_in = refs[3]
    w_out = refs[4 : 4 + SPLIT]
    gb_out, ng_out, keep, send, stage, pg_all, w_all, sems = refs[4 + SPLIT :]
    j = pl.program_id(0)
    steps = pl.num_programs(0)
    npos = stage.shape[0]
    half = npos // 2
    unit_rows = normed.shape[1] // npos
    wout = jnp.concatenate([r[...] for r in w_out], axis=0)
    x, c = normed[...], cot[...]
    many = 2 * npos // SPLIT

    def weight_copies():
        return [pltpu.make_async_copy(w_in.at[:, pl.ds(pl.multiple_of(tab[n] * UNIT, UNIT), UNIT)],
                                      w_all.at[:, pl.ds(n * UNIT, UNIT)], sems.at[many + n]) for n in range(npos)]

    @pl.when(j == 0)
    def _():
        start_all(weight_copies())

    pg = dot(c, wout, NT) * dg[...].astype(F32)
    gb = jnp.sum(pg, axis=0, keepdims=True)
    pg = pg.astype(BF)
    first = (j + steps // 2) % steps * SPLIT
    pg_all[:, pl.ds(pl.multiple_of(first * UNIT, SPLIT * UNIT), SPLIT * UNIT)] = pg
    gi = dot(x, pg, TN).astype(BF)
    for s in range(SPLIT):
        place = tab[64 + first + s]
        gb_out[:, pl.ds(pl.multiple_of(place * UNIT, UNIT), UNIT)] = gb[:, s * UNIT : (s + 1) * UNIT]
        row = pl.multiple_of(place // SPLIT * unit_rows, unit_rows)
        lane = pl.multiple_of(place % SPLIT * UNIT, UNIT)
        for i in range(npos):
            stage[tab[16 + i], pl.ds(row, unit_rows), pl.ds(lane, UNIT)] = (
                gi[i * unit_rows : (i + 1) * unit_rows, s * UNIT : (s + 1) * UNIT])

    def copies(step):
        lane = tab[64 + (step + steps // 2) % steps * SPLIT] % SPLIT * UNIT
        cols = pl.ds(pl.multiple_of(lane, UNIT), UNIT)
        return [pltpu.make_async_copy(stage.at[pl.ds(half, half), :, cols], send.at[:, :, cols], sems.at[2 * step]),
                pltpu.make_async_copy(stage.at[pl.ds(0, half), :, cols], keep.at[:, :, cols], sems.at[2 * step + 1])]

    for one in copies(j):
        one.start()

    @pl.when(j == steps - 1)
    def _():
        wait_all(weight_copies())
        ng_out[...] = dot(pg_all[...], w_all[...], NT).astype(BF)
        for step in range(npos // SPLIT):
            for one in copies(step):
                one.wait()


def store_small(stage, at, tab, sums, hid_bias):
    npos = stage.shape[0]
    width = sums.shape[1]
    fill = jnp.zeros((14, 2 * UNIT), F32)
    for i in range(npos):
        tile = slice(i * width // npos // UNIT * UNIT, i * width // npos // UNIT * UNIT + UNIT)
        first = jnp.concatenate([sums[0:1, tile], sums[1:2, tile]], axis=1)
        second = jnp.concatenate([sums[2:3, tile], hid_bias[:, i * UNIT : (i + 1) * UNIT]], axis=1)
        stage[tab[16 + i], at : at + 16, :] = jnp.concatenate([first, second, fill], axis=0).astype(BF)


def gain_sums(total, unit):
    return [jnp.sum(total * unit.astype(F32), axis=0, keepdims=True), jnp.sum(total, axis=0, keepdims=True)]


def pair_back(pr, blocks, do, att, q_in, k_in, v_in, p_in, dk_acc, dv_acc, first, base_col=0):
    cols = slice(base_col + pr * PAIR, base_col + (pr + 1) * PAIR)
    top = (blocks[0] + 1) * QB
    start = blocks[-1] * QB
    q, k, v = q_in[:, cols], k_in[:, cols], v_in[:, cols]
    dob = do[:, cols].astype(BF)
    prod = dob.astype(F32) * att[:, cols].astype(F32)
    zero = jnp.zeros((), BF)
    skip = blocks[-1] * (blocks[-1] + 1) // 2 * QB
    qh, kh, doh, delta = [], [], [], []
    for h in range(2):
        mine = head_lanes((top - start, PAIR), h)
        qh.append(jnp.where(mine, q, zero))
        kh.append(jnp.where(head_lanes((top, PAIR), h), k, zero))
        doh.append(jnp.where(mine, dob, zero))
        delta.append(jnp.sum(jnp.where(mine, prod, 0.0), axis=-1, keepdims=True))
    parts = []
    for i in blocks:
        base = i * (i + 1) // 2 * QB - skip
        ext = (i + 1) * QB
        blk = slice(i * QB - start, ext - start)
        sums = [None, None, None]
        for h in range(2):
            p = jnp.concatenate(
                [p_in[2 * pr + h, base + kb * QB : base + (kb + 1) * QB, :] for kb in range(i + 1)], axis=1)
            dp = dot(doh[h][blk], v[:ext], NT)
            ds = (p.astype(F32) * (dp - delta[h][blk])).astype(BF)
            new = [dot(ds, kh[h][:ext]), dot(qh[h][blk], ds, TN), dot(doh[h][blk], p, TN)]
            sums = [n if old is None else old + n for old, n in zip(sums, new)]
        parts.append(sums[0])
        if first and i == blocks[0]:
            dk_acc[pr], dv_acc[pr] = sums[1], sums[2]
        else:
            dk_acc[pr, :, :ext] += sums[1]
            dv_acc[pr, :, :ext] += sums[2]
    return jnp.concatenate(parts[::-1], axis=0) * 0.125


def out_grads(rows, base, off, leng, cot, wo):
    place = base + lax.broadcasted_iota(jnp.int32, (rows, wo.shape[0]), 0)
    live = (place >= off[0]) & (place < off[0] + leng[0])
    return jnp.where(live, dot(cot, wo[...], NT), 0.0)


def weight_columns(tab, w_hbm, w_in, sem):
    width = w_hbm.shape[0]
    col = lambda n: pl.multiple_of(n * width + tab[48] * (width // 2), width // 2)
    return pltpu.make_async_copy(w_hbm.at[:, pl.ds(col(0), width // 2)], w_in.at[0], sem.at[0]), \
        pltpu.make_async_copy(w_hbm.at[:, pl.ds(col(1), width // 2)], w_in.at[1], sem.at[1]), \
        pltpu.make_async_copy(w_hbm.at[:, pl.ds(col(2), width // 2)], w_in.at[2], sem.at[2])


def store_block(stage, tab, at, grad, gao):
    npos = stage.shape[0]
    rows = grad[0].shape[0] // npos
    for n in range(3):
        for i in range(npos):
            stage[tab[16 + i], at + n * rows : at + (n + 1) * rows, :] = grad[n][i * rows : (i + 1) * rows]
    at += 3 * rows
    rows = gao.shape[0] // npos
    for i in range(npos):
        for n in range(2):
            stage[tab[32 + i], at + n * rows : at + (n + 1) * rows, :] = (
                gao[i * rows : (i + 1) * rows, n * GROUP : (n + 1) * GROUP])


def send_out(stage, keep, send, sems):
    part = stage.shape[0] // 2
    copy = pltpu.make_async_copy
    wait_all(start_all([copy(stage.at[pl.ds(part, part)], send, sems.at[0]),
                        copy(stage.at[pl.ds(0, part)], keep, sems.at[1])]))


def attn_wide_kernel(tab, off, leng, cot, wo, cos_ref, low_ref, high_ref,
                     att_hbm, q_hbm, k_hbm, v_hbm, p_hbm, x_hbm, unit_hbm, ng_hbm, w_hbm, *refs):
    ng_out = refs[:-27]
    (first_out, dqkv_out, dka_out, dva_out, gao_out, sums, keep, send,
     att_in, q_in, k_in, v_in, p_in, p_hi, x_in, unit_in, ng_in, w_in, first, dqkv, dk_acc, dv_acc, dk_hi, dv_hi,
     gao, stage, sems) = refs[-27:]
    rows, width = cot.shape
    half = rows // 2
    nq = rows // QB
    pairs = GROUP // PAIR
    skip = nq // 2 * (nq // 2 + 1) // 2 * QB
    count = p_hi.shape[1]
    lo, hi, group = pl.ds(0, half), pl.ds(half, half), pl.ds(GROUP, GROUP)
    copy = pltpu.make_async_copy
    early = start_all([copy(q_hbm, q_in, sems.at[0]), copy(k_hbm, k_in, sems.at[1]),
                       copy(v_hbm, v_in, sems.at[2]), copy(att_hbm, att_in, sems.at[3])])
    loads = start_all([copy(p_hbm.at[pl.ds(2 * pr, 2)], p_in.at[pl.ds(2 * pr, 2)], sems.at[4 + pr])
                       for pr in range(pairs)])
    loads += start_all([copy(p_hbm.at[pl.ds(2 * (pairs + pr), 2), pl.ds(skip, count)], p_hi.at[pl.ds(2 * pr, 2)],
                             sems.at[4 + pairs + pr]) for pr in range(pairs)])
    at = 4 + 2 * pairs
    late = start_all([copy(x_hbm, x_in, sems.at[at]), *weight_columns(tab, w_hbm, w_in, sems.at[pl.ds(at + 1, 3)]),
                      copy(ng_hbm.at[hi], ng_in, sems.at[at + 4]), copy(unit_hbm.at[hi], unit_in, sems.at[at + 5])])
    cosine, low, high = cos_ref[...], low_ref[...], high_ref[...]
    do = out_grads(rows, 0, off, leng, cot[...], wo)
    blocks = list(reversed(range(nq)))
    wait_all(early)
    for pr in range(pairs):
        loads[pr].wait()
        cols = slice(pr * PAIR, (pr + 1) * PAIR)
        dq = pair_back(pr, blocks, do, att_in, q_in, k_in, v_in, p_in, dk_acc, dv_acc, True)
        first[0, :, cols] = turn_back(dq, cosine, low, high).astype(BF)
        first[1, :, cols] = turn_back(dk_acc[pr].T, cosine, low, high).astype(BF)
        first[2, :, cols] = dv_acc[pr].T.astype(BF)
    outs = start_all([copy(first, first_out, sems.at[0])])
    do = do[half:]
    blocks = list(reversed(range(nq // 2, nq)))
    cosine, low, high = cosine[half:], low[half:], high[half:]
    for pr in range(pairs):
        loads[pairs + pr].wait()
        cols = slice(GROUP + pr * PAIR, GROUP + (pr + 1) * PAIR)
        dq = pair_back(pr, blocks, do, att_in.at[hi], q_in.at[hi], k_in, v_in, p_hi, dk_hi, dv_hi, True, GROUP)
        dqkv[0, :, cols] = turn_back(dq, cosine, low, high).astype(BF)
        dqkv[1, :, cols] = turn_back(dk_hi[pr, :, half:].T, cosine, low, high).astype(BF)
        dqkv[2, :, cols] = dv_hi[pr, :, half:].T.astype(BF)
    outs += start_all([copy(dqkv.at[:, :, group], dqkv_out, sems.at[1]), copy(dk_hi.at[:, :, lo], dka_out, sems.at[2]),
                       copy(dv_hi.at[:, :, lo], dva_out, sems.at[3])])
    all_gao = dot(att_in[...], cot[...], TN).astype(BF)
    gao[...] = all_gao[:, width // 2 :]
    outs += start_all([copy(gao, gao_out, sems.at[4])])
    wait_all(late)
    x = x_in[...]
    store_block(stage, tab, 0, [dot(x, first[n], TN).astype(BF) for n in range(3)], all_gao[:, : width // 2])
    part = stage.shape[0] // 2
    outs += start_all([copy(stage.at[pl.ds(part, part)], send, sems.at[5]), copy(stage.at[pl.ds(0, part)], keep, sems.at[6])])
    total = ng_in[...].astype(F32)
    for n in range(3):
        total = total + dot(first[n, half:], w_in[n, :, :GROUP], NT) + dot(dqkv[n, :, GROUP:], w_in[n, :, GROUP:], NT)
    at = 0
    for to in ng_out:
        to[...] = total[at : at + to.shape[0]].astype(BF)
        at += to.shape[0]
    sums[...] = jnp.concatenate(
        gain_sums(total, unit_in[...]) + [jnp.sum(cot[...].astype(F32), axis=0, keepdims=True), jnp.zeros((5, width), F32)],
        axis=0)
    wait_all(outs)


def attn_low_kernel(tab, off, leng, cot, wo, cos_ref, low_ref, high_ref, hid_bias, sums_in,
                    att_hbm, q_hbm, k_hbm, v_hbm, p_hbm, unit_hbm, ng_hbm, w_hbm, x_hbm, first_hbm, dqkv_hbm, dka_hbm,
                    dva_hbm, gao_hbm, *refs):
    ng_out = refs[:-18]
    (keep, send, stage, att_in, q_in, k_in, v_in, p_in, unit_in, ng_in, w_in, x_in, dqkv, dqkv_hi, dk_acc, dv_acc, gao,
     sems) = refs[-18:]
    half, width = cot.shape
    nq = 2 * half // QB
    pairs = GROUP // PAIR
    count = p_in.shape[1]
    lo, group = pl.ds(0, half), pl.ds(GROUP, GROUP)
    copy = pltpu.make_async_copy
    early = start_all([copy(q_hbm.at[lo, group], q_in, sems.at[0]), copy(k_hbm.at[lo, group], k_in, sems.at[1]),
                       copy(v_hbm.at[lo, group], v_in, sems.at[2]), copy(att_hbm.at[lo, group], att_in, sems.at[3]),
                       copy(dka_hbm, dk_acc, sems.at[4]), copy(dva_hbm, dv_acc, sems.at[5])])
    loads = start_all([copy(p_hbm.at[pl.ds(4 + 2 * pr, 2), pl.ds(0, count)], p_in.at[pl.ds(2 * pr, 2)], sems.at[6 + pr])
                       for pr in range(pairs)])
    at = 6 + pairs
    late = start_all([copy(dqkv_hbm, dqkv_hi, sems.at[at]), copy(x_hbm, x_in, sems.at[at + 1]),
                      *weight_columns(tab, w_hbm, w_in, sems.at[pl.ds(at + 2, 3)]),
                      copy(ng_hbm.at[lo], ng_in, sems.at[at + 5]), copy(unit_hbm.at[lo], unit_in, sems.at[at + 6]),
                      copy(gao_hbm, gao, sems.at[at + 7]),
                      copy(first_hbm.at[:, lo], dqkv.at[:, :, pl.ds(0, GROUP)], sems.at[at + 8])])
    do = out_grads(half, 0, off, leng, cot[...], wo)
    cosine, low, high = cos_ref[...], low_ref[...], high_ref[...]
    blocks = list(reversed(range(nq // 2)))
    wait_all(early)
    for pr in range(pairs):
        loads[pr].wait()
        cols = slice(GROUP + pr * PAIR, GROUP + (pr + 1) * PAIR)
        dq = pair_back(pr, blocks, do, att_in, q_in, k_in, v_in, p_in, dk_acc, dv_acc, False)
        dqkv[0, :, cols] = turn_back(dq, cosine, low, high).astype(BF)
        dqkv[1, :, cols] = turn_back(dk_acc[pr].T, cosine, low, high).astype(BF)
        dqkv[2, :, cols] = dv_acc[pr].T.astype(BF)
    wait_all(late)
    x = x_in[...]
    grad = [(dot(x[:half], dqkv[n, :, GROUP:], TN) + dot(x[half:], dqkv_hi[n], TN)).astype(BF) for n in range(3)]
    store_block(stage, tab, 0, grad, gao[...])
    total = ng_in[...].astype(F32)
    for n in range(3):
        total = total + dot(dqkv[n], w_in[n], NT)
    at = 0
    for to in ng_out:
        to[...] = total[at : at + to.shape[0]].astype(BF)
        at += to.shape[0]
    sums = sums_in[...]
    new = gain_sums(total, unit_in[...])
    store_small(stage, stage.shape[1] - 16, tab,
                jnp.concatenate([sums[0:1] + new[0], sums[1:2] + new[1], sums[2:3]], axis=0), hid_bias[...])
    send_out(stage, keep, send, sems)


def act_kernel(tok, bias, own_low, own_high, recv_low, recv_high, out):
    cut = own_low.shape[0]
    for rows, own, recv in ((slice(0, cut), own_low, recv_low), (slice(cut, tok.shape[0]), own_high, recv_high)):
        base = tok[rows].astype(F32) + bias[...]
        out[rows] = (base + (own[...].astype(F32) + recv[...].astype(F32))).astype(BF)


def finish_kernel(unit_ref, inv, cot, ng_a, ng_b, gain, *refs):
    out = refs[-1]
    unit = unit_ref[...].astype(F32)
    scaled = (ng_a[...].astype(F32) + ng_b[...].astype(F32)) * gain[...]
    mean = jnp.mean(scaled, axis=-1, keepdims=True)
    lean = jnp.mean(scaled * unit, axis=-1, keepdims=True)
    out[...] = (cot[...].astype(F32) + inv[:, :1] * (scaled - mean - unit * lean)).astype(BF)


def const_spec(shape):
    zeros = (0,) * len(shape)
    return pl.BlockSpec(shape, lambda g, *tabs: zeros, pipeline_mode=pl.Buffered(1))


def in_hbm(value):
    return pltpu.with_memory_space_constraint(value, pltpu.HBM)


def params(limit=LIMIT):
    return pltpu.CompilerParams(vmem_limit_bytes=limit)


def rotary_tables(rows):
    lane = np.arange(PAIR) % HEAD
    half = ROT // 2
    angle = np.arange(rows)[:, None] * np.power(10000.0, (lane % half) * (-2.0 / ROT))[None, :]
    inside = (lane < ROT)[None, :]
    cosine = np.where(inside, np.cos(angle), 1.0)
    low = np.where((lane < half)[None, :], -np.sin(angle), 0.0)
    high = np.where(inside & (lane >= half)[None, :], np.sin(angle), 0.0)
    return [jnp.asarray(t, F32) for t in (cosine, low, high)]


def mlp_specs(width, npos):
    steps = npos // SPLIT
    turn_of = lambda j: (j + steps // 2) % steps
    w_in = [pl.BlockSpec((width, UNIT), lambda j, t, s=s: (0, t[turn_of(j) * SPLIT + s])) for s in range(SPLIT)]
    b_in = [pl.BlockSpec((1, UNIT), lambda j, t, s=s: (0, t[turn_of(j) * SPLIT + s])) for s in range(SPLIT)]
    w_out = [pl.BlockSpec((UNIT, width), lambda j, t, s=s: (t[turn_of(j) * SPLIT + s], 0)) for s in range(SPLIT)]
    return w_in, b_in, w_out, lambda rows: pl.BlockSpec((rows, SPLIT * UNIT), lambda j, t: (0, turn_of(j)))


def mlp_forward(tab, tokens, gain, bias, cot, w_in, b_in, w_out, npos):
    rows, width = tokens.shape
    wi, bi, wo, wide = mlp_specs(width, npos)
    steps = npos // SPLIT
    full = jax.ShapeDtypeStruct((rows, width), BF)
    part = jax.ShapeDtypeStruct((npos // 2, 2 * UNIT, 512), BF)
    block = (SPLIT, 2 * UNIT, 512)
    return pl.pallas_call(
        mlp_fwd_kernel,
        grid_spec=pltpu.PrefetchScalarGridSpec(
            num_scalar_prefetch=1,
            grid=(steps,),
            in_specs=[const_spec((rows, width)), const_spec((1, width)), const_spec((1, width)),
                      const_spec((rows, width))] + wi + bi + [pl.BlockSpec(memory_space=pl.ANY)],
            out_specs=[pl.BlockSpec(memory_space=pl.ANY)] * 3 + [wide(rows),
                       const_spec((rows, width)),
                       pl.BlockSpec(block, lambda j, t: (jnp.maximum(j - steps // 2, 0), 0, 0)),
                       pl.BlockSpec(block, lambda j, t: (jnp.minimum(j, steps // 2 - 1), 0, 0))],
            scratch_shapes=[pltpu.VMEM((rows, npos * UNIT), BF), pltpu.VMEM((npos * UNIT, width), BF),
                            pltpu.VMEM((rows, width), BF), pltpu.VMEM((rows, width), BF),
                            pltpu.VMEM((rows, PAIR), F32), pltpu.SemaphoreType.DMA((3 + npos,))],
        ),
        out_shape=[pltpu.HBM((rows, width), BF), pltpu.HBM((rows, width), BF), pltpu.HBM((rows, PAIR), F32),
                   jax.ShapeDtypeStruct((rows, npos * UNIT), BF), full, part, part],
        compiler_params=params(MAIN),
        cost_estimate=pl.CostEstimate(flops=20 * 10**9, bytes_accessed=10**7, transcendentals=0),
        name="mlp_forward",
    )(tab, *[in_hbm(t) for t in (tokens, gain, bias, cot)], *([w_in] * SPLIT), *([in_hbm(b_in)] * SPLIT), w_out)


def attn_forward(tab, off, leng, normed, mlp_out, w_qkv, w_ao, tables):
    rows, width = normed.shape
    groups = width // 2 // GROUP
    tri = (rows // QB) * (rows // QB + 1) // 2 * QB
    anyspec = pl.BlockSpec(memory_space=pl.ANY)
    half = pltpu.HBM((rows, width // 2), BF)
    cols = pltpu.VMEM((rows, width // 2), BF)
    sizes = (rows * ACT_LOW // 16, rows - rows * ACT_LOW // 16)
    return pl.pallas_call(
        attn_fwd_kernel,
        grid_spec=pltpu.PrefetchScalarGridSpec(
            num_scalar_prefetch=3,
            grid=(1,),
            in_specs=[const_spec((rows, width))] + [const_spec((rows, PAIR))] * 3 + [anyspec] * 3,
            out_specs=[anyspec] * 5 + [const_spec((n, width)) for n in sizes],
            scratch_shapes=[pltpu.VMEM((groups, 3, width, GROUP), BF), pltpu.VMEM((width // 2, width), BF),
                            pltpu.VMEM((rows, width), BF), cols, cols, cols, pltpu.VMEM((HEADS // 2, tri, QB), BF), cols,
                            pltpu.SemaphoreType.DMA((3 * groups + 2 + groups * (GROUP // PAIR + 4),))],
        ),
        out_shape=[half, half, half, pltpu.HBM((HEADS // 2, tri, QB), BF), half]
        + [jax.ShapeDtypeStruct((n, width), BF) for n in sizes],
        compiler_params=params(FORWARD),
        cost_estimate=pl.CostEstimate(flops=20 * 10**9, bytes_accessed=10**7, transcendentals=0),
        name="attention_forward",
    )(tab, off, leng, normed, *tables, in_hbm(w_qkv), w_ao, mlp_out)


def mlp_backward(tab, normed, cot, dg, w_in, w_out, npos):
    rows, width = normed.shape
    wi, _, wo, wide = mlp_specs(width, npos)
    unit_rows = width // npos
    ublock = npos // SPLIT * unit_rows
    part = jax.ShapeDtypeStruct((npos // 2, ublock, 512), BF)
    anyspec = pl.BlockSpec(memory_space=pl.ANY)
    return pl.pallas_call(
        mlp_back_kernel,
        grid_spec=pltpu.PrefetchScalarGridSpec(
            num_scalar_prefetch=1,
            grid=(npos // SPLIT,),
            in_specs=[const_spec((rows, width)), const_spec((rows, width)),
                      wide(rows), anyspec] + wo,
            out_specs=[const_spec((1, npos * UNIT)), const_spec((rows, width)), anyspec, anyspec],
            scratch_shapes=[pltpu.VMEM((npos, ublock, 512), BF), pltpu.VMEM((rows, npos * UNIT), BF),
                            pltpu.VMEM((width, npos * UNIT), BF), pltpu.SemaphoreType.DMA((2 * npos // SPLIT + npos,))],
        ),
        out_shape=[jax.ShapeDtypeStruct((1, npos * UNIT), F32), jax.ShapeDtypeStruct((rows, width), BF), part, part],
        compiler_params=params(MAIN),
        cost_estimate=pl.CostEstimate(flops=20 * 10**9, bytes_accessed=10**7, transcendentals=0),
        name="mlp_backward",
    )(tab, normed, cot, dg, w_in, *([w_out] * SPLIT))


def back_specs(width, half_rows, place, group, count):
    row = lambda n: pl.BlockSpec((half_rows, n), lambda i, *t: (place, 0), pipeline_mode=pl.Buffered(1))
    blocks = width // 2 // GROUP // count
    out = pl.BlockSpec((GROUP * count, width), lambda i, t, o, l: (t[48] * blocks + group, 0),
                       pipeline_mode=pl.Buffered(1))
    return [row(width), out] + [row(PAIR)] * 3


def back_call(kernel, name, cost, scratch, in_specs, out_specs, out_shape):
    return pl.pallas_call(
        kernel,
        grid_spec=pltpu.PrefetchScalarGridSpec(
            num_scalar_prefetch=3, grid=(1,), in_specs=in_specs, out_specs=out_specs, scratch_shapes=scratch),
        out_shape=out_shape,
        compiler_params=params(BACK),
        cost_estimate=pl.CostEstimate(flops=cost, bytes_accessed=10**5, transcendentals=0),
        name=name,
    )


def stage_rows(width, npos):
    return 3 * (width // npos) + 2 * (width // 2 // npos)


def attn_back_wide(tab, off, leng, cot, att, q, k, v, p, unit, w_qkv, w_ao, ng, tables, normed, npos):
    rows, width = cot.shape
    half = rows // 2
    nq = rows // QB
    count = p.shape[1] - nq // 2 * (nq // 2 + 1) // 2 * QB
    pairs = GROUP // PAIR
    anyspec = pl.BlockSpec(memory_space=pl.ANY)
    sizes = [size * UNIT for at, size in NG_PARTS if at * UNIT >= half]
    ublock = stage_rows(width, npos)
    part = jax.ShapeDtypeStruct((npos // 2, ublock, GROUP), BF)
    accs = pltpu.HBM((pairs, PAIR, half), F32)
    cols = pltpu.VMEM((rows, width // 2), BF)
    acc = pltpu.VMEM((pairs, PAIR, rows), F32)
    wide = pltpu.VMEM((half, width), BF)
    return back_call(
        attn_wide_kernel, "attention_back_wide", 20 * 10**9,
        [cols, cols, cols, cols, pltpu.VMEM((GROUP // HEAD, p.shape[1], QB), BF), pltpu.VMEM((GROUP // HEAD, count, QB), BF),
         pltpu.VMEM((rows, width), BF), wide, wide, pltpu.VMEM((3, width, width // 2), BF), pltpu.VMEM((3, rows, GROUP), BF),
         pltpu.VMEM((3, half, width // 2), BF), acc, acc, acc, acc, pltpu.VMEM((width // 2, width // 2), BF),
         pltpu.VMEM((npos, ublock, GROUP), BF), pltpu.SemaphoreType.DMA((2 * pairs + 10,))],
        back_specs(width, rows, 0, 0, 2) + [anyspec] * 9,
        [const_spec((n, width)) for n in sizes] + [anyspec] * 5 + [const_spec((8, width)), anyspec, anyspec],
        [jax.ShapeDtypeStruct((n, width), BF) for n in sizes]
        + [pltpu.HBM((3, rows, GROUP), BF), pltpu.HBM((3, half, GROUP), BF), accs, accs,
           pltpu.HBM((width // 2, width // 2), BF), jax.ShapeDtypeStruct((8, width), F32), part, part],
    )(tab, off, leng, cot, w_ao, *tables, att, q, k, v, p, normed, unit, ng, w_qkv)


def attn_back_low(tab, off, leng, cot, att, q, k, v, p, unit, w_qkv, w_ao, ng, tables, normed, hid_bias, first,
                  gao, carried, npos):
    rows, width = cot.shape
    half = rows // 2
    nq = rows // QB
    count = nq // 2 * (nq // 2 + 1) // 2 * QB
    pairs = GROUP // PAIR
    anyspec = pl.BlockSpec(memory_space=pl.ANY)
    sizes = [size * UNIT for at, size in NG_PARTS if at * UNIT < half]
    ublock = stage_rows(width, npos) + 16
    part = jax.ShapeDtypeStruct((npos // 2, ublock, GROUP), BF)
    dqkv, dk_acc, dv_acc, sums = carried
    cols = pltpu.VMEM((half, GROUP), BF)
    acc = pltpu.VMEM((pairs, PAIR, half), F32)
    wide = pltpu.VMEM((half, width), BF)
    return back_call(
        attn_low_kernel, "attention_back_low", 20 * 10**9,
        [pltpu.VMEM((npos, ublock, GROUP), BF), cols, cols, cols, cols, pltpu.VMEM((GROUP // HEAD, count, QB), BF),
         wide, wide, pltpu.VMEM((3, width, width // 2), BF), pltpu.VMEM((rows, width), BF),
         pltpu.VMEM((3, half, width // 2), BF), pltpu.VMEM((3, half, GROUP), BF), acc, acc,
         pltpu.VMEM((width // 2, width // 2), BF), pltpu.SemaphoreType.DMA((pairs + 15,))],
        back_specs(width, half, 0, 1, 1) + [const_spec((1, npos * UNIT)), const_spec((8, width))]
        + [anyspec] * 14,
        [const_spec((n, width)) for n in sizes] + [anyspec, anyspec],
        [jax.ShapeDtypeStruct((n, width), BF) for n in sizes] + [part, part],
    )(tab, off, leng, cot, w_ao, *tables, hid_bias, sums, att, q, k, v, p, unit, ng, w_qkv, normed, first, dqkv,
      dk_acc, dv_acc, gao)


def act_sum(tokens, bias, own, recv):
    return pl.pallas_call(
        act_kernel,
        grid=(1,),
        in_specs=[const_spec(t.shape) for t in (tokens, bias, *own, *recv)],
        out_specs=const_spec(tokens.shape),
        out_shape=jax.ShapeDtypeStruct(tokens.shape, BF),
        compiler_params=params(),
        cost_estimate=pl.CostEstimate(flops=10**6, bytes_accessed=10**6, transcendentals=0),
        name="activations",
    )(in_hbm(tokens), bias, *[in_hbm(t) for t in (*own, *recv)])


def finish(n, unit, inv, cot, ng_a, ng_b, gain, done):
    rows, width = unit.shape
    step = UNIT
    at, count = NG_PARTS[n]
    row = pl.BlockSpec((step, width), lambda r: (at + r, 0))
    part = pl.BlockSpec((step, width), lambda r: (r, 0))
    return pl.pallas_call(
        finish_kernel,
        grid=(count,),
        in_specs=[row, pl.BlockSpec((step, PAIR), lambda r: (at + r, 0)), row, part, part,
                  pl.BlockSpec((1, width), lambda r: (0, 0))]
        + [pl.BlockSpec(memory_space=pl.ANY)] * len(done),
        out_specs=row,
        out_shape=jax.ShapeDtypeStruct((rows, width), BF),
        input_output_aliases={6: 0} if done else {},
        compiler_params=params(),
        cost_estimate=pl.CostEstimate(flops=10**7, bytes_accessed=10**6, transcendentals=0),
        name="norm_backward",
    )(*[in_hbm(t) for t in (unit, inv, cot, ng_a, ng_b)], gain, *done)


def bit_reverse(value, bits):
    out = 0
    for n in range(bits):
        out |= (value >> n & 1) << (bits - 1 - n)
    return out


NPOS = 16
ACT_LOW = 7
NG_PARTS = ((4, 2), (6, 2), (0, 2), (2, 2))


def place_tables(ndp):
    bits = NPOS.bit_length() - 1
    table = np.zeros((ndp, 2, 80), np.int32)
    for d in range(ndp):
        for b in range(2):
            for n in range(NPOS):
                if ndp == NPOS:
                    table[d, b, n] = 2 * (bit_reverse(n, bits) ^ d) + b
                    table[d, b, 64 + n] = bit_reverse(n, bits) ^ d
                    table[d, b, 16 + n] = bit_reverse(n ^ d, bits)
                    rel = 0
                    for k in range(bits - 1):
                        rel |= ((n >> (k + 1) & 1) ^ (d >> k & 1)) << (bits - 1 - k)
                    rel |= (n & 1) ^ (d >> (bits - 1) & 1)
                    table[d, b, 32 + n] = rel
                else:
                    table[d, b, n] = b * NPOS + n
                    table[d, b, 64 + n] = n
                    table[d, b, 16 + n] = n
                    table[d, b, 32 + n] = n
            table[d, b, 48] = b
    return table


def after(values, *others):
    out = lax.optimization_barrier((values,) + others)
    return out[0]


def trade(send, bit, ndp):
    return lax.ppermute(send, "dp", [(d, d ^ bit) for d in range(ndp)])


def add_halves(keep, recv):
    half = keep.shape[0] // 2
    mine = (keep[:half].astype(F32) + recv[:half].astype(F32)).astype(BF)
    other = (keep[half:].astype(F32) + recv[half:].astype(F32)).astype(BF)
    return mine, other


def add_quarters(keep, recv):
    parts = [keep[n].astype(F32) + recv[n].astype(F32) for n in range(4)]
    return parts[0], [part.astype(BF) for part in parts[1:]]


def trade_quarters(parts, ndp):
    return [trade(part, bit, ndp) for part, bit in zip(parts, (8, 4, 12))]


def add_all(mine, recvs):
    for recv in recvs:
        mine = mine + recv.astype(F32)
    return mine


def place_columns_kernel(tab, own, recv, out):
    b = tab[48]
    for n in range(NPOS):
        step, s = n // SPLIT, n % SPLIT
        col = slice(s * UNIT, (s + 1) * UNIT)
        mine = (2 * n + b) * UNIT
        theirs = (2 * n + 1 - b) * UNIT
        out[:, pl.ds(pl.multiple_of(mine, UNIT), UNIT)] = own[step, :, col].astype(F32)
        out[:, pl.ds(pl.multiple_of(theirs, UNIT), UNIT)] = recv[step, :, col].astype(F32)


def shards(ndp, tokens, offsets, lengths, cotangent, ln_gain, ln_bias, w_qkv, w_attn_out, w_in, b_in, w_out, b_out):
    rows, width = tokens.shape
    dp = lax.axis_index("dp")
    b = lax.axis_index("branch")
    hidden = w_in.shape[1]
    tables = rotary_tables(rows)
    all_tab = jnp.asarray(place_tables(ndp))
    tab = lax.dynamic_slice(all_tab, (dp, b, 0), (1, 1, 80)).reshape(80)
    gain = ln_gain.reshape(1, width)
    bias = ln_bias.reshape(1, width)
    swap = [(0, 1), (1, 0)]
    halving = ndp == NPOS

    normed, unit, inv, dg, mlp_out, a_keep, a_send = mlp_forward(
        tab, tokens, gain, bias, cotangent, w_in, b_in.reshape(1, hidden), w_out, NPOS)
    barrier = lax.optimization_barrier
    a_part = (a_keep, a_send)
    a_recv = trade(a_send, 1, ndp) if halving else a_send
    q, k, v, p, att, *act_own = attn_forward(
        tab, offsets, lengths, after(normed, a_send), mlp_out, w_qkv, w_attn_out, tables)
    a_recv, att, *act_own = barrier((a_recv, att, *act_own))
    act_recv = [lax.ppermute(part, "branch", swap) for part in act_own]
    if halving:
        a_keep, a_send = add_halves(a_keep, a_recv)
        a_recv = trade(a_send, 2, ndp)
    gb_in, ng, b_keep, b_send = mlp_backward(tab, normed, cotangent, after(dg, att, a_send), w_in, w_out, NPOS)
    b_part = (b_keep, b_send)
    a_recv, b_send, ng, act_recv[0] = barrier((a_recv, b_send, ng, act_recv[0]))
    if halving:
        b_recv = trade(b_send, 1, ndp)
        a_mine, a_send = add_quarters(a_keep, a_recv)
        a_recv = trade_quarters(a_send, ndp)
        b_keep, b_send = add_halves(b_keep, b_recv)
        b_recv = trade(b_send, 2, ndp)
    else:
        b_recv = b_send
        a_recv, a_send = [a_recv], [a_send]
    *ng_own, first, dqkv, dk_acc, dv_acc, gao, sums, c_keep, c_send = attn_back_wide(
        tab, offsets, lengths, cotangent, after(att, b_send, *a_send), q, k, v, p, unit, w_qkv, w_attn_out, ng, tables,
        normed, NPOS)
    c_part = (c_keep, c_send)
    b_recv, a_recv, act_recv[1], c_send, ng_own = barrier((b_recv, a_recv, act_recv[1], c_send, ng_own))
    ng_recv = [lax.ppermute(part, "branch", swap) for part in ng_own]
    c_recv = c_send
    if halving:
        c_recv = trade(c_send, 1, ndp)
        b_keep, b_send = add_halves(b_keep, b_recv)
        b_recv = trade(b_send, 4, ndp)
        c_recv, b_send = barrier((c_recv, b_send))
        c_keep, c_send = add_halves(c_keep, c_recv)
        c_recv = trade(c_send, 2, ndp)
    *more, d_keep, d_send = attn_back_low(
        tab, offsets, lengths, cotangent, after(att, b_send, c_send, ng_own[0]), q, k, v, p, unit, w_qkv, w_attn_out, ng,
        tables, normed, gb_in, first, gao, (dqkv, dk_acc, dv_acc, sums), NPOS)
    ng_own = ng_own + more
    if not halving:
        ng_recv = [lax.ppermute(part, "branch", swap) for part in ng_own]
        activations = act_sum(tokens, b_out.reshape(1, width), act_own, act_recv)
        input_grad = ()
        for n in range(len(NG_PARTS)):
            input_grad = (finish(n, unit, inv, cotangent, ng_own[n], ng_recv[n], gain, input_grad),)
        return (activations,) + input_grad + natural_sums(b, a_part, b_part, c_part, (d_keep, d_send), width, hidden)

    unit_rows = width // NPOS
    sub = unit_rows // 2
    steps = NPOS // SPLIT
    gao_rows = width // 2 // NPOS
    second = 3 * unit_rows + 2 * gao_rows
    total = lambda keep, recv: keep[0].astype(F32) + recv[0].astype(F32)

    def halves(parts):
        return (lax.dynamic_slice_in_dim(parts, b * sub, sub, 1),
                lax.dynamic_slice_in_dim(parts, (1 - b) * sub, sub, 1).astype(BF))

    b_recv, c_recv, ng_recv[0], d_send, *more = barrier((b_recv, c_recv, ng_recv[0], d_send, *more))
    ng_recv += [lax.ppermute(part, "branch", swap) for part in more]
    d_recv = trade(d_send, 1, ndp)
    c_keep, c_send = add_halves(c_keep, c_recv)
    c_recv = trade(c_send, 4, ndp)
    b_keep, b_send = add_halves(b_keep, b_recv)
    b_recv = trade(b_send, 8, ndp)
    d_recv, c_send, b_send = barrier((d_recv, c_send, b_send))
    d_keep, d_send = add_halves(d_keep, d_recv)
    d_recv = trade(d_send, 2, ndp)
    g_out = add_all(a_mine, after(a_recv, d_send)).reshape(2, UNIT, 512).transpose(1, 0, 2).reshape(UNIT, width)
    act_recv[0] = after(act_recv[0], g_out)
    activations = act_sum(tokens, b_out.reshape(1, width), act_own, act_recv)
    c_recv, d_recv, b_recv, ng_recv[1], activations = barrier((c_recv, d_recv, b_recv, ng_recv[1], activations))
    d_keep, d_send = add_halves(d_keep, d_recv)
    d_recv = trade(d_send, 4, ndp)
    c_keep, c_send = add_halves(c_keep, after(c_recv, d_send))
    c_recv = trade(c_send, 8, ndp)
    gi_own, gi_away = halves(total(b_keep, after(b_recv, c_send)).reshape(steps, unit_rows, 512))
    gi_recv = lax.ppermute(gi_away, "branch", swap)
    grad = finish(0, unit, inv, cotangent, ng_own[0], after(ng_recv[0], gi_away), gain, ())
    c_recv, d_recv, ng_recv[2], grad = barrier((c_recv, d_recv, ng_recv[2], grad))
    d_keep, d_send = add_halves(d_keep, d_recv)
    d_recv = trade(d_send, 8, ndp)
    gc = total(c_keep, after(c_recv, d_send))
    grad = finish(1, unit, inv, cotangent, ng_own[1], after(ng_recv[1], d_send), gain, (grad,))
    grad = finish(2, unit, inv, cotangent, ng_own[2], ng_recv[2], gain, (grad,))
    d_recv, ng_recv[3], gc, gi_recv, grad = barrier((d_recv, ng_recv[3], gc, gi_recv, grad))
    gd = total(d_keep, d_recv)
    gq = jnp.concatenate([gc[: 3 * unit_rows].reshape(3, unit_rows, GROUP), gd[: 3 * unit_rows].reshape(3, unit_rows, GROUP)],
                         axis=2)
    gq_own, gq_away = halves(gq)
    gao = jnp.concatenate([g[3 * unit_rows + n * gao_rows : 3 * unit_rows + (n + 1) * gao_rows]
                           for g in (gc, gd) for n in range(2)], axis=1)
    small = gd[second : second + 2]
    both = jnp.concatenate([gq_away, jnp.broadcast_to(small[:1].astype(BF)[None], (3, sub, GROUP))], axis=2)
    both_recv = lax.ppermute(both, "branch", swap).astype(F32)
    g_in = pl.pallas_call(
        place_columns_kernel,
        grid_spec=pltpu.PrefetchScalarGridSpec(
            num_scalar_prefetch=1, grid=(1,),
            in_specs=[const_spec((steps, sub, 512))] * 2,
            out_specs=const_spec((sub, hidden)),
        ),
        out_shape=jax.ShapeDtypeStruct((sub, hidden), F32),
        compiler_params=params(),
        name="place_columns",
    )(tab, gi_own, after(gi_recv, both))
    top = ndp // 2
    pairs = [(d * 2 + c, (d ^ top) * 2 + 1 - c) for d in range(ndp) for c in range(2) if d // top != c]
    moved = lax.ppermute(gao.astype(BF), ("dp", "branch"), pairs)
    input_grad = finish(3, unit, inv, cotangent, ng_own[3], ng_recv[3], gain, (grad,))
    g_ao = jnp.where(dp // top == b, gao, moved.astype(F32))
    recv = both_recv[:, :, : 2 * GROUP]
    first = jnp.where(b == 0, gq_own, recv)
    second_half = jnp.where(b == 0, recv, gq_own)
    g_qkv = jnp.concatenate(sum([[first[n], second_half[n]] for n in range(3)], []), axis=1)
    per = width // (2 * ndp)
    lane = dp % (UNIT // (2 * per)) * 2 * per + b * per
    row = small[0] + both_recv[0, 0, 2 * GROUP :]
    cut = lambda values, start: lax.dynamic_slice(values, (start,), (per,))
    return (activations, input_grad, cut(row, lane), cut(row, UNIT + lane), g_qkv, g_ao, g_in,
            small[1, UNIT:], g_out, cut(small[1], lane))


def natural_sums(b, a_part, b_part, c_part, d_part, width, hidden):
    axes = ("dp", "branch")
    steps = NPOS // SPLIT
    unit_rows = width // NPOS
    gao_rows = width // 2 // NPOS
    second = 3 * unit_rows + 2 * gao_rows
    wa, wb, wc, wd = [jnp.concatenate(part, axis=0).astype(F32) for part in (a_part, b_part, c_part, d_part)]
    go = wa.reshape(NPOS, 2, UNIT, 512).transpose(0, 2, 1, 3).reshape(NPOS * UNIT, width)
    gi = wb.reshape(NPOS, steps, unit_rows, 512).transpose(0, 2, 1, 3)
    gi = gi.reshape(width, hidden // 2)
    gq = jnp.concatenate([w[:, : 3 * unit_rows].reshape(NPOS, 3, unit_rows, GROUP) for w in (wc, wd)], axis=3)
    gq = gq.transpose(0, 2, 1, 3).reshape(width, 3, 2 * GROUP)
    ga = jnp.concatenate([w[:, 3 * unit_rows : second].reshape(NPOS, 2, gao_rows, GROUP) for w in (wc, wd)], axis=1)
    ga = ga.transpose(0, 2, 1, 3).reshape(NPOS * gao_rows, width)
    tiles = wd[:, second : second + 2]
    per_tile = UNIT // unit_rows

    def vector(row, lane):
        split = tiles[:, row, lane : lane + UNIT].reshape(NPOS // per_tile, per_tile, per_tile, unit_rows)
        return jnp.stack([split[:, n, n] for n in range(per_tile)], axis=1).reshape(width)

    def scatter(part, full, dim):
        starts = [0] * part.ndim
        starts[dim] = b * part.shape[dim]
        whole = lax.dynamic_update_slice(jnp.zeros(full, F32), part, starts)
        return lax.psum_scatter(whole, axes, scatter_dimension=0, tiled=True)

    total = lambda t: lax.psum_scatter(t, axes, scatter_dimension=0, tiled=True)
    g_qkv = scatter(gq, (width, 3, width), 2)
    return (
        total(vector(0, 0)),
        total(vector(0, UNIT)),
        g_qkv.reshape(g_qkv.shape[0], 3 * width),
        scatter(ga, (width, width), 0),
        scatter(gi, (width, hidden), 1),
        scatter(tiles[:, 1, UNIT:].reshape(-1), (hidden,), 0),
        scatter(go, (hidden, width), 0),
        total(jnp.where(b == 0, vector(1, 0), 0.0)),
    )


def solution(mesh):
    return jax.shard_map(
        functools.partial(shards, mesh.shape["dp"]),
        mesh=mesh,
        in_specs=(P("dp", None), P("dp"), P("dp"), P("dp", None)) + (P(),) * 8,
        out_specs=(
            P("dp", None),
            P("dp", None),
            P(("dp", "branch")),
            P(("dp", "branch")),
            P(("dp", "branch"), None),
            P(("dp", "branch"), None),
            P(("dp", "branch"), None),
            P(("dp", "branch")),
            P(("dp", "branch"), None),
            P(("dp", "branch")),
        ),
        check_vma=False,
    )
```

```python
import functools

import jax
import jax.numpy as jnp
import numpy as np
from jax import lax
from jax.experimental import pallas as pl
from jax.experimental.pallas import tpu as pltpu
from jax.sharding import PartitionSpec as P

HEADS = 16
HEAD = 64
ROT = 32
EPSILON = 1e-05
MASKED = -1e30
BF = jnp.bfloat16
F32 = jnp.float32
QB = 256
PAIR = 128
GROUP = 256
UNIT = 128
SPLIT = 4
LIMIT = 60 * 2**20
MAIN = 36 * 2**20
BACK = 48 * 2**20
FORWARD = 44 * 2**20

NN = (((1,), (0,)), ((), ()))
NT = (((1,), (1,)), ((), ()))
TN = (((0,), (0,)), ((), ()))


def dot(left, right, dims=NN):
    return lax.dot_general(left, right, dims, preferred_element_type=F32)


def norm_stats(rows):
    x = rows.astype(F32)
    mean = jnp.mean(x, axis=-1, keepdims=True)
    centred = x - mean
    inv = lax.rsqrt(jnp.mean(centred * centred, axis=-1, keepdims=True) + EPSILON)
    return centred * inv, inv


def gelu_both(u):
    c = 0.7978845608028654
    u2 = u * u
    t = jnp.tanh(u * (c + (c * 0.044715) * u2))
    half = 0.5 + 0.5 * t
    slope = u * (c + (3 * c * 0.044715) * u2)
    return u * half, half + 0.5 * slope * (1.0 - t * t)


def lanes(shape):
    return lax.broadcasted_iota(jnp.int32, shape, 1)


def head_lanes(shape, h):
    lane = lanes(shape)
    return (lane < HEAD) if h == 0 else (lane >= HEAD)


def turn(part, cosine, low, high):
    return part * cosine + pltpu.roll(part, PAIR - ROT // 2, 1) * low + pltpu.roll(part, ROT // 2, 1) * high


def turn_back(grad, cosine, low, high):
    return grad * cosine + pltpu.roll(grad * low, ROT // 2, 1) + pltpu.roll(grad * high, PAIR - ROT // 2, 1)


def start_all(copies):
    for one in copies:
        one.start()
    return copies


def wait_all(copies):
    for one in copies:
        one.wait()


def mlp_fwd_kernel(tab, *refs):
    tok, gain, bias, cot = refs[:4]
    w_in = refs[4 : 4 + SPLIT]
    b_in = refs[4 + SPLIT : 4 + 2 * SPLIT]
    w_out = refs[4 + 2 * SPLIT]
    (normed_out, unit_out, inv_out, dg_out, out_ref, keep, send, hid_all, w_all, normed, unit_in, inv_in,
     sems) = refs[5 + 2 * SPLIT :]
    j = pl.program_id(0)
    last = pl.num_programs(0) - 1

    def norm_copies():
        return [pltpu.make_async_copy(src, dst, sems.at[n])
                for n, (src, dst) in enumerate(((normed, normed_out), (unit_in, unit_out), (inv_in, inv_out)))]

    def weight_copies():
        return [pltpu.make_async_copy(w_out.at[pl.ds(pl.multiple_of(tab[n] * UNIT, UNIT), UNIT)],
                                      w_all.at[pl.ds(n * UNIT, UNIT)], sems.at[3 + n]) for n in range(w_all.shape[0] // UNIT)]

    @pl.when(j == 0)
    def _():
        start_all(weight_copies())
        for r in range(0, tok.shape[0], QB):
            unit, inv = norm_stats(tok[r : r + QB])
            unit_in[r : r + QB] = unit.astype(BF)
            inv_in[r : r + QB] = jnp.broadcast_to(inv, (QB, PAIR))
            normed[r : r + QB] = (unit * gain[...] + bias[...]).astype(BF)
        start_all(norm_copies())

    wi = jnp.concatenate([r[...] for r in w_in], axis=1)
    bi = jnp.concatenate([r[...] for r in b_in], axis=1)
    hid, dg = gelu_both(dot(normed[...], wi) + bi)
    hid = hid.astype(BF)
    dg_out[...] = dg.astype(BF)
    steps = pl.num_programs(0)
    place = (j + steps // 2) % steps * (SPLIT * UNIT)
    hid_all[:, pl.ds(pl.multiple_of(place, SPLIT * UNIT), SPLIT * UNIT)] = hid
    go = dot(hid, cot[...], TN).astype(BF)

    def store(to):
        for s in range(SPLIT):
            for n in range(2):
                to[s, n * UNIT : (n + 1) * UNIT, :] = go[s * UNIT : (s + 1) * UNIT, n * 512 : (n + 1) * 512]

    @pl.when(j <= last // 2)
    def _():
        store(send)

    @pl.when(j > last // 2)
    def _():
        store(keep)

    @pl.when(j == last)
    def _():
        wait_all(weight_copies())
        out_ref[...] = dot(hid_all[...], w_all[...]).astype(BF)
        wait_all(norm_copies())


def attn_fwd_kernel(tab, off, leng, x_ref, cos_ref, low_ref, high_ref, w_hbm, wo_hbm, mlp_hbm,
                    q_out, k_out, v_out, p_out, att_out, act_low, act_high,
                    w_in, wo, mlp, q_in, k_in, v_in, p_in, att_in, sems):
    rows, width = x_ref.shape
    nq = rows // QB
    pairs = GROUP // PAIR
    groups = width // 2 // GROUP
    copy = pltpu.make_async_copy
    def weight_load(g, n):
        col = pl.multiple_of(n * width + tab[48] * (width // 2) + g * GROUP, GROUP)
        return copy(w_hbm.at[:, pl.ds(col, GROUP)], w_in.at[g, n], sems.at[3 * g + n])

    start_all([weight_load(g, n) for g in range(groups) for n in range(3)])
    at = 3 * groups
    late = start_all([copy(wo_hbm.at[pl.ds(pl.multiple_of(tab[48] * (width // 2), width // 2), width // 2)], wo, sems.at[at]),
                      copy(mlp_hbm, mlp, sems.at[at + 1])])
    at += 2
    x = x_ref[...]
    start = off[0]
    stop = start + leng[0]
    place = lax.broadcasted_iota(jnp.int32, (rows, PAIR), 0)
    live = (place >= start) & (place < stop)
    kbias = jnp.where(live, 0.0, MASKED)
    live_f = jnp.where(live, 1.0, 0.0)
    lane = lanes((rows, PAIR))
    diag = lax.broadcasted_iota(jnp.int32, (QB, QB), 0) >= lax.broadcasted_iota(jnp.int32, (QB, QB), 1)
    cosine, low, high = cos_ref[...], low_ref[...], high_ref[...]
    def probs(g, pr):
        two = pl.ds(g * 2 * pairs + 2 * pr, 2)
        return copy(p_in.at[two], p_out.at[two], sems.at[at + g * (pairs + 4) + pr])

    def results(g):
        group = pl.ds(pl.multiple_of(g * GROUP, GROUP), GROUP)
        base = at + g * (pairs + 4)
        return [copy(src.at[:, group], dst.at[:, group], sems.at[base + pairs + n])
                       for n, (src, dst) in enumerate(((q_in, q_out), (k_in, k_out), (v_in, v_out), (att_in, att_out)))]

    @pl.loop(0, groups)
    def _(g):
        wait_all([weight_load(g, n) for n in range(3)])
        qa, ka, va = [dot(x, w_in[g, n]) for n in range(3)]
        for pr in range(pairs):
            cols = slice(pr * PAIR, (pr + 1) * PAIR)
            to = pl.ds(pl.multiple_of(g * GROUP + pr * PAIR, PAIR), PAIR)
            q = turn(qa[:, cols], cosine, low, high).astype(BF).astype(F32) * 0.125
            k = turn(ka[:, cols], cosine, low, high)
            v = va[:, cols]
            q_in[:, to] = q.astype(BF)
            k_in[:, to] = k.astype(BF)
            v_in[:, to] = v.astype(BF)
            qh, kh, vh = [], [], []
            for h in range(2):
                mine = head_lanes((rows, PAIR), h)
                spare = lane == (HEAD if h == 0 else 0)
                qh.append(jnp.where(mine, q, jnp.where(spare, 1.0, 0.0)).astype(BF))
                kh.append(jnp.where(mine, k, jnp.where(spare, kbias, 0.0)).astype(BF))
                vh.append(jnp.where(mine, v, 0.0).astype(BF))
            head = g * 2 * pairs + 2 * pr
            for i in range(nq):
                base = i * (i + 1) // 2 * QB
                ext = (i + 1) * QB
                mixed = None
                scores = [dot(qh[h][i * QB : ext], kh[h][:ext], NT) for h in range(2)]
                for h in range(2):
                    s = scores[h]
                    tail = jnp.where(diag, s[:, i * QB :], MASKED)
                    s = tail if i == 0 else jnp.concatenate([s[:, : i * QB], tail], axis=1)
                    e = jnp.exp(s - jnp.max(s, axis=-1, keepdims=True))
                    p = (e * (1.0 / jnp.sum(e, axis=-1, keepdims=True))).astype(BF)
                    for kb in range(i + 1):
                        p_in[head + h, base + kb * QB : base + (kb + 1) * QB, :] = p[:, kb * QB : (kb + 1) * QB]
                    part = dot(p, vh[h][:ext])
                    mixed = part if mixed is None else mixed + part
                att_in[i * QB : ext, to] = (mixed * live_f[i * QB : ext]).astype(BF)
            probs(g, pr).start()
        start_all(results(g))

    wait_all(late)
    out = mlp[...].astype(F32) + dot(att_in[...], wo[...])
    cut = act_low.shape[0]
    act_low[...] = out[:cut].astype(BF)
    act_high[...] = out[cut:].astype(BF)
    for g in range(groups):
        wait_all([probs(g, pr) for pr in range(pairs)] + results(g))


def mlp_back_kernel(tab, *refs):
    normed, cot, dg = refs[:3]
    w_in = refs[3]
    w_out = refs[4 : 4 + SPLIT]
    gb_out, ng_out, keep, send, stage, pg_all, w_all, sems = refs[4 + SPLIT :]
    j = pl.program_id(0)
    steps = pl.num_programs(0)
    npos = stage.shape[0]
    half = npos // 2
    unit_rows = normed.shape[1] // npos
    wout = jnp.concatenate([r[...] for r in w_out], axis=0)
    x, c = normed[...], cot[...]
    many = 2 * npos // SPLIT

    def weight_copies():
        return [pltpu.make_async_copy(w_in.at[:, pl.ds(pl.multiple_of(tab[n] * UNIT, UNIT), UNIT)],
                                      w_all.at[:, pl.ds(n * UNIT, UNIT)], sems.at[many + n]) for n in range(npos)]

    @pl.when(j == 0)
    def _():
        start_all(weight_copies())

    pg = dot(c, wout, NT) * dg[...].astype(F32)
    gb = jnp.sum(pg, axis=0, keepdims=True)
    pg = pg.astype(BF)
    first = (j + steps // 2) % steps * SPLIT
    pg_all[:, pl.ds(pl.multiple_of(first * UNIT, SPLIT * UNIT), SPLIT * UNIT)] = pg
    gi = dot(x, pg, TN).astype(BF)
    for s in range(SPLIT):
        place = tab[64 + first + s]
        gb_out[:, pl.ds(pl.multiple_of(place * UNIT, UNIT), UNIT)] = gb[:, s * UNIT : (s + 1) * UNIT]
        row = pl.multiple_of(place // SPLIT * unit_rows, unit_rows)
        lane = pl.multiple_of(place % SPLIT * UNIT, UNIT)
        for i in range(npos):
            stage[tab[16 + i], pl.ds(row, unit_rows), pl.ds(lane, UNIT)] = (
                gi[i * unit_rows : (i + 1) * unit_rows, s * UNIT : (s + 1) * UNIT])

    def copies(step):
        lane = tab[64 + (step + steps // 2) % steps * SPLIT] % SPLIT * UNIT
        cols = pl.ds(pl.multiple_of(lane, UNIT), UNIT)
        return [pltpu.make_async_copy(stage.at[pl.ds(half, half), :, cols], send.at[:, :, cols], sems.at[2 * step]),
                pltpu.make_async_copy(stage.at[pl.ds(0, half), :, cols], keep.at[:, :, cols], sems.at[2 * step + 1])]

    for one in copies(j):
        one.start()

    @pl.when(j == steps - 1)
    def _():
        wait_all(weight_copies())
        ng_out[...] = dot(pg_all[...], w_all[...], NT).astype(BF)
        for step in range(npos // SPLIT):
            for one in copies(step):
                one.wait()


def store_small(stage, at, tab, sums, hid_bias):
    npos = stage.shape[0]
    width = sums.shape[1]
    fill = jnp.zeros((14, 2 * UNIT), F32)
    for i in range(npos):
        tile = slice(i * width // npos // UNIT * UNIT, i * width // npos // UNIT * UNIT + UNIT)
        first = jnp.concatenate([sums[0:1, tile], sums[1:2, tile]], axis=1)
        second = jnp.concatenate([sums[2:3, tile], hid_bias[:, i * UNIT : (i + 1) * UNIT]], axis=1)
        stage[tab[16 + i], at : at + 16, :] = jnp.concatenate([first, second, fill], axis=0).astype(BF)


def gain_sums(total, unit):
    return [jnp.sum(total * unit.astype(F32), axis=0, keepdims=True), jnp.sum(total, axis=0, keepdims=True)]


def pair_back(pr, blocks, do, att, q_in, k_in, v_in, p_in, dk_acc, dv_acc, first, base_col=0):
    cols = slice(base_col + pr * PAIR, base_col + (pr + 1) * PAIR)
    top = (blocks[0] + 1) * QB
    start = blocks[-1] * QB
    q, k, v = q_in[:, cols], k_in[:, cols], v_in[:, cols]
    dob = do[:, cols].astype(BF)
    prod = dob.astype(F32) * att[:, cols].astype(F32)
    zero = jnp.zeros((), BF)
    skip = blocks[-1] * (blocks[-1] + 1) // 2 * QB
    qh, kh, doh, delta = [], [], [], []
    for h in range(2):
        mine = head_lanes((top - start, PAIR), h)
        qh.append(jnp.where(mine, q, zero))
        kh.append(jnp.where(head_lanes((top, PAIR), h), k, zero))
        doh.append(jnp.where(mine, dob, zero))
        delta.append(jnp.sum(jnp.where(mine, prod, 0.0), axis=-1, keepdims=True))
    parts = []
    for i in blocks:
        base = i * (i + 1) // 2 * QB - skip
        ext = (i + 1) * QB
        blk = slice(i * QB - start, ext - start)
        sums = [None, None, None]
        for h in range(2):
            p = jnp.concatenate(
                [p_in[2 * pr + h, base + kb * QB : base + (kb + 1) * QB, :] for kb in range(i + 1)], axis=1)
            dp = dot(doh[h][blk], v[:ext], NT)
            ds = (p.astype(F32) * (dp - delta[h][blk])).astype(BF)
            new = [dot(ds, kh[h][:ext]), dot(qh[h][blk], ds, TN), dot(doh[h][blk], p, TN)]
            sums = [n if old is None else old + n for old, n in zip(sums, new)]
        parts.append(sums[0])
        if first and i == blocks[0]:
            dk_acc[pr], dv_acc[pr] = sums[1], sums[2]
        else:
            dk_acc[pr, :, :ext] += sums[1]
            dv_acc[pr, :, :ext] += sums[2]
    return jnp.concatenate(parts[::-1], axis=0) * 0.125


def out_grads(rows, base, off, leng, cot, wo):
    place = base + lax.broadcasted_iota(jnp.int32, (rows, wo.shape[0]), 0)
    live = (place >= off[0]) & (place < off[0] + leng[0])
    return jnp.where(live, dot(cot, wo[...], NT), 0.0)


def weight_columns(tab, w_hbm, w_in, sem):
    width = w_hbm.shape[0]
    col = lambda n: pl.multiple_of(n * width + tab[48] * (width // 2), width // 2)
    return pltpu.make_async_copy(w_hbm.at[:, pl.ds(col(0), width // 2)], w_in.at[0], sem.at[0]), \
        pltpu.make_async_copy(w_hbm.at[:, pl.ds(col(1), width // 2)], w_in.at[1], sem.at[1]), \
        pltpu.make_async_copy(w_hbm.at[:, pl.ds(col(2), width // 2)], w_in.at[2], sem.at[2])


def store_block(stage, tab, at, grad, gao):
    npos = stage.shape[0]
    rows = grad[0].shape[0] // npos
    for n in range(3):
        for i in range(npos):
            stage[tab[16 + i], at + n * rows : at + (n + 1) * rows, :] = grad[n][i * rows : (i + 1) * rows]
    at += 3 * rows
    rows = gao.shape[0] // npos
    for i in range(npos):
        for n in range(2):
            stage[tab[32 + i], at + n * rows : at + (n + 1) * rows, :] = (
                gao[i * rows : (i + 1) * rows, n * GROUP : (n + 1) * GROUP])


def send_out(stage, keep, send, sems):
    part = stage.shape[0] // 2
    copy = pltpu.make_async_copy
    wait_all(start_all([copy(stage.at[pl.ds(part, part)], send, sems.at[0]),
                        copy(stage.at[pl.ds(0, part)], keep, sems.at[1])]))


def attn_wide_kernel(tab, off, leng, cot, wo, cos_ref, low_ref, high_ref,
                     att_hbm, q_hbm, k_hbm, v_hbm, p_hbm, x_hbm, unit_hbm, ng_hbm, w_hbm, *refs):
    ng_out = refs[:-27]
    (first_out, dqkv_out, dka_out, dva_out, gao_out, sums, keep, send,
     att_in, q_in, k_in, v_in, p_in, p_hi, x_in, unit_in, ng_in, w_in, first, dqkv, dk_acc, dv_acc, dk_hi, dv_hi,
     gao, stage, sems) = refs[-27:]
    rows, width = cot.shape
    half = rows // 2
    nq = rows // QB
    pairs = GROUP // PAIR
    skip = nq // 2 * (nq // 2 + 1) // 2 * QB
    count = p_hi.shape[1]
    lo, hi, group = pl.ds(0, half), pl.ds(half, half), pl.ds(GROUP, GROUP)
    copy = pltpu.make_async_copy
    early = start_all([copy(q_hbm, q_in, sems.at[0]), copy(k_hbm, k_in, sems.at[1]),
                       copy(v_hbm, v_in, sems.at[2]), copy(att_hbm, att_in, sems.at[3])])
    loads = start_all([copy(p_hbm.at[pl.ds(2 * pr, 2)], p_in.at[pl.ds(2 * pr, 2)], sems.at[4 + pr])
                       for pr in range(pairs)])
    loads += start_all([copy(p_hbm.at[pl.ds(2 * (pairs + pr), 2), pl.ds(skip, count)], p_hi.at[pl.ds(2 * pr, 2)],
                             sems.at[4 + pairs + pr]) for pr in range(pairs)])
    at = 4 + 2 * pairs
    late = start_all([copy(x_hbm, x_in, sems.at[at]), *weight_columns(tab, w_hbm, w_in, sems.at[pl.ds(at + 1, 3)]),
                      copy(ng_hbm.at[hi], ng_in, sems.at[at + 4]), copy(unit_hbm.at[hi], unit_in, sems.at[at + 5])])
    cosine, low, high = cos_ref[...], low_ref[...], high_ref[...]
    do = out_grads(rows, 0, off, leng, cot[...], wo)
    blocks = list(reversed(range(nq)))
    wait_all(early)
    for pr in range(pairs):
        loads[pr].wait()
        cols = slice(pr * PAIR, (pr + 1) * PAIR)
        dq = pair_back(pr, blocks, do, att_in, q_in, k_in, v_in, p_in, dk_acc, dv_acc, True)
        first[0, :, cols] = turn_back(dq, cosine, low, high).astype(BF)
        first[1, :, cols] = turn_back(dk_acc[pr].T, cosine, low, high).astype(BF)
        first[2, :, cols] = dv_acc[pr].T.astype(BF)
    outs = start_all([copy(first, first_out, sems.at[0])])
    do = do[half:]
    blocks = list(reversed(range(nq // 2, nq)))
    cosine, low, high = cosine[half:], low[half:], high[half:]
    for pr in range(pairs):
        loads[pairs + pr].wait()
        cols = slice(GROUP + pr * PAIR, GROUP + (pr + 1) * PAIR)
        dq = pair_back(pr, blocks, do, att_in.at[hi], q_in.at[hi], k_in, v_in, p_hi, dk_hi, dv_hi, True, GROUP)
        dqkv[0, :, cols] = turn_back(dq, cosine, low, high).astype(BF)
        dqkv[1, :, cols] = turn_back(dk_hi[pr, :, half:].T, cosine, low, high).astype(BF)
        dqkv[2, :, cols] = dv_hi[pr, :, half:].T.astype(BF)
    outs += start_all([copy(dqkv.at[:, :, group], dqkv_out, sems.at[1]), copy(dk_hi.at[:, :, lo], dka_out, sems.at[2]),
                       copy(dv_hi.at[:, :, lo], dva_out, sems.at[3])])
    all_gao = dot(att_in[...], cot[...], TN).astype(BF)
    gao[...] = all_gao[:, width // 2 :]
    outs += start_all([copy(gao, gao_out, sems.at[4])])
    wait_all(late)
    x = x_in[...]
    store_block(stage, tab, 0, [dot(x, first[n], TN).astype(BF) for n in range(3)], all_gao[:, : width // 2])
    part = stage.shape[0] // 2
    outs += start_all([copy(stage.at[pl.ds(part, part)], send, sems.at[5]), copy(stage.at[pl.ds(0, part)], keep, sems.at[6])])
    total = ng_in[...].astype(F32)
    for n in range(3):
        total = total + dot(first[n, half:], w_in[n, :, :GROUP], NT) + dot(dqkv[n, :, GROUP:], w_in[n, :, GROUP:], NT)
    at = 0
    for to in ng_out:
        to[...] = total[at : at + to.shape[0]].astype(BF)
        at += to.shape[0]
    sums[...] = jnp.concatenate(
        gain_sums(total, unit_in[...]) + [jnp.sum(cot[...].astype(F32), axis=0, keepdims=True), jnp.zeros((5, width), F32)],
        axis=0)
    wait_all(outs)


def attn_low_kernel(tab, off, leng, cot, wo, cos_ref, low_ref, high_ref, hid_bias, sums_in,
                    att_hbm, q_hbm, k_hbm, v_hbm, p_hbm, unit_hbm, ng_hbm, w_hbm, x_hbm, first_hbm, dqkv_hbm, dka_hbm,
                    dva_hbm, gao_hbm, *refs):
    ng_out = refs[:-18]
    (keep, send, stage, att_in, q_in, k_in, v_in, p_in, unit_in, ng_in, w_in, x_in, dqkv, dqkv_hi, dk_acc, dv_acc, gao,
     sems) = refs[-18:]
    half, width = cot.shape
    nq = 2 * half // QB
    pairs = GROUP // PAIR
    count = p_in.shape[1]
    lo, group = pl.ds(0, half), pl.ds(GROUP, GROUP)
    copy = pltpu.make_async_copy
    early = start_all([copy(q_hbm.at[lo, group], q_in, sems.at[0]), copy(k_hbm.at[lo, group], k_in, sems.at[1]),
                       copy(v_hbm.at[lo, group], v_in, sems.at[2]), copy(att_hbm.at[lo, group], att_in, sems.at[3]),
                       copy(dka_hbm, dk_acc, sems.at[4]), copy(dva_hbm, dv_acc, sems.at[5])])
    loads = start_all([copy(p_hbm.at[pl.ds(4 + 2 * pr, 2), pl.ds(0, count)], p_in.at[pl.ds(2 * pr, 2)], sems.at[6 + pr])
                       for pr in range(pairs)])
    at = 6 + pairs
    late = start_all([copy(dqkv_hbm, dqkv_hi, sems.at[at]), copy(x_hbm, x_in, sems.at[at + 1]),
                      *weight_columns(tab, w_hbm, w_in, sems.at[pl.ds(at + 2, 3)]),
                      copy(ng_hbm.at[lo], ng_in, sems.at[at + 5]), copy(unit_hbm.at[lo], unit_in, sems.at[at + 6]),
                      copy(gao_hbm, gao, sems.at[at + 7]),
                      copy(first_hbm.at[:, lo], dqkv.at[:, :, pl.ds(0, GROUP)], sems.at[at + 8])])
    do = out_grads(half, 0, off, leng, cot[...], wo)
    cosine, low, high = cos_ref[...], low_ref[...], high_ref[...]
    blocks = list(reversed(range(nq // 2)))
    wait_all(early)
    for pr in range(pairs):
        loads[pr].wait()
        cols = slice(GROUP + pr * PAIR, GROUP + (pr + 1) * PAIR)
        dq = pair_back(pr, blocks, do, att_in, q_in, k_in, v_in, p_in, dk_acc, dv_acc, False)
        dqkv[0, :, cols] = turn_back(dq, cosine, low, high).astype(BF)
        dqkv[1, :, cols] = turn_back(dk_acc[pr].T, cosine, low, high).astype(BF)
        dqkv[2, :, cols] = dv_acc[pr].T.astype(BF)
    wait_all(late)
    x = x_in[...]
    grad = [(dot(x[:half], dqkv[n, :, GROUP:], TN) + dot(x[half:], dqkv_hi[n], TN)).astype(BF) for n in range(3)]
    store_block(stage, tab, 0, grad, gao[...])
    total = ng_in[...].astype(F32)
    for n in range(3):
        total = total + dot(dqkv[n], w_in[n], NT)
    at = 0
    for to in ng_out:
        to[...] = total[at : at + to.shape[0]].astype(BF)
        at += to.shape[0]
    sums = sums_in[...]
    new = gain_sums(total, unit_in[...])
    store_small(stage, stage.shape[1] - 16, tab,
                jnp.concatenate([sums[0:1] + new[0], sums[1:2] + new[1], sums[2:3]], axis=0), hid_bias[...])
    send_out(stage, keep, send, sems)


def act_kernel(tok, bias, own_low, own_high, recv_low, recv_high, out):
    cut = own_low.shape[0]
    for rows, own, recv in ((slice(0, cut), own_low, recv_low), (slice(cut, tok.shape[0]), own_high, recv_high)):
        base = tok[rows].astype(F32) + bias[...]
        out[rows] = (base + (own[...].astype(F32) + recv[...].astype(F32))).astype(BF)


def finish_kernel(unit_ref, inv, cot, ng_a, ng_b, gain, *refs):
    out = refs[-1]
    unit = unit_ref[...].astype(F32)
    scaled = (ng_a[...].astype(F32) + ng_b[...].astype(F32)) * gain[...]
    mean = jnp.mean(scaled, axis=-1, keepdims=True)
    lean = jnp.mean(scaled * unit, axis=-1, keepdims=True)
    out[...] = (cot[...].astype(F32) + inv[:, :1] * (scaled - mean - unit * lean)).astype(BF)


def const_spec(shape):
    zeros = (0,) * len(shape)
    return pl.BlockSpec(shape, lambda g, *tabs: zeros, pipeline_mode=pl.Buffered(1))


def in_hbm(value):
    return pltpu.with_memory_space_constraint(value, pltpu.HBM)


def params(limit=LIMIT):
    return pltpu.CompilerParams(vmem_limit_bytes=limit)


def rotary_tables(rows):
    lane = np.arange(PAIR) % HEAD
    half = ROT // 2
    angle = np.arange(rows)[:, None] * np.power(10000.0, (lane % half) * (-2.0 / ROT))[None, :]
    inside = (lane < ROT)[None, :]
    cosine = np.where(inside, np.cos(angle), 1.0)
    low = np.where((lane < half)[None, :], -np.sin(angle), 0.0)
    high = np.where(inside & (lane >= half)[None, :], np.sin(angle), 0.0)
    return [jnp.asarray(t, F32) for t in (cosine, low, high)]


def mlp_specs(width, npos):
    steps = npos // SPLIT
    turn_of = lambda j: (j + steps // 2) % steps
    w_in = [pl.BlockSpec((width, UNIT), lambda j, t, s=s: (0, t[turn_of(j) * SPLIT + s])) for s in range(SPLIT)]
    b_in = [pl.BlockSpec((1, UNIT), lambda j, t, s=s: (0, t[turn_of(j) * SPLIT + s])) for s in range(SPLIT)]
    w_out = [pl.BlockSpec((UNIT, width), lambda j, t, s=s: (t[turn_of(j) * SPLIT + s], 0)) for s in range(SPLIT)]
    return w_in, b_in, w_out, lambda rows: pl.BlockSpec((rows, SPLIT * UNIT), lambda j, t: (0, turn_of(j)))


def mlp_forward(tab, tokens, gain, bias, cot, w_in, b_in, w_out, npos):
    rows, width = tokens.shape
    wi, bi, wo, wide = mlp_specs(width, npos)
    steps = npos // SPLIT
    full = jax.ShapeDtypeStruct((rows, width), BF)
    part = jax.ShapeDtypeStruct((npos // 2, 2 * UNIT, 512), BF)
    block = (SPLIT, 2 * UNIT, 512)
    return pl.pallas_call(
        mlp_fwd_kernel,
        grid_spec=pltpu.PrefetchScalarGridSpec(
            num_scalar_prefetch=1,
            grid=(steps,),
            in_specs=[const_spec((rows, width)), const_spec((1, width)), const_spec((1, width)),
                      const_spec((rows, width))] + wi + bi + [pl.BlockSpec(memory_space=pl.ANY)],
            out_specs=[pl.BlockSpec(memory_space=pl.ANY)] * 3 + [wide(rows),
                       const_spec((rows, width)),
                       pl.BlockSpec(block, lambda j, t: (jnp.maximum(j - steps // 2, 0), 0, 0)),
                       pl.BlockSpec(block, lambda j, t: (jnp.minimum(j, steps // 2 - 1), 0, 0))],
            scratch_shapes=[pltpu.VMEM((rows, npos * UNIT), BF), pltpu.VMEM((npos * UNIT, width), BF),
                            pltpu.VMEM((rows, width), BF), pltpu.VMEM((rows, width), BF),
                            pltpu.VMEM((rows, PAIR), F32), pltpu.SemaphoreType.DMA((3 + npos,))],
        ),
        out_shape=[pltpu.HBM((rows, width), BF), pltpu.HBM((rows, width), BF), pltpu.HBM((rows, PAIR), F32),
                   pltpu.HBM((rows, npos * UNIT), BF), full, part, part],
        compiler_params=params(MAIN),
        cost_estimate=pl.CostEstimate(flops=20 * 10**9, bytes_accessed=10**7, transcendentals=0),
        name="mlp_forward",
    )(tab, *[in_hbm(t) for t in (tokens, gain, bias, cot)], *([in_hbm(w_in)] * SPLIT), *([in_hbm(b_in)] * SPLIT), in_hbm(w_out))


def attn_forward(tab, off, leng, normed, mlp_out, w_qkv, w_ao, tables):
    rows, width = normed.shape
    groups = width // 2 // GROUP
    tri = (rows // QB) * (rows // QB + 1) // 2 * QB
    anyspec = pl.BlockSpec(memory_space=pl.ANY)
    half = pltpu.HBM((rows, width // 2), BF)
    cols = pltpu.VMEM((rows, width // 2), BF)
    sizes = (rows * ACT_LOW // 16, rows - rows * ACT_LOW // 16)
    return pl.pallas_call(
        attn_fwd_kernel,
        grid_spec=pltpu.PrefetchScalarGridSpec(
            num_scalar_prefetch=3,
            grid=(1,),
            in_specs=[const_spec((rows, width))] + [const_spec((rows, PAIR))] * 3 + [anyspec] * 3,
            out_specs=[anyspec] * 5 + [const_spec((n, width)) for n in sizes],
            scratch_shapes=[pltpu.VMEM((groups, 3, width, GROUP), BF), pltpu.VMEM((width // 2, width), BF),
                            pltpu.VMEM((rows, width), BF), cols, cols, cols, pltpu.VMEM((HEADS // 2, tri, QB), BF), cols,
                            pltpu.SemaphoreType.DMA((3 * groups + 2 + groups * (GROUP // PAIR + 4),))],
        ),
        out_shape=[half, half, half, pltpu.HBM((HEADS // 2, tri, QB), BF), half]
        + [jax.ShapeDtypeStruct((n, width), BF) for n in sizes],
        compiler_params=params(FORWARD),
        cost_estimate=pl.CostEstimate(flops=20 * 10**9, bytes_accessed=10**7, transcendentals=0),
        name="attention_forward",
    )(tab, off, leng, in_hbm(normed), *tables, in_hbm(w_qkv), w_ao, mlp_out)


def mlp_backward(tab, normed, cot, dg, w_in, w_out, npos):
    rows, width = normed.shape
    wi, _, wo, wide = mlp_specs(width, npos)
    unit_rows = width // npos
    ublock = npos // SPLIT * unit_rows
    part = jax.ShapeDtypeStruct((npos // 2, ublock, 512), BF)
    anyspec = pl.BlockSpec(memory_space=pl.ANY)
    return pl.pallas_call(
        mlp_back_kernel,
        grid_spec=pltpu.PrefetchScalarGridSpec(
            num_scalar_prefetch=1,
            grid=(npos // SPLIT,),
            in_specs=[const_spec((rows, width)), const_spec((rows, width)),
                      wide(rows), anyspec] + wo,
            out_specs=[const_spec((1, npos * UNIT)), const_spec((rows, width)), anyspec, anyspec],
            scratch_shapes=[pltpu.VMEM((npos, ublock, 512), BF), pltpu.VMEM((rows, npos * UNIT), BF),
                            pltpu.VMEM((width, npos * UNIT), BF), pltpu.SemaphoreType.DMA((2 * npos // SPLIT + npos,))],
        ),
        out_shape=[jax.ShapeDtypeStruct((1, npos * UNIT), F32), jax.ShapeDtypeStruct((rows, width), BF), part, part],
        compiler_params=params(MAIN),
        cost_estimate=pl.CostEstimate(flops=20 * 10**9, bytes_accessed=10**7, transcendentals=0),
        name="mlp_backward",
    )(tab, normed, cot, dg, w_in, *([w_out] * SPLIT))


def back_specs(width, half_rows, place, group, count):
    row = lambda n: pl.BlockSpec((half_rows, n), lambda i, *t: (place, 0), pipeline_mode=pl.Buffered(1))
    blocks = width // 2 // GROUP // count
    out = pl.BlockSpec((GROUP * count, width), lambda i, t, o, l: (t[48] * blocks + group, 0),
                       pipeline_mode=pl.Buffered(1))
    return [row(width), out] + [row(PAIR)] * 3


def back_call(kernel, name, cost, scratch, in_specs, out_specs, out_shape):
    return pl.pallas_call(
        kernel,
        grid_spec=pltpu.PrefetchScalarGridSpec(
            num_scalar_prefetch=3, grid=(1,), in_specs=in_specs, out_specs=out_specs, scratch_shapes=scratch),
        out_shape=out_shape,
        compiler_params=params(BACK),
        cost_estimate=pl.CostEstimate(flops=cost, bytes_accessed=10**5, transcendentals=0),
        name=name,
    )


def stage_rows(width, npos):
    return 3 * (width // npos) + 2 * (width // 2 // npos)


def attn_back_wide(tab, off, leng, cot, att, q, k, v, p, unit, w_qkv, w_ao, ng, tables, normed, npos):
    rows, width = cot.shape
    half = rows // 2
    nq = rows // QB
    count = p.shape[1] - nq // 2 * (nq // 2 + 1) // 2 * QB
    pairs = GROUP // PAIR
    anyspec = pl.BlockSpec(memory_space=pl.ANY)
    sizes = [size * UNIT for at, size in NG_PARTS if at * UNIT >= half]
    ublock = stage_rows(width, npos)
    part = jax.ShapeDtypeStruct((npos // 2, ublock, GROUP), BF)
    accs = pltpu.HBM((pairs, PAIR, half), F32)
    cols = pltpu.VMEM((rows, width // 2), BF)
    acc = pltpu.VMEM((pairs, PAIR, rows), F32)
    wide = pltpu.VMEM((half, width), BF)
    return back_call(
        attn_wide_kernel, "attention_back_wide", 20 * 10**9,
        [cols, cols, cols, cols, pltpu.VMEM((GROUP // HEAD, p.shape[1], QB), BF), pltpu.VMEM((GROUP // HEAD, count, QB), BF),
         pltpu.VMEM((rows, width), BF), wide, wide, pltpu.VMEM((3, width, width // 2), BF), pltpu.VMEM((3, rows, GROUP), BF),
         pltpu.VMEM((3, half, width // 2), BF), acc, acc, acc, acc, pltpu.VMEM((width // 2, width // 2), BF),
         pltpu.VMEM((npos, ublock, GROUP), BF), pltpu.SemaphoreType.DMA((2 * pairs + 10,))],
        back_specs(width, rows, 0, 0, 2) + [anyspec] * 9,
        [const_spec((n, width)) for n in sizes] + [anyspec] * 5 + [const_spec((8, width)), anyspec, anyspec],
        [jax.ShapeDtypeStruct((n, width), BF) for n in sizes]
        + [pltpu.HBM((3, rows, GROUP), BF), pltpu.HBM((3, half, GROUP), BF), accs, accs,
           pltpu.HBM((width // 2, width // 2), BF), jax.ShapeDtypeStruct((8, width), F32), part, part],
    )(tab, off, leng, cot, w_ao, *tables, att, q, k, v, p, normed, unit, ng, w_qkv)


def attn_back_low(tab, off, leng, cot, att, q, k, v, p, unit, w_qkv, w_ao, ng, tables, normed, hid_bias, first,
                  gao, carried, npos):
    rows, width = cot.shape
    half = rows // 2
    nq = rows // QB
    count = nq // 2 * (nq // 2 + 1) // 2 * QB
    pairs = GROUP // PAIR
    anyspec = pl.BlockSpec(memory_space=pl.ANY)
    sizes = [size * UNIT for at, size in NG_PARTS if at * UNIT < half]
    ublock = stage_rows(width, npos) + 16
    part = jax.ShapeDtypeStruct((npos // 2, ublock, GROUP), BF)
    dqkv, dk_acc, dv_acc, sums = carried
    cols = pltpu.VMEM((half, GROUP), BF)
    acc = pltpu.VMEM((pairs, PAIR, half), F32)
    wide = pltpu.VMEM((half, width), BF)
    return back_call(
        attn_low_kernel, "attention_back_low", 20 * 10**9,
        [pltpu.VMEM((npos, ublock, GROUP), BF), cols, cols, cols, cols, pltpu.VMEM((GROUP // HEAD, count, QB), BF),
         wide, wide, pltpu.VMEM((3, width, width // 2), BF), pltpu.VMEM((rows, width), BF),
         pltpu.VMEM((3, half, width // 2), BF), pltpu.VMEM((3, half, GROUP), BF), acc, acc,
         pltpu.VMEM((width // 2, width // 2), BF), pltpu.SemaphoreType.DMA((pairs + 15,))],
        back_specs(width, half, 0, 1, 1) + [const_spec((1, npos * UNIT)), const_spec((8, width))]
        + [anyspec] * 14,
        [const_spec((n, width)) for n in sizes] + [anyspec, anyspec],
        [jax.ShapeDtypeStruct((n, width), BF) for n in sizes] + [part, part],
    )(tab, off, leng, cot, w_ao, *tables, hid_bias, sums, att, q, k, v, p, unit, ng, w_qkv, normed, first, dqkv,
      dk_acc, dv_acc, gao)


def act_sum(tokens, bias, own, recv):
    return pl.pallas_call(
        act_kernel,
        grid=(1,),
        in_specs=[const_spec(t.shape) for t in (tokens, bias, *own, *recv)],
        out_specs=const_spec(tokens.shape),
        out_shape=jax.ShapeDtypeStruct(tokens.shape, BF),
        compiler_params=params(),
        cost_estimate=pl.CostEstimate(flops=10**6, bytes_accessed=10**6, transcendentals=0),
        name="activations",
    )(in_hbm(tokens), bias, *[in_hbm(t) for t in (*own, *recv)])


def finish(n, unit, inv, cot, ng_a, ng_b, gain, done):
    rows, width = unit.shape
    step = UNIT
    at, count = NG_PARTS[n]
    row = pl.BlockSpec((step, width), lambda r: (at + r, 0))
    part = pl.BlockSpec((step, width), lambda r: (r, 0))
    return pl.pallas_call(
        finish_kernel,
        grid=(count,),
        in_specs=[row, pl.BlockSpec((step, PAIR), lambda r: (at + r, 0)), row, part, part,
                  pl.BlockSpec((1, width), lambda r: (0, 0))]
        + [pl.BlockSpec(memory_space=pl.ANY)] * len(done),
        out_specs=row,
        out_shape=jax.ShapeDtypeStruct((rows, width), BF),
        input_output_aliases={6: 0} if done else {},
        compiler_params=params(),
        cost_estimate=pl.CostEstimate(flops=10**7, bytes_accessed=10**6, transcendentals=0),
        name="norm_backward",
    )(*[in_hbm(t) for t in (unit, inv, cot, ng_a, ng_b)], gain, *done)


def bit_reverse(value, bits):
    out = 0
    for n in range(bits):
        out |= (value >> n & 1) << (bits - 1 - n)
    return out


NPOS = 16
ACT_LOW = 7
NG_PARTS = ((4, 2), (6, 2), (0, 2), (2, 2))


def place_tables(ndp):
    bits = NPOS.bit_length() - 1
    table = np.zeros((ndp, 2, 80), np.int32)
    for d in range(ndp):
        for b in range(2):
            for n in range(NPOS):
                if ndp == NPOS:
                    table[d, b, n] = 2 * (bit_reverse(n, bits) ^ d) + b
                    table[d, b, 64 + n] = bit_reverse(n, bits) ^ d
                    table[d, b, 16 + n] = bit_reverse(n ^ d, bits)
                    rel = 0
                    for k in range(bits - 1):
                        rel |= ((n >> (k + 1) & 1) ^ (d >> k & 1)) << (bits - 1 - k)
                    rel |= (n & 1) ^ (d >> (bits - 1) & 1)
                    table[d, b, 32 + n] = rel
                else:
                    table[d, b, n] = b * NPOS + n
                    table[d, b, 64 + n] = n
                    table[d, b, 16 + n] = n
                    table[d, b, 32 + n] = n
            table[d, b, 48] = b
    return table


def after(values, *others):
    out = lax.optimization_barrier((values,) + others)
    return out[0]


def trade(send, bit, ndp):
    return lax.ppermute(send, "dp", [(d, d ^ bit) for d in range(ndp)])


def add_halves(keep, recv):
    half = keep.shape[0] // 2
    mine = (keep[:half].astype(F32) + recv[:half].astype(F32)).astype(BF)
    other = (keep[half:].astype(F32) + recv[half:].astype(F32)).astype(BF)
    return mine, other


def add_quarters(keep, recv):
    parts = [keep[n].astype(F32) + recv[n].astype(F32) for n in range(4)]
    return parts[0], [part.astype(BF) for part in parts[1:]]


def trade_quarters(parts, ndp):
    return [trade(part, bit, ndp) for part, bit in zip(parts, (8, 4, 12))]


def add_all(mine, recvs):
    for recv in recvs:
        mine = mine + recv.astype(F32)
    return mine


def place_columns_kernel(tab, own, recv, out):
    b = tab[48]
    for n in range(NPOS):
        step, s = n // SPLIT, n % SPLIT
        col = slice(s * UNIT, (s + 1) * UNIT)
        mine = (2 * n + b) * UNIT
        theirs = (2 * n + 1 - b) * UNIT
        out[:, pl.ds(pl.multiple_of(mine, UNIT), UNIT)] = own[step, :, col].astype(F32)
        out[:, pl.ds(pl.multiple_of(theirs, UNIT), UNIT)] = recv[step, :, col].astype(F32)


def shards(ndp, tokens, offsets, lengths, cotangent, ln_gain, ln_bias, w_qkv, w_attn_out, w_in, b_in, w_out, b_out):
    rows, width = tokens.shape
    dp = lax.axis_index("dp")
    b = lax.axis_index("branch")
    hidden = w_in.shape[1]
    tables = rotary_tables(rows)
    all_tab = jnp.asarray(place_tables(ndp))
    tab = lax.dynamic_slice(all_tab, (dp, b, 0), (1, 1, 80)).reshape(80)
    gain = ln_gain.reshape(1, width)
    bias = ln_bias.reshape(1, width)
    swap = [(0, 1), (1, 0)]
    halving = ndp == NPOS

    normed, unit, inv, dg, mlp_out, a_keep, a_send = mlp_forward(
        tab, tokens, gain, bias, cotangent, w_in, b_in.reshape(1, hidden), w_out, NPOS)
    barrier = lax.optimization_barrier
    a_part = (a_keep, a_send)
    a_recv = trade(a_send, 1, ndp) if halving else a_send
    q, k, v, p, att, *act_own = attn_forward(
        tab, offsets, lengths, after(normed, a_send), mlp_out, w_qkv, w_attn_out, tables)
    a_recv, att, *act_own = barrier((a_recv, att, *act_own))
    act_recv = [lax.ppermute(part, "branch", swap) for part in act_own]
    if halving:
        a_keep, a_send = add_halves(a_keep, a_recv)
        a_recv = trade(a_send, 2, ndp)
    gb_in, ng, b_keep, b_send = mlp_backward(tab, normed, cotangent, after(dg, att, a_send), w_in, w_out, NPOS)
    b_part = (b_keep, b_send)
    a_recv, b_send, ng, act_recv[0] = barrier((a_recv, b_send, ng, act_recv[0]))
    if halving:
        b_recv = trade(b_send, 1, ndp)
        a_mine, a_send = add_quarters(a_keep, a_recv)
        a_recv = trade_quarters(a_send, ndp)
        b_keep, b_send = add_halves(b_keep, b_recv)
        b_recv = trade(b_send, 2, ndp)
    else:
        b_recv = b_send
        a_recv, a_send = [a_recv], [a_send]
    *ng_own, first, dqkv, dk_acc, dv_acc, gao, sums, c_keep, c_send = attn_back_wide(
        tab, offsets, lengths, cotangent, after(att, b_send, *a_send), q, k, v, p, unit, w_qkv, w_attn_out, ng, tables,
        normed, NPOS)
    c_part = (c_keep, c_send)
    b_recv, a_recv, act_recv[1], c_send, ng_own = barrier((b_recv, a_recv, act_recv[1], c_send, ng_own))
    ng_recv = [lax.ppermute(part, "branch", swap) for part in ng_own]
    c_recv = c_send
    if halving:
        c_recv = trade(c_send, 1, ndp)
        b_keep, b_send = add_halves(b_keep, b_recv)
        b_recv = trade(b_send, 4, ndp)
        c_recv, b_send = barrier((c_recv, b_send))
        c_keep, c_send = add_halves(c_keep, c_recv)
        c_recv = trade(c_send, 2, ndp)
    *more, d_keep, d_send = attn_back_low(
        tab, offsets, lengths, cotangent, after(att, b_send, c_send, ng_own[0]), q, k, v, p, unit, w_qkv, w_attn_out, ng,
        tables, normed, gb_in, first, gao, (dqkv, dk_acc, dv_acc, sums), NPOS)
    ng_own = ng_own + more
    if not halving:
        ng_recv = [lax.ppermute(part, "branch", swap) for part in ng_own]
        activations = act_sum(tokens, b_out.reshape(1, width), act_own, act_recv)
        input_grad = ()
        for n in range(len(NG_PARTS)):
            input_grad = (finish(n, unit, inv, cotangent, ng_own[n], ng_recv[n], gain, input_grad),)
        return (activations,) + input_grad + natural_sums(b, a_part, b_part, c_part, (d_keep, d_send), width, hidden)

    unit_rows = width // NPOS
    sub = unit_rows // 2
    steps = NPOS // SPLIT
    gao_rows = width // 2 // NPOS
    second = 3 * unit_rows + 2 * gao_rows
    total = lambda keep, recv: keep[0].astype(F32) + recv[0].astype(F32)

    def halves(parts):
        return (lax.dynamic_slice_in_dim(parts, b * sub, sub, 1),
                lax.dynamic_slice_in_dim(parts, (1 - b) * sub, sub, 1).astype(BF))

    b_recv, c_recv, ng_recv[0], d_send, *more = barrier((b_recv, c_recv, ng_recv[0], d_send, *more))
    ng_recv += [lax.ppermute(part, "branch", swap) for part in more]
    d_recv = trade(d_send, 1, ndp)
    c_keep, c_send = add_halves(c_keep, c_recv)
    c_recv = trade(c_send, 4, ndp)
    b_keep, b_send = add_halves(b_keep, b_recv)
    b_recv = trade(b_send, 8, ndp)
    d_recv, c_send, b_send = barrier((d_recv, c_send, b_send))
    d_keep, d_send = add_halves(d_keep, d_recv)
    d_recv = trade(d_send, 2, ndp)
    g_out = add_all(a_mine, after(a_recv, d_send)).reshape(2, UNIT, 512).transpose(1, 0, 2).reshape(UNIT, width)
    act_recv[0] = after(act_recv[0], g_out)
    activations = act_sum(tokens, b_out.reshape(1, width), act_own, act_recv)
    c_recv, d_recv, b_recv, ng_recv[1], activations = barrier((c_recv, d_recv, b_recv, ng_recv[1], activations))
    d_keep, d_send = add_halves(d_keep, d_recv)
    d_recv = trade(d_send, 4, ndp)
    c_keep, c_send = add_halves(c_keep, after(c_recv, d_send))
    c_recv = trade(c_send, 8, ndp)
    gi_own, gi_away = halves(total(b_keep, after(b_recv, c_send)).reshape(steps, unit_rows, 512))
    gi_recv = lax.ppermute(gi_away, "branch", swap)
    grad = finish(0, unit, inv, cotangent, ng_own[0], after(ng_recv[0], gi_away), gain, ())
    c_recv, d_recv, ng_recv[2], grad = barrier((c_recv, d_recv, ng_recv[2], grad))
    d_keep, d_send = add_halves(d_keep, d_recv)
    d_recv = trade(d_send, 8, ndp)
    gc = total(c_keep, after(c_recv, d_send))
    grad = finish(1, unit, inv, cotangent, ng_own[1], after(ng_recv[1], d_send), gain, (grad,))
    grad = finish(2, unit, inv, cotangent, ng_own[2], ng_recv[2], gain, (grad,))
    d_recv, gc, grad = barrier((d_recv, gc, grad))
    gd = total(d_keep, d_recv)
    gq = jnp.concatenate([gc[: 3 * unit_rows].reshape(3, unit_rows, GROUP), gd[: 3 * unit_rows].reshape(3, unit_rows, GROUP)],
                         axis=2)
    gq_own, gq_away = halves(gq)
    gao = jnp.concatenate([g[3 * unit_rows + n * gao_rows : 3 * unit_rows + (n + 1) * gao_rows]
                           for g in (gc, gd) for n in range(2)], axis=1)
    small = gd[second : second + 2]
    both = jnp.concatenate([gq_away, jnp.broadcast_to(small[:1].astype(BF)[None], (3, sub, GROUP))], axis=2)
    both_recv = lax.ppermute(both, "branch", swap).astype(F32)
    g_in = pl.pallas_call(
        place_columns_kernel,
        grid_spec=pltpu.PrefetchScalarGridSpec(
            num_scalar_prefetch=1, grid=(1,),
            in_specs=[const_spec((steps, sub, 512))] * 2,
            out_specs=const_spec((sub, hidden)),
        ),
        out_shape=jax.ShapeDtypeStruct((sub, hidden), F32),
        compiler_params=params(),
        name="place_columns",
    )(tab, gi_own, after(gi_recv, both))
    top = ndp // 2
    pairs = [(d * 2 + c, (d ^ top) * 2 + 1 - c) for d in range(ndp) for c in range(2) if d // top != c]
    moved = lax.ppermute(gao.astype(BF), ("dp", "branch"), pairs)
    input_grad = finish(3, unit, inv, cotangent, ng_own[3], after(ng_recv[3], both), gain, (grad,))
    g_ao = jnp.where(dp // top == b, gao, moved.astype(F32))
    recv = both_recv[:, :, : 2 * GROUP]
    first = jnp.where(b == 0, gq_own, recv)
    second_half = jnp.where(b == 0, recv, gq_own)
    g_qkv = jnp.concatenate(sum([[first[n], second_half[n]] for n in range(3)], []), axis=1)
    per = width // (2 * ndp)
    lane = dp % (UNIT // (2 * per)) * 2 * per + b * per
    row = small[0] + both_recv[0, 0, 2 * GROUP :]
    cut = lambda values, start: lax.dynamic_slice(values, (start,), (per,))
    return (activations, input_grad, cut(row, lane), cut(row, UNIT + lane), g_qkv, g_ao, g_in,
            small[1, UNIT:], g_out, cut(small[1], lane))


def natural_sums(b, a_part, b_part, c_part, d_part, width, hidden):
    axes = ("dp", "branch")
    steps = NPOS // SPLIT
    unit_rows = width // NPOS
    gao_rows = width // 2 // NPOS
    second = 3 * unit_rows + 2 * gao_rows
    wa, wb, wc, wd = [jnp.concatenate(part, axis=0).astype(F32) for part in (a_part, b_part, c_part, d_part)]
    go = wa.reshape(NPOS, 2, UNIT, 512).transpose(0, 2, 1, 3).reshape(NPOS * UNIT, width)
    gi = wb.reshape(NPOS, steps, unit_rows, 512).transpose(0, 2, 1, 3)
    gi = gi.reshape(width, hidden // 2)
    gq = jnp.concatenate([w[:, : 3 * unit_rows].reshape(NPOS, 3, unit_rows, GROUP) for w in (wc, wd)], axis=3)
    gq = gq.transpose(0, 2, 1, 3).reshape(width, 3, 2 * GROUP)
    ga = jnp.concatenate([w[:, 3 * unit_rows : second].reshape(NPOS, 2, gao_rows, GROUP) for w in (wc, wd)], axis=1)
    ga = ga.transpose(0, 2, 1, 3).reshape(NPOS * gao_rows, width)
    tiles = wd[:, second : second + 2]
    per_tile = UNIT // unit_rows

    def vector(row, lane):
        split = tiles[:, row, lane : lane + UNIT].reshape(NPOS // per_tile, per_tile, per_tile, unit_rows)
        return jnp.stack([split[:, n, n] for n in range(per_tile)], axis=1).reshape(width)

    def scatter(part, full, dim):
        starts = [0] * part.ndim
        starts[dim] = b * part.shape[dim]
        whole = lax.dynamic_update_slice(jnp.zeros(full, F32), part, starts)
        return lax.psum_scatter(whole, axes, scatter_dimension=0, tiled=True)

    total = lambda t: lax.psum_scatter(t, axes, scatter_dimension=0, tiled=True)
    g_qkv = scatter(gq, (width, 3, width), 2)
    return (
        total(vector(0, 0)),
        total(vector(0, UNIT)),
        g_qkv.reshape(g_qkv.shape[0], 3 * width),
        scatter(ga, (width, width), 0),
        scatter(gi, (width, hidden), 1),
        scatter(tiles[:, 1, UNIT:].reshape(-1), (hidden,), 0),
        scatter(go, (hidden, width), 0),
        total(jnp.where(b == 0, vector(1, 0), 0.0)),
    )


def solution(mesh):
    return jax.shard_map(
        functools.partial(shards, mesh.shape["dp"]),
        mesh=mesh,
        in_specs=(P("dp", None), P("dp"), P("dp"), P("dp", None)) + (P(),) * 8,
        out_specs=(
            P("dp", None),
            P("dp", None),
            P(("dp", "branch")),
            P(("dp", "branch")),
            P(("dp", "branch"), None),
            P(("dp", "branch"), None),
            P(("dp", "branch"), None),
            P(("dp", "branch")),
            P(("dp", "branch"), None),
            P(("dp", "branch")),
        ),
        check_vma=False,
    )
```

```python
import functools

import jax
import jax.numpy as jnp
import numpy as np
from jax import lax
from jax.experimental import pallas as pl
from jax.experimental.pallas import tpu as pltpu
from jax.sharding import PartitionSpec as P

HEADS = 16
HEAD = 64
ROT = 32
EPSILON = 1e-05
MASKED = -1e30
BF = jnp.bfloat16
F32 = jnp.float32
QB = 256
PAIR = 128
GROUP = 256
UNIT = 128
SPLIT = 4
LIMIT = 60 * 2**20
MAIN = 36 * 2**20
BACK = 40 * 2**20
FORWARD = 40 * 2**20

NN = (((1,), (0,)), ((), ()))
NT = (((1,), (1,)), ((), ()))
TN = (((0,), (0,)), ((), ()))


def dot(left, right, dims=NN):
    return lax.dot_general(left, right, dims, preferred_element_type=F32)


def norm_stats(rows):
    x = rows.astype(F32)
    mean = jnp.mean(x, axis=-1, keepdims=True)
    centred = x - mean
    inv = lax.rsqrt(jnp.mean(centred * centred, axis=-1, keepdims=True) + EPSILON)
    return centred * inv, inv


def gelu_both(u):
    c = 0.7978845608028654
    u2 = u * u
    t = jnp.tanh(u * (c + (c * 0.044715) * u2))
    half = 0.5 + 0.5 * t
    slope = u * (c + (3 * c * 0.044715) * u2)
    return u * half, half + 0.5 * slope * (1.0 - t * t)


def lanes(shape):
    return lax.broadcasted_iota(jnp.int32, shape, 1)


def head_lanes(shape, h):
    lane = lanes(shape)
    return (lane < HEAD) if h == 0 else (lane >= HEAD)


def turn(part, cosine, low, high):
    return part * cosine + pltpu.roll(part, PAIR - ROT // 2, 1) * low + pltpu.roll(part, ROT // 2, 1) * high


def turn_back(grad, cosine, low, high):
    return grad * cosine + pltpu.roll(grad * low, ROT // 2, 1) + pltpu.roll(grad * high, PAIR - ROT // 2, 1)


def start_all(copies):
    for one in copies:
        one.start()
    return copies


def wait_all(copies):
    for one in copies:
        one.wait()


def mlp_fwd_kernel(tab, *refs):
    tok, gain, bias, cot = refs[:4]
    w_in = refs[4 : 4 + SPLIT]
    b_in = refs[4 + SPLIT : 4 + 2 * SPLIT]
    w_out = refs[4 + 2 * SPLIT]
    (normed_out, unit_out, inv_out, dg_out, out_ref, keep, send, hid_all, w_all, normed, unit_in, inv_in,
     sems) = refs[5 + 2 * SPLIT :]
    j = pl.program_id(0)
    last = pl.num_programs(0) - 1

    def norm_copies():
        return [pltpu.make_async_copy(src, dst, sems.at[n])
                for n, (src, dst) in enumerate(((normed, normed_out), (unit_in, unit_out), (inv_in, inv_out)))]

    def weight_copies():
        return [pltpu.make_async_copy(w_out.at[pl.ds(pl.multiple_of(tab[n] * UNIT, UNIT), UNIT)],
                                      w_all.at[pl.ds(n * UNIT, UNIT)], sems.at[3 + n]) for n in range(w_all.shape[0] // UNIT)]

    @pl.when(j == 0)
    def _():
        start_all(weight_copies())
        for r in range(0, tok.shape[0], QB):
            unit, inv = norm_stats(tok[r : r + QB])
            unit_in[r : r + QB] = unit.astype(BF)
            inv_in[r : r + QB] = jnp.broadcast_to(inv, (QB, PAIR))
            normed[r : r + QB] = (unit * gain[...] + bias[...]).astype(BF)
        start_all(norm_copies())

    wi = jnp.concatenate([r[...] for r in w_in], axis=1)
    bi = jnp.concatenate([r[...] for r in b_in], axis=1)
    hid, dg = gelu_both(dot(normed[...], wi) + bi)
    hid = hid.astype(BF)
    dg_out[...] = dg.astype(BF)
    steps = pl.num_programs(0)
    place = (j + steps // 2) % steps * (SPLIT * UNIT)
    hid_all[:, pl.ds(pl.multiple_of(place, SPLIT * UNIT), SPLIT * UNIT)] = hid
    go = dot(hid, cot[...], TN).astype(BF)

    def store(to):
        for s in range(SPLIT):
            to[s] = go[s * UNIT : (s + 1) * UNIT]

    @pl.when(j <= last // 2)
    def _():
        store(send)

    @pl.when(j > last // 2)
    def _():
        store(keep)

    @pl.when(j == last)
    def _():
        wait_all(weight_copies())
        out_ref[...] = dot(hid_all[...], w_all[...]).astype(BF)
        wait_all(norm_copies())


def attn_fwd_kernel(tab, off, leng, x_ref, cos_ref, low_ref, high_ref, w_hbm, wo_hbm, mlp_hbm,
                    q_out, k_out, v_out, p_out, att_out, act_low, act_high,
                    w_in, wo, mlp, q_in, k_in, v_in, p_in, att_in, sems):
    rows, width = x_ref.shape
    nq = rows // QB
    pairs = GROUP // PAIR
    groups = width // 2 // GROUP
    copy = pltpu.make_async_copy
    def weight_load(g, n):
        col = pl.multiple_of(n * width + tab[48] * (width // 2) + g * GROUP, GROUP)
        return copy(w_hbm.at[:, pl.ds(col, GROUP)], w_in.at[g, n], sems.at[3 * g + n])

    start_all([weight_load(g, n) for g in range(groups) for n in range(3)])
    at = 3 * groups
    late = start_all([copy(wo_hbm.at[pl.ds(pl.multiple_of(tab[48] * (width // 2), width // 2), width // 2)], wo, sems.at[at]),
                      copy(mlp_hbm, mlp, sems.at[at + 1])])
    at += 2
    x = x_ref[...]
    start = off[0]
    stop = start + leng[0]
    place = lax.broadcasted_iota(jnp.int32, (rows, PAIR), 0)
    live = (place >= start) & (place < stop)
    kbias = jnp.where(live, 0.0, MASKED)
    live_f = jnp.where(live, 1.0, 0.0)
    lane = lanes((rows, PAIR))
    diag = lax.broadcasted_iota(jnp.int32, (QB, QB), 0) >= lax.broadcasted_iota(jnp.int32, (QB, QB), 1)
    cosine, low, high = cos_ref[...], low_ref[...], high_ref[...]
    def probs(g, pr):
        two = pl.ds(g * 2 * pairs + 2 * pr, 2)
        return copy(p_in.at[two], p_out.at[two], sems.at[at + g * (pairs + 4) + pr])

    def results(g):
        group = pl.ds(pl.multiple_of(g * GROUP, GROUP), GROUP)
        base = at + g * (pairs + 4)
        return [copy(src.at[:, group], dst.at[:, group], sems.at[base + pairs + n])
                       for n, (src, dst) in enumerate(((q_in, q_out), (k_in, k_out), (v_in, v_out), (att_in, att_out)))]

    @pl.loop(0, groups)
    def _(g):
        wait_all([weight_load(g, n) for n in range(3)])
        qa, ka, va = [dot(x, w_in[g, n]) for n in range(3)]
        for pr in range(pairs):
            cols = slice(pr * PAIR, (pr + 1) * PAIR)
            to = pl.ds(pl.multiple_of(g * GROUP + pr * PAIR, PAIR), PAIR)
            q = turn(qa[:, cols], cosine, low, high).astype(BF).astype(F32) * 0.125
            k = turn(ka[:, cols], cosine, low, high)
            v = va[:, cols]
            q_in[:, to] = q.astype(BF)
            k_in[:, to] = k.astype(BF)
            v_in[:, to] = v.astype(BF)
            qh, kh, vh = [], [], []
            for h in range(2):
                mine = head_lanes((rows, PAIR), h)
                spare = lane == (HEAD if h == 0 else 0)
                qh.append(jnp.where(mine, q, jnp.where(spare, 1.0, 0.0)).astype(BF))
                kh.append(jnp.where(mine, k, jnp.where(spare, kbias, 0.0)).astype(BF))
                vh.append(jnp.where(mine, v, 0.0).astype(BF))
            head = g * 2 * pairs + 2 * pr
            for i in range(nq):
                base = i * (i + 1) // 2 * QB
                ext = (i + 1) * QB
                mixed = None
                scores = [dot(qh[h][i * QB : ext], kh[h][:ext], NT) for h in range(2)]
                for h in range(2):
                    s = scores[h]
                    tail = jnp.where(diag, s[:, i * QB :], MASKED)
                    s = tail if i == 0 else jnp.concatenate([s[:, : i * QB], tail], axis=1)
                    e = jnp.exp(s - jnp.max(s, axis=-1, keepdims=True))
                    p = (e * (1.0 / jnp.sum(e, axis=-1, keepdims=True))).astype(BF)
                    for kb in range(i + 1):
                        p_in[head + h, base + kb * QB : base + (kb + 1) * QB, :] = p[:, kb * QB : (kb + 1) * QB]
                    part = dot(p, vh[h][:ext])
                    mixed = part if mixed is None else mixed + part
                att_in[i * QB : ext, to] = (mixed * live_f[i * QB : ext]).astype(BF)
            probs(g, pr).start()
        start_all(results(g))

    wait_all(late)
    out = mlp[...].astype(F32) + dot(att_in[...], wo[...])
    cut = act_low.shape[0]
    act_low[...] = out[:cut].astype(BF)
    act_high[...] = out[cut:].astype(BF)
    for g in range(groups):
        wait_all([probs(g, pr) for pr in range(pairs)] + results(g))


def mlp_back_kernel(tab, *refs):
    normed, cot, dg = refs[:3]
    w_in = refs[3]
    w_out = refs[4 : 4 + SPLIT]
    gb_out, ng_out, keep, send, stage, pg_all, w_all, sems = refs[4 + SPLIT :]
    j = pl.program_id(0)
    steps = pl.num_programs(0)
    npos = stage.shape[0]
    half = npos // 2
    unit_rows = normed.shape[1] // npos
    wout = jnp.concatenate([r[...] for r in w_out], axis=0)
    x, c = normed[...], cot[...]
    many = 2 * npos // SPLIT

    def weight_copies():
        return [pltpu.make_async_copy(w_in.at[:, pl.ds(pl.multiple_of(tab[n] * UNIT, UNIT), UNIT)],
                                      w_all.at[:, pl.ds(n * UNIT, UNIT)], sems.at[many + n]) for n in range(npos)]

    @pl.when(j == 0)
    def _():
        start_all(weight_copies())

    pg = dot(c, wout, NT) * dg[...].astype(F32)
    gb = jnp.sum(pg, axis=0, keepdims=True)
    pg = pg.astype(BF)
    first = (j + steps // 2) % steps * SPLIT
    pg_all[:, pl.ds(pl.multiple_of(first * UNIT, SPLIT * UNIT), SPLIT * UNIT)] = pg
    gi = dot(x, pg, TN).astype(BF)
    for s in range(SPLIT):
        place = tab[64 + first + s]
        gb_out[:, pl.ds(pl.multiple_of(place * UNIT, UNIT), UNIT)] = gb[:, s * UNIT : (s + 1) * UNIT]
        row = pl.multiple_of(place // SPLIT * unit_rows, unit_rows)
        lane = pl.multiple_of(place % SPLIT * UNIT, UNIT)
        for i in range(npos):
            stage[tab[16 + i], pl.ds(row, unit_rows), pl.ds(lane, UNIT)] = (
                gi[i * unit_rows : (i + 1) * unit_rows, s * UNIT : (s + 1) * UNIT])

    def copies(step):
        lane = tab[64 + (step + steps // 2) % steps * SPLIT] % SPLIT * UNIT
        cols = pl.ds(pl.multiple_of(lane, UNIT), UNIT)
        return [pltpu.make_async_copy(stage.at[pl.ds(half, half), :, cols], send.at[:, :, cols], sems.at[2 * step]),
                pltpu.make_async_copy(stage.at[pl.ds(0, half), :, cols], keep.at[:, :, cols], sems.at[2 * step + 1])]

    for one in copies(j):
        one.start()

    @pl.when(j == steps - 1)
    def _():
        wait_all(weight_copies())
        ng_out[...] = dot(pg_all[...], w_all[...], NT).astype(BF)
        for step in range(npos // SPLIT):
            for one in copies(step):
                one.wait()


def store_small(stage, at, tab, sums, hid_bias):
    npos = stage.shape[0]
    width = sums.shape[1]
    fill = jnp.zeros((14, 2 * UNIT), F32)
    for i in range(npos):
        tile = slice(i * width // npos // UNIT * UNIT, i * width // npos // UNIT * UNIT + UNIT)
        first = jnp.concatenate([sums[0:1, tile], sums[1:2, tile]], axis=1)
        second = jnp.concatenate([sums[2:3, tile], hid_bias[:, i * UNIT : (i + 1) * UNIT]], axis=1)
        stage[tab[16 + i], at : at + 16, :] = jnp.concatenate([first, second, fill], axis=0).astype(BF)


def gain_sums(total, unit):
    return [jnp.sum(total * unit.astype(F32), axis=0, keepdims=True), jnp.sum(total, axis=0, keepdims=True)]


def pair_back(pr, blocks, do, att, q_in, k_in, v_in, p_in, dk_acc, dv_acc, first, base_col=0):
    cols = slice(base_col + pr * PAIR, base_col + (pr + 1) * PAIR)
    top = (blocks[0] + 1) * QB
    start = blocks[-1] * QB
    q, k, v = q_in[:, cols], k_in[:, cols], v_in[:, cols]
    dob = do[:, cols].astype(BF)
    prod = dob.astype(F32) * att[:, cols].astype(F32)
    zero = jnp.zeros((), BF)
    skip = blocks[-1] * (blocks[-1] + 1) // 2 * QB
    qh, kh, doh, delta = [], [], [], []
    for h in range(2):
        mine = head_lanes((top - start, PAIR), h)
        qh.append(jnp.where(mine, q, zero))
        kh.append(jnp.where(head_lanes((top, PAIR), h), k, zero))
        doh.append(jnp.where(mine, dob, zero))
        delta.append(jnp.sum(jnp.where(mine, prod, 0.0), axis=-1, keepdims=True))
    parts = []
    for i in blocks:
        base = i * (i + 1) // 2 * QB - skip
        ext = (i + 1) * QB
        blk = slice(i * QB - start, ext - start)
        probs = [jnp.concatenate(
            [p_in[2 * pr + h, base + kb * QB : base + (kb + 1) * QB, :] for kb in range(i + 1)], axis=1) for h in range(2)]
        dps = [dot(doh[h][blk], v[:ext], NT) for h in range(2)]
        dv_new = dot(doh[0][blk], probs[0], TN) + dot(doh[1][blk], probs[1], TN)
        ds = [(probs[h].astype(F32) * (dps[h] - delta[h][blk])).astype(BF) for h in range(2)]
        sums = [dot(ds[0], kh[0][:ext]) + dot(ds[1], kh[1][:ext]),
                dot(qh[0][blk], ds[0], TN) + dot(qh[1][blk], ds[1], TN), dv_new]
        parts.append(sums[0])
        if first and i == blocks[0]:
            dk_acc[pr], dv_acc[pr] = sums[1], sums[2]
        else:
            dk_acc[pr, :, :ext] += sums[1]
            dv_acc[pr, :, :ext] += sums[2]
    return jnp.concatenate(parts[::-1], axis=0) * 0.125


def out_grads(rows, base, off, leng, cot, wo):
    place = base + lax.broadcasted_iota(jnp.int32, (rows, wo.shape[0]), 0)
    live = (place >= off[0]) & (place < off[0] + leng[0])
    return jnp.where(live, dot(cot, wo[...], NT), 0.0)


def weight_columns(tab, w_hbm, w_in, sem):
    width = w_hbm.shape[0]
    col = lambda n: pl.multiple_of(n * width + tab[48] * (width // 2), width // 2)
    return pltpu.make_async_copy(w_hbm.at[:, pl.ds(col(0), width // 2)], w_in.at[0], sem.at[0]), \
        pltpu.make_async_copy(w_hbm.at[:, pl.ds(col(1), width // 2)], w_in.at[1], sem.at[1]), \
        pltpu.make_async_copy(w_hbm.at[:, pl.ds(col(2), width // 2)], w_in.at[2], sem.at[2])


def store_block(stage, tab, at, grad, gao):
    npos = stage.shape[0]
    rows = grad[0].shape[0] // npos
    for n in range(3):
        for i in range(npos):
            stage[tab[16 + i], at + n * rows : at + (n + 1) * rows, :] = grad[n][i * rows : (i + 1) * rows]
    at += 3 * rows
    rows = gao.shape[0] // npos
    for i in range(npos):
        for n in range(2):
            stage[tab[32 + i], at + n * rows : at + (n + 1) * rows, :] = (
                gao[i * rows : (i + 1) * rows, n * GROUP : (n + 1) * GROUP])


def send_out(stage, keep, send, sems):
    part = stage.shape[0] // 2
    copy = pltpu.make_async_copy
    wait_all(start_all([copy(stage.at[pl.ds(part, part)], send, sems.at[0]),
                        copy(stage.at[pl.ds(0, part)], keep, sems.at[1])]))


def attn_wide_kernel(tab, off, leng, cot, wo, cos_ref, low_ref, high_ref,
                     att_hbm, q_hbm, k_hbm, v_hbm, p_hbm, x_hbm, unit_hbm, ng_hbm, w_hbm, *refs):
    ng_out = refs[:-27]
    (first_out, dqkv_out, dka_out, dva_out, gao_out, sums, keep, send,
     att_in, q_in, k_in, v_in, p_in, p_hi, x_in, unit_in, ng_in, w_in, first, dqkv, dk_acc, dv_acc, dk_hi, dv_hi,
     gao, stage, sems) = refs[-27:]
    rows, width = cot.shape
    half = rows // 2
    nq = rows // QB
    pairs = GROUP // PAIR
    skip = nq // 2 * (nq // 2 + 1) // 2 * QB
    count = p_hi.shape[1]
    lo, hi, group = pl.ds(0, half), pl.ds(half, half), pl.ds(GROUP, GROUP)
    copy = pltpu.make_async_copy
    early = start_all([copy(q_hbm, q_in, sems.at[0]), copy(k_hbm, k_in, sems.at[1]),
                       copy(v_hbm, v_in, sems.at[2]), copy(att_hbm, att_in, sems.at[3])])
    loads = start_all([copy(p_hbm.at[pl.ds(2 * pr, 2)], p_in.at[pl.ds(2 * pr, 2)], sems.at[4 + pr])
                       for pr in range(pairs)])
    loads += start_all([copy(p_hbm.at[pl.ds(2 * (pairs + pr), 2), pl.ds(skip, count)], p_hi.at[pl.ds(2 * pr, 2)],
                             sems.at[4 + pairs + pr]) for pr in range(pairs)])
    at = 4 + 2 * pairs
    late = start_all([copy(x_hbm, x_in, sems.at[at]), *weight_columns(tab, w_hbm, w_in, sems.at[pl.ds(at + 1, 3)]),
                      copy(ng_hbm.at[hi], ng_in, sems.at[at + 4]), copy(unit_hbm.at[hi], unit_in, sems.at[at + 5])])
    cosine, low, high = cos_ref[...], low_ref[...], high_ref[...]
    do = out_grads(rows, 0, off, leng, cot[...], wo)
    blocks = list(reversed(range(nq)))
    wait_all(early)
    for pr in range(pairs):
        loads[pr].wait()
        cols = slice(pr * PAIR, (pr + 1) * PAIR)
        dq = pair_back(pr, blocks, do, att_in, q_in, k_in, v_in, p_in, dk_acc, dv_acc, True)
        first[0, :, cols] = turn_back(dq, cosine, low, high).astype(BF)
        first[1, :, cols] = turn_back(dk_acc[pr].T, cosine, low, high).astype(BF)
        first[2, :, cols] = dv_acc[pr].T.astype(BF)
    outs = start_all([copy(first, first_out, sems.at[0])])
    do = do[half:]
    blocks = list(reversed(range(nq // 2, nq)))
    cosine, low, high = cosine[half:], low[half:], high[half:]
    for pr in range(pairs):
        loads[pairs + pr].wait()
        cols = slice(GROUP + pr * PAIR, GROUP + (pr + 1) * PAIR)
        dq = pair_back(pr, blocks, do, att_in.at[hi], q_in.at[hi], k_in, v_in, p_hi, dk_hi, dv_hi, True, GROUP)
        dqkv[0, :, cols] = turn_back(dq, cosine, low, high).astype(BF)
        dqkv[1, :, cols] = turn_back(dk_hi[pr, :, half:].T, cosine, low, high).astype(BF)
        dqkv[2, :, cols] = dv_hi[pr, :, half:].T.astype(BF)
    outs += start_all([copy(dqkv.at[:, :, group], dqkv_out, sems.at[1]), copy(dk_hi.at[:, :, lo], dka_out, sems.at[2]),
                       copy(dv_hi.at[:, :, lo], dva_out, sems.at[3])])
    all_gao = dot(att_in[...], cot[...], TN).astype(BF)
    gao[...] = all_gao[:, width // 2 :]
    outs += start_all([copy(gao, gao_out, sems.at[4])])
    wait_all(late)
    x = x_in[...]
    store_block(stage, tab, 0, [dot(x, first[n], TN).astype(BF) for n in range(3)], all_gao[:, : width // 2])
    part = stage.shape[0] // 2
    outs += start_all([copy(stage.at[pl.ds(part, part)], send, sems.at[5]), copy(stage.at[pl.ds(0, part)], keep, sems.at[6])])
    total = ng_in[...].astype(F32)
    for n in range(3):
        total = total + dot(first[n, half:], w_in[n, :, :GROUP], NT) + dot(dqkv[n, :, GROUP:], w_in[n, :, GROUP:], NT)
    at = 0
    for to in ng_out:
        to[...] = total[at : at + to.shape[0]].astype(BF)
        at += to.shape[0]
    sums[...] = jnp.concatenate(
        gain_sums(total, unit_in[...]) + [jnp.sum(cot[...].astype(F32), axis=0, keepdims=True), jnp.zeros((5, width), F32)],
        axis=0)
    wait_all(outs)


def attn_low_kernel(tab, off, leng, cot, wo, cos_ref, low_ref, high_ref, hid_bias, sums_in,
                    att_hbm, q_hbm, k_hbm, v_hbm, p_hbm, unit_hbm, ng_hbm, w_hbm, x_hbm, first_hbm, dqkv_hbm, dka_hbm,
                    dva_hbm, gao_hbm, *refs):
    ng_out = refs[:-18]
    (keep, send, stage, att_in, q_in, k_in, v_in, p_in, unit_in, ng_in, w_in, x_in, dqkv, dqkv_hi, dk_acc, dv_acc, gao,
     sems) = refs[-18:]
    half, width = cot.shape
    nq = 2 * half // QB
    pairs = GROUP // PAIR
    count = p_in.shape[1]
    lo, group = pl.ds(0, half), pl.ds(GROUP, GROUP)
    copy = pltpu.make_async_copy
    early = start_all([copy(q_hbm.at[lo, group], q_in, sems.at[0]), copy(k_hbm.at[lo, group], k_in, sems.at[1]),
                       copy(v_hbm.at[lo, group], v_in, sems.at[2]), copy(att_hbm.at[lo, group], att_in, sems.at[3]),
                       copy(dka_hbm, dk_acc, sems.at[4]), copy(dva_hbm, dv_acc, sems.at[5])])
    loads = start_all([copy(p_hbm.at[pl.ds(4 + 2 * pr, 2), pl.ds(0, count)], p_in.at[pl.ds(2 * pr, 2)], sems.at[6 + pr])
                       for pr in range(pairs)])
    at = 6 + pairs
    late = start_all([copy(dqkv_hbm, dqkv_hi, sems.at[at]), copy(x_hbm, x_in, sems.at[at + 1]),
                      *weight_columns(tab, w_hbm, w_in, sems.at[pl.ds(at + 2, 3)]),
                      copy(ng_hbm.at[lo], ng_in, sems.at[at + 5]), copy(unit_hbm.at[lo], unit_in, sems.at[at + 6]),
                      copy(gao_hbm, gao, sems.at[at + 7]),
                      copy(first_hbm.at[:, lo], dqkv.at[:, :, pl.ds(0, GROUP)], sems.at[at + 8])])
    do = out_grads(half, 0, off, leng, cot[...], wo)
    cosine, low, high = cos_ref[...], low_ref[...], high_ref[...]
    blocks = list(reversed(range(nq // 2)))
    wait_all(early)
    for pr in range(pairs):
        loads[pr].wait()
        cols = slice(GROUP + pr * PAIR, GROUP + (pr + 1) * PAIR)
        dq = pair_back(pr, blocks, do, att_in, q_in, k_in, v_in, p_in, dk_acc, dv_acc, False)
        dqkv[0, :, cols] = turn_back(dq, cosine, low, high).astype(BF)
        dqkv[1, :, cols] = turn_back(dk_acc[pr].T, cosine, low, high).astype(BF)
        dqkv[2, :, cols] = dv_acc[pr].T.astype(BF)
    wait_all(late)
    x = x_in[...]
    grad = [(dot(x[:half], dqkv[n, :, GROUP:], TN) + dot(x[half:], dqkv_hi[n], TN)).astype(BF) for n in range(3)]
    store_block(stage, tab, 0, grad, gao[...])
    total = ng_in[...].astype(F32)
    for n in range(3):
        total = total + dot(dqkv[n], w_in[n], NT)
    at = 0
    for to in ng_out:
        to[...] = total[at : at + to.shape[0]].astype(BF)
        at += to.shape[0]
    sums = sums_in[...]
    new = gain_sums(total, unit_in[...])
    store_small(stage, stage.shape[1] - 16, tab,
                jnp.concatenate([sums[0:1] + new[0], sums[1:2] + new[1], sums[2:3]], axis=0), hid_bias[...])
    send_out(stage, keep, send, sems)


def act_kernel(tok, bias, own_low, own_high, recv_low, recv_high, out):
    cut = own_low.shape[0]
    for rows, own, recv in ((slice(0, cut), own_low, recv_low), (slice(cut, tok.shape[0]), own_high, recv_high)):
        base = tok[rows].astype(F32) + bias[...]
        out[rows] = (base + (own[...].astype(F32) + recv[...].astype(F32))).astype(BF)


def finish_kernel(counts, unit_ref, inv, cot, gain, *refs):
    out = refs[-1]
    unit = unit_ref[...].astype(F32)
    start = 0
    for n, count in enumerate(counts):
        own, recv = refs[2 * n], refs[2 * n + 1]

        @pl.when((pl.program_id(0) >= start) & (pl.program_id(0) < start + count))
        def _():
            scaled = (own[...].astype(F32) + recv[...].astype(F32)) * gain[...]
            mean = jnp.mean(scaled, axis=-1, keepdims=True)
            lean = jnp.mean(scaled * unit, axis=-1, keepdims=True)
            out[...] = (cot[...].astype(F32) + inv[:, :1] * (scaled - mean - unit * lean)).astype(BF)

        start += count


def const_spec(shape):
    zeros = (0,) * len(shape)
    return pl.BlockSpec(shape, lambda g, *tabs: zeros, pipeline_mode=pl.Buffered(1))


def in_hbm(value):
    return pltpu.with_memory_space_constraint(value, pltpu.HBM)


def params(limit=LIMIT):
    return pltpu.CompilerParams(vmem_limit_bytes=limit)


def rotary_tables(rows):
    lane = np.arange(PAIR) % HEAD
    half = ROT // 2
    angle = np.arange(rows)[:, None] * np.power(10000.0, (lane % half) * (-2.0 / ROT))[None, :]
    inside = (lane < ROT)[None, :]
    cosine = np.where(inside, np.cos(angle), 1.0)
    low = np.where((lane < half)[None, :], -np.sin(angle), 0.0)
    high = np.where(inside & (lane >= half)[None, :], np.sin(angle), 0.0)
    return [jnp.asarray(t, F32) for t in (cosine, low, high)]


def mlp_specs(width, npos):
    steps = npos // SPLIT
    turn_of = lambda j: (j + steps // 2) % steps
    w_in = [pl.BlockSpec((width, UNIT), lambda j, t, s=s: (0, t[turn_of(j) * SPLIT + s])) for s in range(SPLIT)]
    b_in = [pl.BlockSpec((1, UNIT), lambda j, t, s=s: (0, t[turn_of(j) * SPLIT + s])) for s in range(SPLIT)]
    w_out = [pl.BlockSpec((UNIT, width), lambda j, t, s=s: (t[turn_of(j) * SPLIT + s], 0)) for s in range(SPLIT)]
    return w_in, b_in, w_out, lambda rows: pl.BlockSpec((rows, SPLIT * UNIT), lambda j, t: (0, turn_of(j)))


def mlp_forward(tab, tokens, gain, bias, cot, w_in, b_in, w_out, npos):
    rows, width = tokens.shape
    wi, bi, wo, wide = mlp_specs(width, npos)
    steps = npos // SPLIT
    full = jax.ShapeDtypeStruct((rows, width), BF)
    part = jax.ShapeDtypeStruct((npos // 2, UNIT, width), BF)
    block = (SPLIT, UNIT, width)
    return pl.pallas_call(
        mlp_fwd_kernel,
        grid_spec=pltpu.PrefetchScalarGridSpec(
            num_scalar_prefetch=1,
            grid=(steps,),
            in_specs=[const_spec((rows, width)), const_spec((1, width)), const_spec((1, width)),
                      const_spec((rows, width))] + wi + bi + [pl.BlockSpec(memory_space=pl.ANY)],
            out_specs=[pl.BlockSpec(memory_space=pl.ANY)] * 3 + [wide(rows),
                       const_spec((rows, width)),
                       pl.BlockSpec(block, lambda j, t: (jnp.maximum(j - steps // 2, 0), 0, 0)),
                       pl.BlockSpec(block, lambda j, t: (jnp.minimum(j, steps // 2 - 1), 0, 0))],
            scratch_shapes=[pltpu.VMEM((rows, npos * UNIT), BF), pltpu.VMEM((npos * UNIT, width), BF),
                            pltpu.VMEM((rows, width), BF), pltpu.VMEM((rows, width), BF),
                            pltpu.VMEM((rows, PAIR), F32), pltpu.SemaphoreType.DMA((3 + npos,))],
        ),
        out_shape=[pltpu.HBM((rows, width), BF), pltpu.HBM((rows, width), BF), pltpu.HBM((rows, PAIR), F32),
                   pltpu.HBM((rows, npos * UNIT), BF), full, part, part],
        compiler_params=params(MAIN),
        cost_estimate=pl.CostEstimate(flops=20 * 10**9, bytes_accessed=10**7, transcendentals=0),
        name="mlp_forward",
    )(tab, *[in_hbm(t) for t in (tokens, gain, bias, cot)], *([in_hbm(w_in)] * SPLIT), *([in_hbm(b_in)] * SPLIT), in_hbm(w_out))


def attn_forward(tab, off, leng, normed, mlp_out, w_qkv, w_ao, tables):
    rows, width = normed.shape
    groups = width // 2 // GROUP
    tri = (rows // QB) * (rows // QB + 1) // 2 * QB
    anyspec = pl.BlockSpec(memory_space=pl.ANY)
    half = pltpu.HBM((rows, width // 2), BF)
    cols = pltpu.VMEM((rows, width // 2), BF)
    sizes = (rows * ACT_LOW // 16, rows - rows * ACT_LOW // 16)
    return pl.pallas_call(
        attn_fwd_kernel,
        grid_spec=pltpu.PrefetchScalarGridSpec(
            num_scalar_prefetch=3,
            grid=(1,),
            in_specs=[const_spec((rows, width))] + [const_spec((rows, PAIR))] * 3 + [anyspec] * 3,
            out_specs=[anyspec] * 5 + [const_spec((n, width)) for n in sizes],
            scratch_shapes=[pltpu.VMEM((groups, 3, width, GROUP), BF), pltpu.VMEM((width // 2, width), BF),
                            pltpu.VMEM((rows, width), BF), cols, cols, cols, pltpu.VMEM((HEADS // 2, tri, QB), BF), cols,
                            pltpu.SemaphoreType.DMA((3 * groups + 2 + groups * (GROUP // PAIR + 4),))],
        ),
        out_shape=[half, half, half, pltpu.HBM((HEADS // 2, tri, QB), BF), half]
        + [jax.ShapeDtypeStruct((n, width), BF) for n in sizes],
        compiler_params=params(FORWARD),
        cost_estimate=pl.CostEstimate(flops=20 * 10**9, bytes_accessed=10**7, transcendentals=0),
        name="attention_forward",
    )(tab, off, leng, in_hbm(normed), *tables, in_hbm(w_qkv), w_ao, mlp_out)


def mlp_backward(tab, normed, cot, dg, w_in, w_out, npos):
    rows, width = normed.shape
    wi, _, wo, wide = mlp_specs(width, npos)
    unit_rows = width // npos
    ublock = npos // SPLIT * unit_rows
    part = jax.ShapeDtypeStruct((npos // 2, ublock, 512), BF)
    anyspec = pl.BlockSpec(memory_space=pl.ANY)
    return pl.pallas_call(
        mlp_back_kernel,
        grid_spec=pltpu.PrefetchScalarGridSpec(
            num_scalar_prefetch=1,
            grid=(npos // SPLIT,),
            in_specs=[const_spec((rows, width)), const_spec((rows, width)),
                      wide(rows), anyspec] + wo,
            out_specs=[const_spec((1, npos * UNIT)), const_spec((rows, width)), anyspec, anyspec],
            scratch_shapes=[pltpu.VMEM((npos, ublock, 512), BF), pltpu.VMEM((rows, npos * UNIT), BF),
                            pltpu.VMEM((width, npos * UNIT), BF), pltpu.SemaphoreType.DMA((2 * npos // SPLIT + npos,))],
        ),
        out_shape=[jax.ShapeDtypeStruct((1, npos * UNIT), F32), jax.ShapeDtypeStruct((rows, width), BF), part, part],
        compiler_params=params(MAIN),
        cost_estimate=pl.CostEstimate(flops=20 * 10**9, bytes_accessed=10**7, transcendentals=0),
        name="mlp_backward",
    )(tab, normed, cot, dg, w_in, *([w_out] * SPLIT))


def back_specs(width, half_rows, place, group, count):
    row = lambda n: pl.BlockSpec((half_rows, n), lambda i, *t: (place, 0), pipeline_mode=pl.Buffered(1))
    blocks = width // 2 // GROUP // count
    out = pl.BlockSpec((GROUP * count, width), lambda i, t, o, l: (t[48] * blocks + group, 0),
                       pipeline_mode=pl.Buffered(1))
    return [row(width), out] + [row(PAIR)] * 3


def back_call(kernel, name, cost, scratch, in_specs, out_specs, out_shape):
    return pl.pallas_call(
        kernel,
        grid_spec=pltpu.PrefetchScalarGridSpec(
            num_scalar_prefetch=3, grid=(1,), in_specs=in_specs, out_specs=out_specs, scratch_shapes=scratch),
        out_shape=out_shape,
        compiler_params=params(BACK),
        cost_estimate=pl.CostEstimate(flops=cost, bytes_accessed=10**5, transcendentals=0),
        name=name,
    )


def stage_rows(width, npos):
    return 3 * (width // npos) + 2 * (width // 2 // npos)


def attn_back_wide(tab, off, leng, cot, att, q, k, v, p, unit, w_qkv, w_ao, ng, tables, normed, npos):
    rows, width = cot.shape
    half = rows // 2
    nq = rows // QB
    count = p.shape[1] - nq // 2 * (nq // 2 + 1) // 2 * QB
    pairs = GROUP // PAIR
    anyspec = pl.BlockSpec(memory_space=pl.ANY)
    sizes = [size * UNIT for at, size in NG_PARTS if at * UNIT >= half]
    ublock = stage_rows(width, npos)
    part = jax.ShapeDtypeStruct((npos // 2, ublock, GROUP), BF)
    accs = pltpu.HBM((pairs, PAIR, half), F32)
    cols = pltpu.VMEM((rows, width // 2), BF)
    acc = pltpu.VMEM((pairs, PAIR, rows), F32)
    wide = pltpu.VMEM((half, width), BF)
    return back_call(
        attn_wide_kernel, "attention_back_wide", 20 * 10**9,
        [cols, cols, cols, cols, pltpu.VMEM((GROUP // HEAD, p.shape[1], QB), BF), pltpu.VMEM((GROUP // HEAD, count, QB), BF),
         pltpu.VMEM((rows, width), BF), wide, wide, pltpu.VMEM((3, width, width // 2), BF), pltpu.VMEM((3, rows, GROUP), BF),
         pltpu.VMEM((3, half, width // 2), BF), acc, acc, acc, acc, pltpu.VMEM((width // 2, width // 2), BF),
         pltpu.VMEM((npos, ublock, GROUP), BF), pltpu.SemaphoreType.DMA((2 * pairs + 10,))],
        back_specs(width, rows, 0, 0, 2) + [anyspec] * 9,
        [const_spec((n, width)) for n in sizes] + [anyspec] * 5 + [const_spec((8, width)), anyspec, anyspec],
        [jax.ShapeDtypeStruct((n, width), BF) for n in sizes]
        + [pltpu.HBM((3, rows, GROUP), BF), pltpu.HBM((3, half, GROUP), BF), accs, accs,
           pltpu.HBM((width // 2, width // 2), BF), jax.ShapeDtypeStruct((8, width), F32), part, part],
    )(tab, off, leng, cot, w_ao, *tables, att, q, k, v, p, normed, unit, ng, w_qkv)


def attn_back_low(tab, off, leng, cot, att, q, k, v, p, unit, w_qkv, w_ao, ng, tables, normed, hid_bias, first,
                  gao, carried, npos):
    rows, width = cot.shape
    half = rows // 2
    nq = rows // QB
    count = nq // 2 * (nq // 2 + 1) // 2 * QB
    pairs = GROUP // PAIR
    anyspec = pl.BlockSpec(memory_space=pl.ANY)
    sizes = [size * UNIT for at, size in NG_PARTS if at * UNIT < half]
    ublock = stage_rows(width, npos) + 16
    part = jax.ShapeDtypeStruct((npos // 2, ublock, GROUP), BF)
    dqkv, dk_acc, dv_acc, sums = carried
    cols = pltpu.VMEM((half, GROUP), BF)
    acc = pltpu.VMEM((pairs, PAIR, half), F32)
    wide = pltpu.VMEM((half, width), BF)
    return back_call(
        attn_low_kernel, "attention_back_low", 20 * 10**9,
        [pltpu.VMEM((npos, ublock, GROUP), BF), cols, cols, cols, cols, pltpu.VMEM((GROUP // HEAD, count, QB), BF),
         wide, wide, pltpu.VMEM((3, width, width // 2), BF), pltpu.VMEM((rows, width), BF),
         pltpu.VMEM((3, half, width // 2), BF), pltpu.VMEM((3, half, GROUP), BF), acc, acc,
         pltpu.VMEM((width // 2, width // 2), BF), pltpu.SemaphoreType.DMA((pairs + 15,))],
        back_specs(width, half, 0, 1, 1) + [const_spec((1, npos * UNIT)), const_spec((8, width))]
        + [anyspec] * 14,
        [const_spec((n, width)) for n in sizes] + [anyspec, anyspec],
        [jax.ShapeDtypeStruct((n, width), BF) for n in sizes] + [part, part],
    )(tab, off, leng, cot, w_ao, *tables, hid_bias, sums, att, q, k, v, p, unit, ng, w_qkv, normed, first, dqkv,
      dk_acc, dv_acc, gao)


def act_sum(tokens, bias, own, recv):
    return pl.pallas_call(
        act_kernel,
        grid=(1,),
        in_specs=[const_spec(t.shape) for t in (tokens, bias, *own, *recv)],
        out_specs=const_spec(tokens.shape),
        out_shape=jax.ShapeDtypeStruct(tokens.shape, BF),
        compiler_params=params(),
        cost_estimate=pl.CostEstimate(flops=10**6, bytes_accessed=10**6, transcendentals=0),
        name="activations",
    )(in_hbm(tokens), bias, *[in_hbm(t) for t in (*own, *recv)])


def finish(pieces, unit, inv, cot, parts, gain, done):
    rows, width = unit.shape
    counts = [NG_PARTS[n][1] for n in pieces]

    def place(r):
        at, start = NG_PARTS[pieces[0]][0] + r, counts[0]
        for n, count in zip(pieces[1:], counts[1:]):
            at = jnp.where(r >= start, NG_PARTS[n][0] + r - start, at)
            start += count
        return at

    row = pl.BlockSpec((UNIT, width), lambda r: (place(r), 0))
    specs, start = [], 0
    for count in counts:
        specs += [pl.BlockSpec((UNIT, width), lambda r, lo=start, top=count - 1: (jnp.clip(r - lo, 0, top), 0))] * 2
        start += count
    return pl.pallas_call(
        functools.partial(finish_kernel, counts),
        grid=(start,),
        in_specs=[row, pl.BlockSpec((UNIT, PAIR), lambda r: (place(r), 0)), row, pl.BlockSpec((1, width), lambda r: (0, 0))]
        + specs + [pl.BlockSpec(memory_space=pl.ANY)] * len(done),
        out_specs=row,
        out_shape=jax.ShapeDtypeStruct((rows, width), BF),
        input_output_aliases={4 + 2 * len(pieces): 0} if done else {},
        compiler_params=params(),
        cost_estimate=pl.CostEstimate(flops=10**7, bytes_accessed=10**6, transcendentals=0),
        name="norm_backward",
    )(*[in_hbm(t) for t in (unit, inv, cot)], gain, *[in_hbm(t) for pair in parts for t in pair], *done)


def bit_reverse(value, bits):
    out = 0
    for n in range(bits):
        out |= (value >> n & 1) << (bits - 1 - n)
    return out


NPOS = 16
ACT_LOW = 7
NG_PARTS = ((4, 2), (6, 2), (0, 2), (2, 2))


def place_tables(ndp):
    bits = NPOS.bit_length() - 1
    table = np.zeros((ndp, 2, 80), np.int32)
    for d in range(ndp):
        for b in range(2):
            for n in range(NPOS):
                if ndp == NPOS:
                    table[d, b, n] = 2 * (bit_reverse(n, bits) ^ d) + b
                    table[d, b, 64 + n] = bit_reverse(n, bits) ^ d
                    table[d, b, 16 + n] = bit_reverse(n ^ d, bits)
                    rel = 0
                    for k in range(bits - 1):
                        rel |= ((n >> (k + 1) & 1) ^ (d >> k & 1)) << (bits - 1 - k)
                    rel |= (n & 1) ^ (d >> (bits - 1) & 1)
                    table[d, b, 32 + n] = rel
                else:
                    table[d, b, n] = b * NPOS + n
                    table[d, b, 64 + n] = n
                    table[d, b, 16 + n] = n
                    table[d, b, 32 + n] = n
            table[d, b, 48] = b
    return table


def after(values, *others):
    out = lax.optimization_barrier((values,) + others)
    return out[0]


def trade(send, bit, ndp):
    return lax.ppermute(send, "dp", [(d, d ^ bit) for d in range(ndp)])


def add_halves(keep, recv):
    half = keep.shape[0] // 2
    mine = (keep[:half].astype(F32) + recv[:half].astype(F32)).astype(BF)
    other = (keep[half:].astype(F32) + recv[half:].astype(F32)).astype(BF)
    return mine, other


def add_quarters(keep, recv):
    parts = [keep[n].astype(F32) + recv[n].astype(F32) for n in range(4)]
    return parts[0], [part.astype(BF) for part in parts[1:]]


def trade_quarters(parts, ndp):
    return [trade(part, bit, ndp) for part, bit in zip(parts, (8, 4, 12))]


def add_all(mine, recvs):
    for recv in recvs:
        mine = mine + recv.astype(F32)
    return mine


def place_columns_kernel(tab, own, recv, out):
    b = tab[48]
    for n in range(NPOS):
        step, s = n // SPLIT, n % SPLIT
        col = slice(s * UNIT, (s + 1) * UNIT)
        mine = (2 * n + b) * UNIT
        theirs = (2 * n + 1 - b) * UNIT
        out[:, pl.ds(pl.multiple_of(mine, UNIT), UNIT)] = own[step, :, col].astype(F32)
        out[:, pl.ds(pl.multiple_of(theirs, UNIT), UNIT)] = recv[step, :, col].astype(F32)


def shards(ndp, tokens, offsets, lengths, cotangent, ln_gain, ln_bias, w_qkv, w_attn_out, w_in, b_in, w_out, b_out):
    rows, width = tokens.shape
    dp = lax.axis_index("dp")
    b = lax.axis_index("branch")
    hidden = w_in.shape[1]
    tables = rotary_tables(rows)
    all_tab = jnp.asarray(place_tables(ndp))
    tab = lax.dynamic_slice(all_tab, (dp, b, 0), (1, 1, 80)).reshape(80)
    gain = ln_gain.reshape(1, width)
    bias = ln_bias.reshape(1, width)
    swap = [(0, 1), (1, 0)]
    halving = ndp == NPOS

    normed, unit, inv, dg, mlp_out, a_keep, a_send = mlp_forward(
        tab, tokens, gain, bias, cotangent, w_in, b_in.reshape(1, hidden), w_out, NPOS)
    barrier = lax.optimization_barrier
    a_part = (a_keep, a_send)
    a_recv = trade(a_send, 1, ndp) if halving else a_send
    q, k, v, p, att, *act_own = attn_forward(
        tab, offsets, lengths, after(normed, a_send), mlp_out, w_qkv, w_attn_out, tables)
    a_recv, att, *act_own = barrier((a_recv, att, *act_own))
    act_recv = [lax.ppermute(part, "branch", swap) for part in act_own]
    if halving:
        a_keep, a_send = add_halves(a_keep, a_recv)
        a_recv = trade(a_send, 2, ndp)
    gb_in, ng, b_keep, b_send = mlp_backward(tab, normed, cotangent, after(dg, att, a_send), w_in, w_out, NPOS)
    b_part = (b_keep, b_send)
    a_recv, b_send, ng, act_recv[0] = barrier((a_recv, b_send, ng, act_recv[0]))
    if halving:
        b_recv = trade(b_send, 1, ndp)
        a_mine, a_send = add_quarters(a_keep, a_recv)
        a_recv = trade_quarters(a_send, ndp)
        b_keep, b_send = add_halves(b_keep, b_recv)
        b_recv = trade(b_send, 2, ndp)
    else:
        b_recv = b_send
        a_recv, a_send = [a_recv], [a_send]
    *ng_own, first, dqkv, dk_acc, dv_acc, gao, sums, c_keep, c_send = attn_back_wide(
        tab, offsets, lengths, cotangent, after(att, b_send, *a_send), q, k, v, p, unit, w_qkv, w_attn_out, ng, tables,
        normed, NPOS)
    c_part = (c_keep, c_send)
    b_recv, a_recv, act_recv[1], c_send, ng_own = barrier((b_recv, a_recv, act_recv[1], c_send, ng_own))
    ng_recv = [lax.ppermute(part, "branch", swap) for part in ng_own]
    c_recv = c_send
    if halving:
        c_recv = trade(c_send, 1, ndp)
        b_keep, b_send = add_halves(b_keep, b_recv)
        b_recv = trade(b_send, 4, ndp)
        c_recv, b_send = barrier((c_recv, b_send))
        c_keep, c_send = add_halves(c_keep, c_recv)
        c_recv = trade(c_send, 2, ndp)
    *more, d_keep, d_send = attn_back_low(
        tab, offsets, lengths, cotangent, after(att, b_send, c_send, ng_own[0]), q, k, v, p, unit, w_qkv, w_attn_out, ng,
        tables, normed, gb_in, first, gao, (dqkv, dk_acc, dv_acc, sums), NPOS)
    ng_own = ng_own + more
    if not halving:
        ng_recv = [lax.ppermute(part, "branch", swap) for part in ng_own]
        activations = act_sum(tokens, b_out.reshape(1, width), act_own, act_recv)
        input_grad = ()
        for n in range(len(NG_PARTS)):
            input_grad = (finish([n], unit, inv, cotangent, [(ng_own[n], ng_recv[n])], gain, input_grad),)
        return (activations,) + input_grad + natural_sums(b, a_part, b_part, c_part, (d_keep, d_send), width, hidden)

    unit_rows = width // NPOS
    sub = unit_rows // 2
    steps = NPOS // SPLIT
    gao_rows = width // 2 // NPOS
    second = 3 * unit_rows + 2 * gao_rows
    total = lambda keep, recv: keep[0].astype(F32) + recv[0].astype(F32)

    def halves(parts):
        return (lax.dynamic_slice_in_dim(parts, b * sub, sub, 1),
                lax.dynamic_slice_in_dim(parts, (1 - b) * sub, sub, 1).astype(BF))

    b_recv, c_recv, ng_recv[0], d_send, *more = barrier((b_recv, c_recv, ng_recv[0], d_send, *more))
    ng_recv += [lax.ppermute(part, "branch", swap) for part in more]
    d_recv = trade(d_send, 1, ndp)
    c_keep, c_send = add_halves(c_keep, c_recv)
    c_recv = trade(c_send, 4, ndp)
    b_keep, b_send = add_halves(b_keep, b_recv)
    b_recv = trade(b_send, 8, ndp)
    d_recv, c_send, b_send = barrier((d_recv, c_send, b_send))
    d_keep, d_send = add_halves(d_keep, d_recv)
    d_recv = trade(d_send, 2, ndp)
    g_out = add_all(a_mine, after(a_recv, d_send))
    act_recv[0] = after(act_recv[0], g_out)
    activations = act_sum(tokens, b_out.reshape(1, width), act_own, act_recv)
    c_recv, d_recv, b_recv, ng_recv[1], activations = barrier((c_recv, d_recv, b_recv, ng_recv[1], activations))
    d_keep, d_send = add_halves(d_keep, d_recv)
    d_recv = trade(d_send, 4, ndp)
    c_keep, c_send = add_halves(c_keep, after(c_recv, d_send))
    c_recv = trade(c_send, 8, ndp)
    gi_own, gi_away = halves(total(b_keep, after(b_recv, c_send)).reshape(steps, unit_rows, 512))
    gi_recv = lax.ppermute(gi_away, "branch", swap)
    grad = finish([0], unit, inv, cotangent, [(ng_own[0], after(ng_recv[0], gi_away))], gain, ())
    c_recv, d_recv, ng_recv[2], grad = barrier((c_recv, d_recv, ng_recv[2], grad))
    d_keep, d_send = add_halves(d_keep, d_recv)
    d_recv = trade(d_send, 8, ndp)
    gc = total(c_keep, after(c_recv, d_send))
    grad = finish([1, 2], unit, inv, cotangent, [(ng_own[1], after(ng_recv[1], d_send)), (ng_own[2], ng_recv[2])], gain,
                  (grad,))
    d_recv, gc, grad = barrier((d_recv, gc, grad))
    gd = total(d_keep, d_recv)
    gq = jnp.concatenate([gc[: 3 * unit_rows].reshape(3, unit_rows, GROUP), gd[: 3 * unit_rows].reshape(3, unit_rows, GROUP)],
                         axis=2)
    gq_own, gq_away = halves(gq)
    gao = jnp.concatenate([g[3 * unit_rows + n * gao_rows : 3 * unit_rows + (n + 1) * gao_rows]
                           for g in (gc, gd) for n in range(2)], axis=1)
    small = gd[second : second + 2]
    both = jnp.concatenate([gq_away, jnp.broadcast_to(small[:1].astype(BF)[None], (3, sub, GROUP))], axis=2)
    both_recv = lax.ppermute(both, "branch", swap).astype(F32)
    g_in = pl.pallas_call(
        place_columns_kernel,
        grid_spec=pltpu.PrefetchScalarGridSpec(
            num_scalar_prefetch=1, grid=(1,),
            in_specs=[const_spec((steps, sub, 512))] * 2,
            out_specs=const_spec((sub, hidden)),
        ),
        out_shape=jax.ShapeDtypeStruct((sub, hidden), F32),
        compiler_params=params(),
        name="place_columns",
    )(tab, gi_own, after(gi_recv, both))
    top = ndp // 2
    pairs = [(d * 2 + c, (d ^ top) * 2 + 1 - c) for d in range(ndp) for c in range(2) if d // top != c]
    moved = lax.ppermute(gao.astype(BF), ("dp", "branch"), pairs)
    input_grad = finish([3], unit, inv, cotangent, [(ng_own[3], after(ng_recv[3], both))], gain, (grad,))
    g_ao = jnp.where(dp // top == b, gao, moved.astype(F32))
    recv = both_recv[:, :, : 2 * GROUP]
    first = jnp.where(b == 0, gq_own, recv)
    second_half = jnp.where(b == 0, recv, gq_own)
    g_qkv = jnp.concatenate(sum([[first[n], second_half[n]] for n in range(3)], []), axis=1)
    per = width // (2 * ndp)
    lane = dp % (UNIT // (2 * per)) * 2 * per + b * per
    row = small[0] + both_recv[0, 0, 2 * GROUP :]
    cut = lambda values, start: lax.dynamic_slice(values, (start,), (per,))
    return (activations, input_grad, cut(row, lane), cut(row, UNIT + lane), g_qkv, g_ao, g_in,
            small[1, UNIT:], g_out, cut(small[1], lane))


def natural_sums(b, a_part, b_part, c_part, d_part, width, hidden):
    axes = ("dp", "branch")
    steps = NPOS // SPLIT
    unit_rows = width // NPOS
    gao_rows = width // 2 // NPOS
    second = 3 * unit_rows + 2 * gao_rows
    wa, wb, wc, wd = [jnp.concatenate(part, axis=0).astype(F32) for part in (a_part, b_part, c_part, d_part)]
    go = wa.reshape(NPOS * UNIT, width)
    gi = wb.reshape(NPOS, steps, unit_rows, 512).transpose(0, 2, 1, 3)
    gi = gi.reshape(width, hidden // 2)
    gq = jnp.concatenate([w[:, : 3 * unit_rows].reshape(NPOS, 3, unit_rows, GROUP) for w in (wc, wd)], axis=3)
    gq = gq.transpose(0, 2, 1, 3).reshape(width, 3, 2 * GROUP)
    ga = jnp.concatenate([w[:, 3 * unit_rows : second].reshape(NPOS, 2, gao_rows, GROUP) for w in (wc, wd)], axis=1)
    ga = ga.transpose(0, 2, 1, 3).reshape(NPOS * gao_rows, width)
    tiles = wd[:, second : second + 2]
    per_tile = UNIT // unit_rows

    def vector(row, lane):
        split = tiles[:, row, lane : lane + UNIT].reshape(NPOS // per_tile, per_tile, per_tile, unit_rows)
        return jnp.stack([split[:, n, n] for n in range(per_tile)], axis=1).reshape(width)

    def scatter(part, full, dim):
        starts = [0] * part.ndim
        starts[dim] = b * part.shape[dim]
        whole = lax.dynamic_update_slice(jnp.zeros(full, F32), part, starts)
        return lax.psum_scatter(whole, axes, scatter_dimension=0, tiled=True)

    total = lambda t: lax.psum_scatter(t, axes, scatter_dimension=0, tiled=True)
    g_qkv = scatter(gq, (width, 3, width), 2)
    return (
        total(vector(0, 0)),
        total(vector(0, UNIT)),
        g_qkv.reshape(g_qkv.shape[0], 3 * width),
        scatter(ga, (width, width), 0),
        scatter(gi, (width, hidden), 1),
        scatter(tiles[:, 1, UNIT:].reshape(-1), (hidden,), 0),
        scatter(go, (hidden, width), 0),
        total(jnp.where(b == 0, vector(1, 0), 0.0)),
    )


def solution(mesh):
    return jax.shard_map(
        functools.partial(shards, mesh.shape["dp"]),
        mesh=mesh,
        in_specs=(P("dp", None), P("dp"), P("dp"), P("dp", None)) + (P(),) * 8,
        out_specs=(
            P("dp", None),
            P("dp", None),
            P(("dp", "branch")),
            P(("dp", "branch")),
            P(("dp", "branch"), None),
            P(("dp", "branch"), None),
            P(("dp", "branch"), None),
            P(("dp", "branch")),
            P(("dp", "branch"), None),
            P(("dp", "branch")),
        ),
        check_vma=False,
    )
```

```python
import functools

import jax
import jax.numpy as jnp
import numpy as np
from jax import lax
from jax.experimental import pallas as pl
from jax.experimental.pallas import tpu as pltpu
from jax.sharding import PartitionSpec as P

HEADS = 16
HEAD = 64
ROT = 32
EPSILON = 1e-05
MASKED = -1e30
BF = jnp.bfloat16
F32 = jnp.float32
QB = 256
PAIR = 128
GROUP = 256
UNIT = 128
SPLIT = 4
LIMIT = 60 * 2**20
MAIN = 36 * 2**20
BACK = 40 * 2**20
FORWARD = 40 * 2**20

NN = (((1,), (0,)), ((), ()))
NT = (((1,), (1,)), ((), ()))
TN = (((0,), (0,)), ((), ()))


def dot(left, right, dims=NN):
    return lax.dot_general(left, right, dims, preferred_element_type=F32)


def norm_stats(rows):
    x = rows.astype(F32)
    mean = jnp.mean(x, axis=-1, keepdims=True)
    centred = x - mean
    inv = lax.rsqrt(jnp.mean(centred * centred, axis=-1, keepdims=True) + EPSILON)
    return centred * inv, inv


def gelu_both(u):
    c = 0.7978845608028654
    u2 = u * u
    t = jnp.tanh(u * (c + (c * 0.044715) * u2))
    half = 0.5 + 0.5 * t
    slope = u * (c + (3 * c * 0.044715) * u2)
    return u * half, half + 0.5 * slope * (1.0 - t * t)


def lanes(shape):
    return lax.broadcasted_iota(jnp.int32, shape, 1)


def head_lanes(shape, h):
    lane = lanes(shape)
    return (lane < HEAD) if h == 0 else (lane >= HEAD)


def turn(part, cosine, low, high):
    return part * cosine + pltpu.roll(part, PAIR - ROT // 2, 1) * low + pltpu.roll(part, ROT // 2, 1) * high


def turn_back(grad, cosine, low, high):
    return grad * cosine + pltpu.roll(grad * low, ROT // 2, 1) + pltpu.roll(grad * high, PAIR - ROT // 2, 1)


def start_all(copies):
    for one in copies:
        one.start()
    return copies


def wait_all(copies):
    for one in copies:
        one.wait()


def mlp_fwd_kernel(tab, *refs):
    tok, gain, bias, cot = refs[:4]
    w_in = refs[4 : 4 + SPLIT]
    b_in = refs[4 + SPLIT : 4 + 2 * SPLIT]
    w_out = refs[4 + 2 * SPLIT]
    (normed_out, unit_out, inv_out, dg_out, out_ref, keep, send, hid_all, w_all, normed, unit_in, inv_in,
     sems) = refs[5 + 2 * SPLIT :]
    j = pl.program_id(0)
    last = pl.num_programs(0) - 1

    def norm_copies():
        return [pltpu.make_async_copy(src, dst, sems.at[n])
                for n, (src, dst) in enumerate(((normed, normed_out), (unit_in, unit_out), (inv_in, inv_out)))]

    def weight_copies():
        return [pltpu.make_async_copy(w_out.at[pl.ds(pl.multiple_of(tab[n] * UNIT, UNIT), UNIT)],
                                      w_all.at[pl.ds(n * UNIT, UNIT)], sems.at[3 + n]) for n in range(w_all.shape[0] // UNIT)]

    @pl.when(j == 0)
    def _():
        start_all(weight_copies())
        for r in range(0, tok.shape[0], QB):
            unit, inv = norm_stats(tok[r : r + QB])
            unit_in[r : r + QB] = unit.astype(BF)
            inv_in[r : r + QB] = jnp.broadcast_to(inv, (QB, PAIR))
            normed[r : r + QB] = (unit * gain[...] + bias[...]).astype(BF)
        start_all(norm_copies())

    wi = jnp.concatenate([r[...] for r in w_in], axis=1)
    bi = jnp.concatenate([r[...] for r in b_in], axis=1)
    hid, dg = gelu_both(dot(normed[...], wi) + bi)
    hid = hid.astype(BF)
    dg_out[...] = dg.astype(BF)
    steps = pl.num_programs(0)
    place = (j + steps // 2) % steps * (SPLIT * UNIT)
    hid_all[:, pl.ds(pl.multiple_of(place, SPLIT * UNIT), SPLIT * UNIT)] = hid
    go = dot(hid, cot[...], TN).astype(BF)

    def store(to):
        for s in range(SPLIT):
            to[s] = go[s * UNIT : (s + 1) * UNIT]

    @pl.when(j <= last // 2)
    def _():
        store(send)

    @pl.when(j > last // 2)
    def _():
        store(keep)

    @pl.when(j == last)
    def _():
        wait_all(weight_copies())
        out_ref[...] = dot(hid_all[...], w_all[...]).astype(BF)
        wait_all(norm_copies())


def attn_fwd_kernel(tab, off, leng, x_ref, cos_ref, low_ref, high_ref, w_hbm, wo_hbm, mlp_hbm,
                    q_out, k_out, v_out, p_out, att_out, act_low, act_high,
                    w_in, wo, mlp, q_in, k_in, v_in, p_in, att_in, sems):
    rows, width = x_ref.shape
    nq = rows // QB
    pairs = GROUP // PAIR
    groups = width // 2 // GROUP
    copy = pltpu.make_async_copy
    def weight_load(g, n):
        col = pl.multiple_of(n * width + tab[48] * (width // 2) + g * GROUP, GROUP)
        return copy(w_hbm.at[:, pl.ds(col, GROUP)], w_in.at[g, n], sems.at[3 * g + n])

    start_all([weight_load(g, n) for g in range(groups) for n in range(3)])
    at = 3 * groups
    late = start_all([copy(wo_hbm.at[pl.ds(pl.multiple_of(tab[48] * (width // 2), width // 2), width // 2)], wo, sems.at[at]),
                      copy(mlp_hbm, mlp, sems.at[at + 1])])
    at += 2
    x = x_ref[...]
    start = off[0]
    stop = start + leng[0]
    place = lax.broadcasted_iota(jnp.int32, (rows, PAIR), 0)
    live = (place >= start) & (place < stop)
    kbias = jnp.where(live, 0.0, MASKED)
    live_f = jnp.where(live, 1.0, 0.0)
    lane = lanes((rows, PAIR))
    diag = lax.broadcasted_iota(jnp.int32, (QB, QB), 0) >= lax.broadcasted_iota(jnp.int32, (QB, QB), 1)
    cosine, low, high = cos_ref[...], low_ref[...], high_ref[...]
    def probs(g, pr):
        two = pl.ds(g * 2 * pairs + 2 * pr, 2)
        return copy(p_in.at[two], p_out.at[two], sems.at[at + g * (pairs + 4) + pr])

    def results(g):
        group = pl.ds(pl.multiple_of(g * GROUP, GROUP), GROUP)
        base = at + g * (pairs + 4)
        return [copy(src.at[:, group], dst.at[:, group], sems.at[base + pairs + n])
                       for n, (src, dst) in enumerate(((q_in, q_out), (k_in, k_out), (v_in, v_out), (att_in, att_out)))]

    @pl.loop(0, groups)
    def _(g):
        wait_all([weight_load(g, n) for n in range(3)])
        qa, ka, va = [dot(x, w_in[g, n]) for n in range(3)]
        for pr in range(pairs):
            cols = slice(pr * PAIR, (pr + 1) * PAIR)
            to = pl.ds(pl.multiple_of(g * GROUP + pr * PAIR, PAIR), PAIR)
            q = turn(qa[:, cols], cosine, low, high).astype(BF).astype(F32) * 0.125
            k = turn(ka[:, cols], cosine, low, high)
            v = va[:, cols]
            q_in[:, to] = q.astype(BF)
            k_in[:, to] = k.astype(BF)
            v_in[:, to] = v.astype(BF)
            qh, kh, vh = [], [], []
            for h in range(2):
                mine = head_lanes((rows, PAIR), h)
                spare = lane == (HEAD if h == 0 else 0)
                qh.append(jnp.where(mine, q, jnp.where(spare, 1.0, 0.0)).astype(BF))
                kh.append(jnp.where(mine, k, jnp.where(spare, kbias, 0.0)).astype(BF))
                vh.append(jnp.where(mine, v, 0.0).astype(BF))
            head = g * 2 * pairs + 2 * pr
            for i in range(nq):
                base = i * (i + 1) // 2 * QB
                ext = (i + 1) * QB
                mixed = None
                scores = [dot(qh[h][i * QB : ext], kh[h][:ext], NT) for h in range(2)]
                for h in range(2):
                    s = scores[h]
                    tail = jnp.where(diag, s[:, i * QB :], MASKED)
                    s = tail if i == 0 else jnp.concatenate([s[:, : i * QB], tail], axis=1)
                    e = jnp.exp(s - jnp.max(s, axis=-1, keepdims=True))
                    p = (e * (1.0 / jnp.sum(e, axis=-1, keepdims=True))).astype(BF)
                    for kb in range(i + 1):
                        p_in[head + h, base + kb * QB : base + (kb + 1) * QB, :] = p[:, kb * QB : (kb + 1) * QB]
                    part = dot(p, vh[h][:ext])
                    mixed = part if mixed is None else mixed + part
                att_in[i * QB : ext, to] = (mixed * live_f[i * QB : ext]).astype(BF)
            probs(g, pr).start()
        start_all(results(g))

    wait_all(late)
    out = mlp[...].astype(F32) + dot(att_in[...], wo[...])
    cut = act_low.shape[0]
    act_low[...] = out[:cut].astype(BF)
    act_high[...] = out[cut:].astype(BF)
    for g in range(groups):
        wait_all([probs(g, pr) for pr in range(pairs)] + results(g))


def mlp_back_kernel(tab, *refs):
    normed, cot, dg = refs[:3]
    w_in = refs[3]
    w_out = refs[4 : 4 + SPLIT]
    gb_out, ng_out, keep, send, stage, pg_all, w_all, sems = refs[4 + SPLIT :]
    j = pl.program_id(0)
    steps = pl.num_programs(0)
    npos = stage.shape[0]
    half = npos // 2
    unit_rows = normed.shape[1] // npos
    wout = jnp.concatenate([r[...] for r in w_out], axis=0)
    x, c = normed[...], cot[...]
    many = 2 * npos // SPLIT

    def weight_copies():
        return [pltpu.make_async_copy(w_in.at[:, pl.ds(pl.multiple_of(tab[n] * UNIT, UNIT), UNIT)],
                                      w_all.at[:, pl.ds(n * UNIT, UNIT)], sems.at[many + n]) for n in range(npos)]

    @pl.when(j == 0)
    def _():
        start_all(weight_copies())

    pg = dot(c, wout, NT) * dg[...].astype(F32)
    gb = jnp.sum(pg, axis=0, keepdims=True)
    pg = pg.astype(BF)
    first = (j + steps // 2) % steps * SPLIT
    pg_all[:, pl.ds(pl.multiple_of(first * UNIT, SPLIT * UNIT), SPLIT * UNIT)] = pg
    gi = dot(x, pg, TN).astype(BF)
    for s in range(SPLIT):
        place = tab[64 + first + s]
        gb_out[:, pl.ds(pl.multiple_of(place * UNIT, UNIT), UNIT)] = gb[:, s * UNIT : (s + 1) * UNIT]
        row = pl.multiple_of(place // SPLIT * unit_rows, unit_rows)
        lane = pl.multiple_of(place % SPLIT * UNIT, UNIT)
        for i in range(npos):
            stage[tab[16 + i], pl.ds(row, unit_rows), pl.ds(lane, UNIT)] = (
                gi[i * unit_rows : (i + 1) * unit_rows, s * UNIT : (s + 1) * UNIT])

    def copies(step):
        lane = tab[64 + (step + steps // 2) % steps * SPLIT] % SPLIT * UNIT
        cols = pl.ds(pl.multiple_of(lane, UNIT), UNIT)
        return [pltpu.make_async_copy(stage.at[pl.ds(half, half), :, cols], send.at[:, :, cols], sems.at[2 * step]),
                pltpu.make_async_copy(stage.at[pl.ds(0, half), :, cols], keep.at[:, :, cols], sems.at[2 * step + 1])]

    for one in copies(j):
        one.start()

    @pl.when(j == steps - 1)
    def _():
        wait_all(weight_copies())
        ng_out[...] = dot(pg_all[...], w_all[...], NT).astype(BF)
        for step in range(npos // SPLIT):
            for one in copies(step):
                one.wait()


def store_small(stage, at, tab, sums, hid_bias):
    npos = stage.shape[0]
    width = sums.shape[1]
    fill = jnp.zeros((14, 2 * UNIT), F32)
    for i in range(npos):
        tile = slice(i * width // npos // UNIT * UNIT, i * width // npos // UNIT * UNIT + UNIT)
        first = jnp.concatenate([sums[0:1, tile], sums[1:2, tile]], axis=1)
        second = jnp.concatenate([sums[2:3, tile], hid_bias[:, i * UNIT : (i + 1) * UNIT]], axis=1)
        stage[tab[16 + i], at : at + 16, :] = jnp.concatenate([first, second, fill], axis=0).astype(BF)


def gain_sums(total, unit):
    return [jnp.sum(total * unit.astype(F32), axis=0, keepdims=True), jnp.sum(total, axis=0, keepdims=True)]


def pair_back(pr, blocks, do, att, q_in, k_in, v_in, p_in, dk_acc, dv_acc, first, base_col=0):
    cols = slice(base_col + pr * PAIR, base_col + (pr + 1) * PAIR)
    top = (blocks[0] + 1) * QB
    start = blocks[-1] * QB
    q, k, v = q_in[:, cols], k_in[:, cols], v_in[:, cols]
    dob = do[:, cols].astype(BF)
    prod = dob.astype(F32) * att[:, cols].astype(F32)
    zero = jnp.zeros((), BF)
    skip = blocks[-1] * (blocks[-1] + 1) // 2 * QB
    qh, kh, doh, delta = [], [], [], []
    for h in range(2):
        mine = head_lanes((top - start, PAIR), h)
        qh.append(jnp.where(mine, q, zero))
        kh.append(jnp.where(head_lanes((top, PAIR), h), k, zero))
        doh.append(jnp.where(mine, dob, zero))
        delta.append(jnp.sum(jnp.where(mine, prod, 0.0), axis=-1, keepdims=True))
    parts = []
    for i in blocks:
        base = i * (i + 1) // 2 * QB - skip
        ext = (i + 1) * QB
        blk = slice(i * QB - start, ext - start)
        probs = [jnp.concatenate(
            [p_in[2 * pr + h, base + kb * QB : base + (kb + 1) * QB, :] for kb in range(i + 1)], axis=1) for h in range(2)]
        dps = [dot(doh[h][blk], v[:ext], NT) for h in range(2)]
        dv_new = dot(doh[0][blk], probs[0], TN) + dot(doh[1][blk], probs[1], TN)
        ds = [(probs[h].astype(F32) * (dps[h] - delta[h][blk])).astype(BF) for h in range(2)]
        sums = [dot(ds[0], kh[0][:ext]) + dot(ds[1], kh[1][:ext]),
                dot(qh[0][blk], ds[0], TN) + dot(qh[1][blk], ds[1], TN), dv_new]
        parts.append(sums[0])
        if first and i == blocks[0]:
            dk_acc[pr], dv_acc[pr] = sums[1], sums[2]
        else:
            dk_acc[pr, :, :ext] += sums[1]
            dv_acc[pr, :, :ext] += sums[2]
    return jnp.concatenate(parts[::-1], axis=0) * 0.125


def out_grads(rows, base, off, leng, cot, wo):
    place = base + lax.broadcasted_iota(jnp.int32, (rows, wo.shape[0]), 0)
    live = (place >= off[0]) & (place < off[0] + leng[0])
    return jnp.where(live, dot(cot, wo[...], NT), 0.0)


def weight_columns(tab, w_hbm, w_in, sem):
    width = w_hbm.shape[0]
    col = lambda n: pl.multiple_of(n * width + tab[48] * (width // 2), width // 2)
    return pltpu.make_async_copy(w_hbm.at[:, pl.ds(col(0), width // 2)], w_in.at[0], sem.at[0]), \
        pltpu.make_async_copy(w_hbm.at[:, pl.ds(col(1), width // 2)], w_in.at[1], sem.at[1]), \
        pltpu.make_async_copy(w_hbm.at[:, pl.ds(col(2), width // 2)], w_in.at[2], sem.at[2])


def store_block(stage, tab, at, grad, gao):
    npos = stage.shape[0]
    rows = grad[0].shape[0] // npos
    for n in range(3):
        for i in range(npos):
            stage[tab[16 + i], at + n * rows : at + (n + 1) * rows, :] = grad[n][i * rows : (i + 1) * rows]
    at += 3 * rows
    rows = gao.shape[0] // npos
    for i in range(npos):
        for n in range(2):
            stage[tab[32 + i], at + n * rows : at + (n + 1) * rows, :] = (
                gao[i * rows : (i + 1) * rows, n * GROUP : (n + 1) * GROUP])


def send_out(stage, keep, send, sems):
    part = stage.shape[0] // 2
    copy = pltpu.make_async_copy
    wait_all(start_all([copy(stage.at[pl.ds(part, part)], send, sems.at[0]),
                        copy(stage.at[pl.ds(0, part)], keep, sems.at[1])]))


def attn_wide_kernel(tab, off, leng, cot, wo, cos_ref, low_ref, high_ref,
                     att_hbm, q_hbm, k_hbm, v_hbm, p_hbm, x_hbm, unit_hbm, ng_hbm, w_hbm, *refs):
    ng_out = refs[:-27]
    (first_out, dqkv_out, dka_out, dva_out, gao_out, sums, keep, send,
     att_in, q_in, k_in, v_in, p_in, p_hi, x_in, unit_in, ng_in, w_in, first, dqkv, dk_acc, dv_acc, dk_hi, dv_hi,
     gao, stage, sems) = refs[-27:]
    rows, width = cot.shape
    half = rows // 2
    nq = rows // QB
    pairs = GROUP // PAIR
    skip = nq // 2 * (nq // 2 + 1) // 2 * QB
    count = p_hi.shape[1]
    lo, hi, group = pl.ds(0, half), pl.ds(half, half), pl.ds(GROUP, GROUP)
    copy = pltpu.make_async_copy
    early = start_all([copy(q_hbm, q_in, sems.at[0]), copy(k_hbm, k_in, sems.at[1]),
                       copy(v_hbm, v_in, sems.at[2]), copy(att_hbm, att_in, sems.at[3])])
    loads = start_all([copy(p_hbm.at[pl.ds(2 * pr, 2)], p_in.at[pl.ds(2 * pr, 2)], sems.at[4 + pr])
                       for pr in range(pairs)])
    loads += start_all([copy(p_hbm.at[pl.ds(2 * (pairs + pr), 2), pl.ds(skip, count)], p_hi.at[pl.ds(2 * pr, 2)],
                             sems.at[4 + pairs + pr]) for pr in range(pairs)])
    at = 4 + 2 * pairs
    late = start_all([copy(x_hbm, x_in, sems.at[at]), *weight_columns(tab, w_hbm, w_in, sems.at[pl.ds(at + 1, 3)]),
                      copy(ng_hbm.at[hi], ng_in, sems.at[at + 4]), copy(unit_hbm.at[hi], unit_in, sems.at[at + 5])])
    cosine, low, high = cos_ref[...], low_ref[...], high_ref[...]
    do = out_grads(rows, 0, off, leng, cot[...], wo)
    blocks = list(reversed(range(nq)))
    wait_all(early)
    for pr in range(pairs):
        loads[pr].wait()
        cols = slice(pr * PAIR, (pr + 1) * PAIR)
        dq = pair_back(pr, blocks, do, att_in, q_in, k_in, v_in, p_in, dk_acc, dv_acc, True)
        first[0, :, cols] = turn_back(dq, cosine, low, high).astype(BF)
        first[1, :, cols] = turn_back(dk_acc[pr].T, cosine, low, high).astype(BF)
        first[2, :, cols] = dv_acc[pr].T.astype(BF)
    outs = start_all([copy(first, first_out, sems.at[0])])
    do = do[half:]
    blocks = list(reversed(range(nq // 2, nq)))
    cosine, low, high = cosine[half:], low[half:], high[half:]
    for pr in range(pairs):
        loads[pairs + pr].wait()
        cols = slice(GROUP + pr * PAIR, GROUP + (pr + 1) * PAIR)
        dq = pair_back(pr, blocks, do, att_in.at[hi], q_in.at[hi], k_in, v_in, p_hi, dk_hi, dv_hi, True, GROUP)
        dqkv[0, :, cols] = turn_back(dq, cosine, low, high).astype(BF)
        dqkv[1, :, cols] = turn_back(dk_hi[pr, :, half:].T, cosine, low, high).astype(BF)
        dqkv[2, :, cols] = dv_hi[pr, :, half:].T.astype(BF)
    outs += start_all([copy(dqkv.at[:, :, group], dqkv_out, sems.at[1]), copy(dk_hi.at[:, :, lo], dka_out, sems.at[2]),
                       copy(dv_hi.at[:, :, lo], dva_out, sems.at[3])])
    all_gao = dot(att_in[...], cot[...], TN).astype(BF)
    gao[...] = all_gao[:, width // 2 :]
    outs += start_all([copy(gao, gao_out, sems.at[4])])
    wait_all(late)
    x = x_in[...]
    store_block(stage, tab, 0, [dot(x, first[n], TN).astype(BF) for n in range(3)], all_gao[:, : width // 2])
    part = stage.shape[0] // 2
    outs += start_all([copy(stage.at[pl.ds(part, part)], send, sems.at[5]), copy(stage.at[pl.ds(0, part)], keep, sems.at[6])])
    total = ng_in[...].astype(F32)
    for n in range(3):
        total = total + dot(first[n, half:], w_in[n, :, :GROUP], NT) + dot(dqkv[n, :, GROUP:], w_in[n, :, GROUP:], NT)
    at = 0
    for to in ng_out:
        to[...] = total[at : at + to.shape[0]].astype(BF)
        at += to.shape[0]
    sums[...] = jnp.concatenate(
        gain_sums(total, unit_in[...]) + [jnp.sum(cot[...].astype(F32), axis=0, keepdims=True), jnp.zeros((5, width), F32)],
        axis=0)
    wait_all(outs)


def attn_low_kernel(tab, off, leng, cot, wo, cos_ref, low_ref, high_ref, hid_bias, sums_in,
                    att_hbm, q_hbm, k_hbm, v_hbm, p_hbm, unit_hbm, ng_hbm, w_hbm, x_hbm, first_hbm, dqkv_hbm, dka_hbm,
                    dva_hbm, gao_hbm, *refs):
    ng_out = refs[:-18]
    (keep, send, stage, att_in, q_in, k_in, v_in, p_in, unit_in, ng_in, w_in, x_in, dqkv, dqkv_hi, dk_acc, dv_acc, gao,
     sems) = refs[-18:]
    half, width = cot.shape
    nq = 2 * half // QB
    pairs = GROUP // PAIR
    count = p_in.shape[1]
    lo, group = pl.ds(0, half), pl.ds(GROUP, GROUP)
    copy = pltpu.make_async_copy
    early = start_all([copy(q_hbm.at[lo, group], q_in, sems.at[0]), copy(k_hbm.at[lo, group], k_in, sems.at[1]),
                       copy(v_hbm.at[lo, group], v_in, sems.at[2]), copy(att_hbm.at[lo, group], att_in, sems.at[3]),
                       copy(dka_hbm, dk_acc, sems.at[4]), copy(dva_hbm, dv_acc, sems.at[5])])
    loads = start_all([copy(p_hbm.at[pl.ds(4 + 2 * pr, 2), pl.ds(0, count)], p_in.at[pl.ds(2 * pr, 2)], sems.at[6 + pr])
                       for pr in range(pairs)])
    at = 6 + pairs
    late = start_all([copy(dqkv_hbm, dqkv_hi, sems.at[at]), copy(x_hbm, x_in, sems.at[at + 1]),
                      *weight_columns(tab, w_hbm, w_in, sems.at[pl.ds(at + 2, 3)]),
                      copy(ng_hbm.at[lo], ng_in, sems.at[at + 5]), copy(unit_hbm.at[lo], unit_in, sems.at[at + 6]),
                      copy(gao_hbm, gao, sems.at[at + 7]),
                      copy(first_hbm.at[:, lo], dqkv.at[:, :, pl.ds(0, GROUP)], sems.at[at + 8])])
    do = out_grads(half, 0, off, leng, cot[...], wo)
    cosine, low, high = cos_ref[...], low_ref[...], high_ref[...]
    blocks = list(reversed(range(nq // 2)))
    wait_all(early)
    for pr in range(pairs):
        loads[pr].wait()
        cols = slice(GROUP + pr * PAIR, GROUP + (pr + 1) * PAIR)
        dq = pair_back(pr, blocks, do, att_in, q_in, k_in, v_in, p_in, dk_acc, dv_acc, False)
        dqkv[0, :, cols] = turn_back(dq, cosine, low, high).astype(BF)
        dqkv[1, :, cols] = turn_back(dk_acc[pr].T, cosine, low, high).astype(BF)
        dqkv[2, :, cols] = dv_acc[pr].T.astype(BF)
    wait_all(late)
    x = x_in[...]
    grad = [(dot(x[:half], dqkv[n, :, GROUP:], TN) + dot(x[half:], dqkv_hi[n], TN)).astype(BF) for n in range(3)]
    store_block(stage, tab, 0, grad, gao[...])
    total = ng_in[...].astype(F32)
    for n in range(3):
        total = total + dot(dqkv[n], w_in[n], NT)
    at = 0
    for to in ng_out:
        to[...] = total[at : at + to.shape[0]].astype(BF)
        at += to.shape[0]
    sums = sums_in[...]
    new = gain_sums(total, unit_in[...])
    store_small(stage, stage.shape[1] - 16, tab,
                jnp.concatenate([sums[0:1] + new[0], sums[1:2] + new[1], sums[2:3]], axis=0), hid_bias[...])
    send_out(stage, keep, send, sems)


def act_kernel(tok, bias, own_low, own_high, recv_low, recv_high, out):
    cut = own_low.shape[0]
    for rows, own, recv in ((slice(0, cut), own_low, recv_low), (slice(cut, tok.shape[0]), own_high, recv_high)):
        base = tok[rows].astype(F32) + bias[...]
        out[rows] = (base + (own[...].astype(F32) + recv[...].astype(F32))).astype(BF)


def finish_kernel(counts, unit_ref, inv, cot, gain, *refs):
    out = refs[-1]
    unit = unit_ref[...].astype(F32)
    start = 0
    for n, count in enumerate(counts):
        own, recv = refs[2 * n], refs[2 * n + 1]

        @pl.when((pl.program_id(0) >= start) & (pl.program_id(0) < start + count))
        def _():
            scaled = (own[...].astype(F32) + recv[...].astype(F32)) * gain[...]
            mean = jnp.mean(scaled, axis=-1, keepdims=True)
            lean = jnp.mean(scaled * unit, axis=-1, keepdims=True)
            out[...] = (cot[...].astype(F32) + inv[:, :1] * (scaled - mean - unit * lean)).astype(BF)

        start += count


def const_spec(shape):
    zeros = (0,) * len(shape)
    return pl.BlockSpec(shape, lambda g, *tabs: zeros, pipeline_mode=pl.Buffered(1))


def in_hbm(value):
    return pltpu.with_memory_space_constraint(value, pltpu.HBM)


def params(limit=LIMIT):
    return pltpu.CompilerParams(vmem_limit_bytes=limit)


def rotary_tables(rows):
    lane = np.arange(PAIR) % HEAD
    half = ROT // 2
    angle = np.arange(rows)[:, None] * np.power(10000.0, (lane % half) * (-2.0 / ROT))[None, :]
    inside = (lane < ROT)[None, :]
    cosine = np.where(inside, np.cos(angle), 1.0)
    low = np.where((lane < half)[None, :], -np.sin(angle), 0.0)
    high = np.where(inside & (lane >= half)[None, :], np.sin(angle), 0.0)
    return [jnp.asarray(t, F32) for t in (cosine, low, high)]


def mlp_specs(width, npos):
    steps = npos // SPLIT
    turn_of = lambda j: (j + steps // 2) % steps
    w_in = [pl.BlockSpec((width, UNIT), lambda j, t, s=s: (0, t[turn_of(j) * SPLIT + s])) for s in range(SPLIT)]
    b_in = [pl.BlockSpec((1, UNIT), lambda j, t, s=s: (0, t[turn_of(j) * SPLIT + s])) for s in range(SPLIT)]
    w_out = [pl.BlockSpec((UNIT, width), lambda j, t, s=s: (t[turn_of(j) * SPLIT + s], 0)) for s in range(SPLIT)]
    return w_in, b_in, w_out, lambda rows: pl.BlockSpec((rows, SPLIT * UNIT), lambda j, t: (0, turn_of(j)))


def mlp_forward(tab, tokens, gain, bias, cot, w_in, b_in, w_out, npos):
    rows, width = tokens.shape
    wi, bi, wo, wide = mlp_specs(width, npos)
    steps = npos // SPLIT
    full = jax.ShapeDtypeStruct((rows, width), BF)
    part = jax.ShapeDtypeStruct((npos // 2, UNIT, width), BF)
    block = (SPLIT, UNIT, width)
    return pl.pallas_call(
        mlp_fwd_kernel,
        grid_spec=pltpu.PrefetchScalarGridSpec(
            num_scalar_prefetch=1,
            grid=(steps,),
            in_specs=[const_spec((rows, width)), const_spec((1, width)), const_spec((1, width)),
                      const_spec((rows, width))] + wi + bi + [pl.BlockSpec(memory_space=pl.ANY)],
            out_specs=[pl.BlockSpec(memory_space=pl.ANY)] * 3 + [wide(rows),
                       const_spec((rows, width)),
                       pl.BlockSpec(block, lambda j, t: (jnp.maximum(j - steps // 2, 0), 0, 0)),
                       pl.BlockSpec(block, lambda j, t: (jnp.minimum(j, steps // 2 - 1), 0, 0))],
            scratch_shapes=[pltpu.VMEM((rows, npos * UNIT), BF), pltpu.VMEM((npos * UNIT, width), BF),
                            pltpu.VMEM((rows, width), BF), pltpu.VMEM((rows, width), BF),
                            pltpu.VMEM((rows, PAIR), F32), pltpu.SemaphoreType.DMA((3 + npos,))],
        ),
        out_shape=[pltpu.HBM((rows, width), BF), pltpu.HBM((rows, width), BF), pltpu.HBM((rows, PAIR), F32),
                   pltpu.HBM((rows, npos * UNIT), BF), full, part, part],
        compiler_params=params(MAIN),
        cost_estimate=pl.CostEstimate(flops=20 * 10**9, bytes_accessed=10**7, transcendentals=0),
        name="mlp_forward",
    )(tab, *[in_hbm(t) for t in (tokens, gain, bias, cot)], *([in_hbm(w_in)] * SPLIT), *([in_hbm(b_in)] * SPLIT), in_hbm(w_out))


def attn_forward(tab, off, leng, normed, mlp_out, w_qkv, w_ao, tables):
    rows, width = normed.shape
    groups = width // 2 // GROUP
    tri = (rows // QB) * (rows // QB + 1) // 2 * QB
    anyspec = pl.BlockSpec(memory_space=pl.ANY)
    half = pltpu.HBM((rows, width // 2), BF)
    cols = pltpu.VMEM((rows, width // 2), BF)
    sizes = (rows * ACT_LOW // 16, rows - rows * ACT_LOW // 16)
    return pl.pallas_call(
        attn_fwd_kernel,
        grid_spec=pltpu.PrefetchScalarGridSpec(
            num_scalar_prefetch=3,
            grid=(1,),
            in_specs=[const_spec((rows, width))] + [const_spec((rows, PAIR))] * 3 + [anyspec] * 3,
            out_specs=[anyspec] * 5 + [const_spec((n, width)) for n in sizes],
            scratch_shapes=[pltpu.VMEM((groups, 3, width, GROUP), BF), pltpu.VMEM((width // 2, width), BF),
                            pltpu.VMEM((rows, width), BF), cols, cols, cols, pltpu.VMEM((HEADS // 2, tri, QB), BF), cols,
                            pltpu.SemaphoreType.DMA((3 * groups + 2 + groups * (GROUP // PAIR + 4),))],
        ),
        out_shape=[half, half, half, pltpu.HBM((HEADS // 2, tri, QB), BF), half]
        + [jax.ShapeDtypeStruct((n, width), BF) for n in sizes],
        compiler_params=params(FORWARD),
        cost_estimate=pl.CostEstimate(flops=20 * 10**9, bytes_accessed=10**7, transcendentals=0),
        name="attention_forward",
    )(tab, off, leng, in_hbm(normed), *tables, in_hbm(w_qkv), w_ao, mlp_out)


def mlp_backward(tab, normed, cot, dg, w_in, w_out, npos):
    rows, width = normed.shape
    wi, _, wo, wide = mlp_specs(width, npos)
    unit_rows = width // npos
    ublock = npos // SPLIT * unit_rows
    part = jax.ShapeDtypeStruct((npos // 2, ublock, 512), BF)
    anyspec = pl.BlockSpec(memory_space=pl.ANY)
    return pl.pallas_call(
        mlp_back_kernel,
        grid_spec=pltpu.PrefetchScalarGridSpec(
            num_scalar_prefetch=1,
            grid=(npos // SPLIT,),
            in_specs=[const_spec((rows, width)), const_spec((rows, width)),
                      wide(rows), anyspec] + wo,
            out_specs=[const_spec((1, npos * UNIT)), const_spec((rows, width)), anyspec, anyspec],
            scratch_shapes=[pltpu.VMEM((npos, ublock, 512), BF), pltpu.VMEM((rows, npos * UNIT), BF),
                            pltpu.VMEM((width, npos * UNIT), BF), pltpu.SemaphoreType.DMA((2 * npos // SPLIT + npos,))],
        ),
        out_shape=[jax.ShapeDtypeStruct((1, npos * UNIT), F32), jax.ShapeDtypeStruct((rows, width), BF), part, part],
        compiler_params=params(MAIN),
        cost_estimate=pl.CostEstimate(flops=20 * 10**9, bytes_accessed=10**7, transcendentals=0),
        name="mlp_backward",
    )(tab, normed, cot, dg, w_in, *([w_out] * SPLIT))


def back_specs(width, half_rows, place, group, count):
    row = lambda n: pl.BlockSpec((half_rows, n), lambda i, *t: (place, 0), pipeline_mode=pl.Buffered(1))
    blocks = width // 2 // GROUP // count
    out = pl.BlockSpec((GROUP * count, width), lambda i, t, o, l: (t[48] * blocks + group, 0),
                       pipeline_mode=pl.Buffered(1))
    return [row(width), out] + [row(PAIR)] * 3


def back_call(kernel, name, cost, scratch, in_specs, out_specs, out_shape):
    return pl.pallas_call(
        kernel,
        grid_spec=pltpu.PrefetchScalarGridSpec(
            num_scalar_prefetch=3, grid=(1,), in_specs=in_specs, out_specs=out_specs, scratch_shapes=scratch),
        out_shape=out_shape,
        compiler_params=params(BACK),
        cost_estimate=pl.CostEstimate(flops=cost, bytes_accessed=10**5, transcendentals=0),
        name=name,
    )


def stage_rows(width, npos):
    return 3 * (width // npos) + 2 * (width // 2 // npos)


def attn_back_wide(tab, off, leng, cot, att, q, k, v, p, unit, w_qkv, w_ao, ng, tables, normed, npos):
    rows, width = cot.shape
    half = rows // 2
    nq = rows // QB
    count = p.shape[1] - nq // 2 * (nq // 2 + 1) // 2 * QB
    pairs = GROUP // PAIR
    anyspec = pl.BlockSpec(memory_space=pl.ANY)
    sizes = [size * UNIT for at, size in NG_PARTS if at * UNIT >= half]
    ublock = stage_rows(width, npos)
    part = jax.ShapeDtypeStruct((npos // 2, ublock, GROUP), BF)
    accs = pltpu.HBM((pairs, PAIR, half), F32)
    cols = pltpu.VMEM((rows, width // 2), BF)
    acc = pltpu.VMEM((pairs, PAIR, rows), F32)
    wide = pltpu.VMEM((half, width), BF)
    return back_call(
        attn_wide_kernel, "attention_back_wide", 20 * 10**9,
        [cols, cols, cols, cols, pltpu.VMEM((GROUP // HEAD, p.shape[1], QB), BF), pltpu.VMEM((GROUP // HEAD, count, QB), BF),
         pltpu.VMEM((rows, width), BF), wide, wide, pltpu.VMEM((3, width, width // 2), BF), pltpu.VMEM((3, rows, GROUP), BF),
         pltpu.VMEM((3, half, width // 2), BF), acc, acc, acc, acc, pltpu.VMEM((width // 2, width // 2), BF),
         pltpu.VMEM((npos, ublock, GROUP), BF), pltpu.SemaphoreType.DMA((2 * pairs + 10,))],
        back_specs(width, rows, 0, 0, 2) + [anyspec] * 9,
        [const_spec((n, width)) for n in sizes] + [anyspec] * 5 + [const_spec((8, width)), anyspec, anyspec],
        [jax.ShapeDtypeStruct((n, width), BF) for n in sizes]
        + [pltpu.HBM((3, rows, GROUP), BF), pltpu.HBM((3, half, GROUP), BF), accs, accs,
           pltpu.HBM((width // 2, width // 2), BF), jax.ShapeDtypeStruct((8, width), F32), part, part],
    )(tab, off, leng, cot, w_ao, *tables, att, q, k, v, p, normed, unit, ng, w_qkv)


def attn_back_low(tab, off, leng, cot, att, q, k, v, p, unit, w_qkv, w_ao, ng, tables, normed, hid_bias, first,
                  gao, carried, npos):
    rows, width = cot.shape
    half = rows // 2
    nq = rows // QB
    count = nq // 2 * (nq // 2 + 1) // 2 * QB
    pairs = GROUP // PAIR
    anyspec = pl.BlockSpec(memory_space=pl.ANY)
    sizes = [size * UNIT for at, size in NG_PARTS if at * UNIT < half]
    ublock = stage_rows(width, npos) + 16
    part = jax.ShapeDtypeStruct((npos // 2, ublock, GROUP), BF)
    dqkv, dk_acc, dv_acc, sums = carried
    cols = pltpu.VMEM((half, GROUP), BF)
    acc = pltpu.VMEM((pairs, PAIR, half), F32)
    wide = pltpu.VMEM((half, width), BF)
    return back_call(
        attn_low_kernel, "attention_back_low", 20 * 10**9,
        [pltpu.VMEM((npos, ublock, GROUP), BF), cols, cols, cols, cols, pltpu.VMEM((GROUP // HEAD, count, QB), BF),
         wide, wide, pltpu.VMEM((3, width, width // 2), BF), pltpu.VMEM((rows, width), BF),
         pltpu.VMEM((3, half, width // 2), BF), pltpu.VMEM((3, half, GROUP), BF), acc, acc,
         pltpu.VMEM((width // 2, width // 2), BF), pltpu.SemaphoreType.DMA((pairs + 15,))],
        back_specs(width, half, 0, 1, 1) + [const_spec((1, npos * UNIT)), const_spec((8, width))]
        + [anyspec] * 14,
        [const_spec((n, width)) for n in sizes] + [anyspec, anyspec],
        [jax.ShapeDtypeStruct((n, width), BF) for n in sizes] + [part, part],
    )(tab, off, leng, cot, w_ao, *tables, hid_bias, sums, att, q, k, v, p, unit, ng, w_qkv, normed, first, dqkv,
      dk_acc, dv_acc, gao)


def act_sum(tokens, bias, own, recv):
    return pl.pallas_call(
        act_kernel,
        grid=(1,),
        in_specs=[const_spec(t.shape) for t in (tokens, bias, *own, *recv)],
        out_specs=const_spec(tokens.shape),
        out_shape=jax.ShapeDtypeStruct(tokens.shape, BF),
        compiler_params=params(),
        cost_estimate=pl.CostEstimate(flops=10**6, bytes_accessed=10**6, transcendentals=0),
        name="activations",
    )(in_hbm(tokens), bias, *[in_hbm(t) for t in (*own, *recv)])


def finish(pieces, unit, inv, cot, parts, gain, done):
    rows, width = unit.shape
    counts = [NG_PARTS[n][1] for n in pieces]

    def place(r):
        at, start = NG_PARTS[pieces[0]][0] + r, counts[0]
        for n, count in zip(pieces[1:], counts[1:]):
            at = jnp.where(r >= start, NG_PARTS[n][0] + r - start, at)
            start += count
        return at

    row = pl.BlockSpec((UNIT, width), lambda r: (place(r), 0))
    specs, start = [], 0
    for count in counts:
        specs += [pl.BlockSpec((UNIT, width), lambda r, lo=start, top=count - 1: (jnp.clip(r - lo, 0, top), 0))] * 2
        start += count
    return pl.pallas_call(
        functools.partial(finish_kernel, counts),
        grid=(start,),
        in_specs=[row, pl.BlockSpec((UNIT, PAIR), lambda r: (place(r), 0)), row, pl.BlockSpec((1, width), lambda r: (0, 0))]
        + specs + [pl.BlockSpec(memory_space=pl.ANY)] * len(done),
        out_specs=row,
        out_shape=jax.ShapeDtypeStruct((rows, width), BF),
        input_output_aliases={4 + 2 * len(pieces): 0} if done else {},
        compiler_params=params(),
        cost_estimate=pl.CostEstimate(flops=10**7, bytes_accessed=10**6, transcendentals=0),
        name="norm_backward",
    )(*[in_hbm(t) for t in (unit, inv, cot)], gain, *[in_hbm(t) for pair in parts for t in pair], *done)


def bit_reverse(value, bits):
    out = 0
    for n in range(bits):
        out |= (value >> n & 1) << (bits - 1 - n)
    return out


NPOS = 16
ACT_LOW = 7
NG_PARTS = ((4, 2), (6, 2), (0, 2), (2, 2))


def place_tables(ndp):
    bits = NPOS.bit_length() - 1
    table = np.zeros((ndp, 2, 80), np.int32)
    for d in range(ndp):
        for b in range(2):
            for n in range(NPOS):
                if ndp == NPOS:
                    table[d, b, n] = 2 * (bit_reverse(n, bits) ^ d) + b
                    table[d, b, 64 + n] = bit_reverse(n, bits) ^ d
                    table[d, b, 16 + n] = bit_reverse(n ^ d, bits)
                    rel = 0
                    for k in range(bits - 1):
                        rel |= ((n >> (k + 1) & 1) ^ (d >> k & 1)) << (bits - 1 - k)
                    rel |= (n & 1) ^ (d >> (bits - 1) & 1)
                    table[d, b, 32 + n] = rel
                else:
                    table[d, b, n] = b * NPOS + n
                    table[d, b, 64 + n] = n
                    table[d, b, 16 + n] = n
                    table[d, b, 32 + n] = n
            table[d, b, 48] = b
    return table


def after(values, *others):
    out = lax.optimization_barrier((values,) + others)
    return out[0]


def trade(send, bit, ndp):
    return lax.ppermute(send, "dp", [(d, d ^ bit) for d in range(ndp)])


def add_halves(keep, recv):
    half = keep.shape[0] // 2
    mine = (keep[:half].astype(F32) + recv[:half].astype(F32)).astype(BF)
    other = (keep[half:].astype(F32) + recv[half:].astype(F32)).astype(BF)
    return mine, other


def add_quarters(keep, recv):
    parts = [keep[n].astype(F32) + recv[n].astype(F32) for n in range(4)]
    return parts[0], [part.astype(BF) for part in parts[1:]]


def trade_quarters(parts, ndp):
    return [trade(part, bit, ndp) for part, bit in zip(parts, (8, 4, 12))]


def add_all(mine, recvs):
    for recv in recvs:
        mine = mine + recv.astype(F32)
    return mine


def shards(ndp, tokens, offsets, lengths, cotangent, ln_gain, ln_bias, w_qkv, w_attn_out, w_in, b_in, w_out, b_out):
    rows, width = tokens.shape
    dp = lax.axis_index("dp")
    b = lax.axis_index("branch")
    hidden = w_in.shape[1]
    tables = rotary_tables(rows)
    all_tab = jnp.asarray(place_tables(ndp))
    tab = lax.dynamic_slice(all_tab, (dp, b, 0), (1, 1, 80)).reshape(80)
    gain = ln_gain.reshape(1, width)
    bias = ln_bias.reshape(1, width)
    swap = [(0, 1), (1, 0)]
    halving = ndp == NPOS

    normed, unit, inv, dg, mlp_out, a_keep, a_send = mlp_forward(
        tab, tokens, gain, bias, cotangent, w_in, b_in.reshape(1, hidden), w_out, NPOS)
    barrier = lax.optimization_barrier
    a_part = (a_keep, a_send)
    a_recv = trade(a_send, 1, ndp) if halving else a_send
    q, k, v, p, att, *act_own = attn_forward(
        tab, offsets, lengths, after(normed, a_send), mlp_out, w_qkv, w_attn_out, tables)
    a_recv, att, *act_own = barrier((a_recv, att, *act_own))
    act_recv = [lax.ppermute(part, "branch", swap) for part in act_own]
    if halving:
        a_keep, a_send = add_halves(a_keep, a_recv)
        a_recv = trade(a_send, 2, ndp)
    gb_in, ng, b_keep, b_send = mlp_backward(tab, normed, cotangent, after(dg, att, a_send), w_in, w_out, NPOS)
    b_part = (b_keep, b_send)
    a_recv, b_send, ng, act_recv[0] = barrier((a_recv, b_send, ng, act_recv[0]))
    if halving:
        b_recv = trade(b_send, 1, ndp)
        a_mine, a_send = add_quarters(a_keep, a_recv)
        a_recv = trade_quarters(a_send, ndp)
        b_keep, b_send = add_halves(b_keep, b_recv)
        b_recv = trade(b_send, 2, ndp)
    else:
        b_recv = b_send
        a_recv, a_send = [a_recv], [a_send]
    *ng_own, first, dqkv, dk_acc, dv_acc, gao, sums, c_keep, c_send = attn_back_wide(
        tab, offsets, lengths, cotangent, after(att, b_send, *a_send), q, k, v, p, unit, w_qkv, w_attn_out, ng, tables,
        normed, NPOS)
    c_part = (c_keep, c_send)
    b_recv, a_recv, act_recv[1], c_send, ng_own = barrier((b_recv, a_recv, act_recv[1], c_send, ng_own))
    ng_recv = [lax.ppermute(part, "branch", swap) for part in ng_own]
    c_recv = c_send
    if halving:
        c_recv = trade(c_send, 1, ndp)
        b_keep, b_send = add_halves(b_keep, b_recv)
        b_recv = trade(b_send, 4, ndp)
        c_recv, b_send = barrier((c_recv, b_send))
        c_keep, c_send = add_halves(c_keep, c_recv)
        c_recv = trade(c_send, 2, ndp)
    *more, d_keep, d_send = attn_back_low(
        tab, offsets, lengths, cotangent, after(att, b_send, c_send, ng_own[0]), q, k, v, p, unit, w_qkv, w_attn_out, ng,
        tables, normed, gb_in, first, gao, (dqkv, dk_acc, dv_acc, sums), NPOS)
    ng_own = ng_own + more
    if not halving:
        ng_recv = [lax.ppermute(part, "branch", swap) for part in ng_own]
        activations = act_sum(tokens, b_out.reshape(1, width), act_own, act_recv)
        input_grad = ()
        for n in range(len(NG_PARTS)):
            input_grad = (finish([n], unit, inv, cotangent, [(ng_own[n], ng_recv[n])], gain, input_grad),)
        return (activations,) + input_grad + natural_sums(b, a_part, b_part, c_part, (d_keep, d_send), width, hidden)

    unit_rows = width // NPOS
    sub = unit_rows // 2
    steps = NPOS // SPLIT
    gao_rows = width // 2 // NPOS
    second = 3 * unit_rows + 2 * gao_rows
    total = lambda keep, recv: keep[0].astype(F32) + recv[0].astype(F32)

    def halves(parts):
        return (lax.dynamic_slice_in_dim(parts, b * sub, sub, 1),
                lax.dynamic_slice_in_dim(parts, (1 - b) * sub, sub, 1).astype(BF))

    b_recv, c_recv, ng_recv[0], d_send, *more = barrier((b_recv, c_recv, ng_recv[0], d_send, *more))
    ng_recv += [lax.ppermute(part, "branch", swap) for part in more]
    d_recv = trade(d_send, 1, ndp)
    c_keep, c_send = add_halves(c_keep, c_recv)
    c_recv = trade(c_send, 4, ndp)
    b_keep, b_send = add_halves(b_keep, b_recv)
    b_recv = trade(b_send, 8, ndp)
    d_recv, c_send, b_send = barrier((d_recv, c_send, b_send))
    d_keep, d_send = add_halves(d_keep, d_recv)
    d_recv = trade(d_send, 2, ndp)
    g_out = add_all(a_mine, after(a_recv, d_send))
    act_recv[0] = after(act_recv[0], g_out)
    activations = act_sum(tokens, b_out.reshape(1, width), act_own, act_recv)
    c_recv, d_recv, b_recv, ng_recv[1], activations = barrier((c_recv, d_recv, b_recv, ng_recv[1], activations))
    d_keep, d_send = add_halves(d_keep, d_recv)
    d_recv = trade(d_send, 4, ndp)
    c_keep, c_send = add_halves(c_keep, after(c_recv, d_send))
    c_recv = trade(c_send, 8, ndp)
    gi_own, gi_away = halves(total(b_keep, after(b_recv, c_send)).reshape(steps, unit_rows, 512))
    gi_recv = lax.ppermute(gi_away, "branch", swap)
    grad = finish([0], unit, inv, cotangent, [(ng_own[0], after(ng_recv[0], gi_away))], gain, ())
    c_recv, d_recv, ng_recv[2], grad = barrier((c_recv, d_recv, ng_recv[2], grad))
    d_keep, d_send = add_halves(d_keep, d_recv)
    d_recv = trade(d_send, 8, ndp)
    gc = total(c_keep, after(c_recv, d_send))
    grad = finish([1, 2], unit, inv, cotangent, [(ng_own[1], after(ng_recv[1], d_send)), (ng_own[2], ng_recv[2])], gain,
                  (grad,))
    d_recv, gc, grad = barrier((d_recv, gc, grad))
    gd = total(d_keep, d_recv)
    gq = jnp.concatenate([gc[: 3 * unit_rows].reshape(3, unit_rows, GROUP), gd[: 3 * unit_rows].reshape(3, unit_rows, GROUP)],
                         axis=2)
    gq_own, gq_away = halves(gq)
    gao = jnp.concatenate([g[3 * unit_rows + n * gao_rows : 3 * unit_rows + (n + 1) * gao_rows]
                           for g in (gc, gd) for n in range(2)], axis=1)
    small = gd[second : second + 2]
    both = jnp.concatenate([gq_away, jnp.broadcast_to(small[:1].astype(BF)[None], (3, sub, GROUP))], axis=2)
    both_recv = lax.ppermute(both, "branch", swap).astype(F32)
    columns = lambda part: part.astype(F32).reshape(steps, sub, SPLIT, UNIT).transpose(1, 0, 2, 3).reshape(sub, NPOS, UNIT)
    near, far = columns(gi_own), columns(after(gi_recv, both))
    g_in = jnp.stack([jnp.where(b == 0, near, far), jnp.where(b == 0, far, near)], axis=2).reshape(sub, hidden)
    top = ndp // 2
    pairs = [(d * 2 + c, (d ^ top) * 2 + 1 - c) for d in range(ndp) for c in range(2) if d // top != c]
    moved = lax.ppermute(gao.astype(BF), ("dp", "branch"), pairs)
    input_grad = finish([3], unit, inv, cotangent, [(ng_own[3], after(ng_recv[3], both))], gain, (grad,))
    g_ao = jnp.where(dp // top == b, gao, moved.astype(F32))
    recv = both_recv[:, :, : 2 * GROUP]
    first = jnp.where(b == 0, gq_own, recv)
    second_half = jnp.where(b == 0, recv, gq_own)
    g_qkv = jnp.concatenate(sum([[first[n], second_half[n]] for n in range(3)], []), axis=1)
    per = width // (2 * ndp)
    lane = dp % (UNIT // (2 * per)) * 2 * per + b * per
    row = small[0] + both_recv[0, 0, 2 * GROUP :]
    cut = lambda values, start: lax.dynamic_slice(values, (start,), (per,))
    return (activations, input_grad, cut(row, lane), cut(row, UNIT + lane), g_qkv, g_ao, g_in,
            small[1, UNIT:], g_out, cut(small[1], lane))


def natural_sums(b, a_part, b_part, c_part, d_part, width, hidden):
    axes = ("dp", "branch")
    steps = NPOS // SPLIT
    unit_rows = width // NPOS
    gao_rows = width // 2 // NPOS
    second = 3 * unit_rows + 2 * gao_rows
    wa, wb, wc, wd = [jnp.concatenate(part, axis=0).astype(F32) for part in (a_part, b_part, c_part, d_part)]
    go = wa.reshape(NPOS * UNIT, width)
    gi = wb.reshape(NPOS, steps, unit_rows, 512).transpose(0, 2, 1, 3)
    gi = gi.reshape(width, hidden // 2)
    gq = jnp.concatenate([w[:, : 3 * unit_rows].reshape(NPOS, 3, unit_rows, GROUP) for w in (wc, wd)], axis=3)
    gq = gq.transpose(0, 2, 1, 3).reshape(width, 3, 2 * GROUP)
    ga = jnp.concatenate([w[:, 3 * unit_rows : second].reshape(NPOS, 2, gao_rows, GROUP) for w in (wc, wd)], axis=1)
    ga = ga.transpose(0, 2, 1, 3).reshape(NPOS * gao_rows, width)
    tiles = wd[:, second : second + 2]
    per_tile = UNIT // unit_rows

    def vector(row, lane):
        split = tiles[:, row, lane : lane + UNIT].reshape(NPOS // per_tile, per_tile, per_tile, unit_rows)
        return jnp.stack([split[:, n, n] for n in range(per_tile)], axis=1).reshape(width)

    def scatter(part, full, dim):
        starts = [0] * part.ndim
        starts[dim] = b * part.shape[dim]
        whole = lax.dynamic_update_slice(jnp.zeros(full, F32), part, starts)
        return lax.psum_scatter(whole, axes, scatter_dimension=0, tiled=True)

    total = lambda t: lax.psum_scatter(t, axes, scatter_dimension=0, tiled=True)
    g_qkv = scatter(gq, (width, 3, width), 2)
    return (
        total(vector(0, 0)),
        total(vector(0, UNIT)),
        g_qkv.reshape(g_qkv.shape[0], 3 * width),
        scatter(ga, (width, width), 0),
        scatter(gi, (width, hidden), 1),
        scatter(tiles[:, 1, UNIT:].reshape(-1), (hidden,), 0),
        scatter(go, (hidden, width), 0),
        total(jnp.where(b == 0, vector(1, 0), 0.0)),
    )


def solution(mesh):
    return jax.shard_map(
        functools.partial(shards, mesh.shape["dp"]),
        mesh=mesh,
        in_specs=(P("dp", None), P("dp"), P("dp"), P("dp", None)) + (P(),) * 8,
        out_specs=(
            P("dp", None),
            P("dp", None),
            P(("dp", "branch")),
            P(("dp", "branch")),
            P(("dp", "branch"), None),
            P(("dp", "branch"), None),
            P(("dp", "branch"), None),
            P(("dp", "branch")),
            P(("dp", "branch"), None),
            P(("dp", "branch")),
        ),
        check_vma=False,
    )
```
